128 devices in a mesh: row: 32 (over z, x, core), col: 4 (over y).
Axes of the slice: x: 4, y: 4, z: 4, core: 2. Of those that a mesh axis runs over, the one named last changes fastest.
Arguments:
- doc_taps: bfloat16 [98304, 2, 5120], P(('row', 'col')), may hold values from -24 to 24
- w_down: bfloat16 [5120, 512], replicated, may hold values from -0.078125 to 0.078125
- owner_of: int32 [4, 24576], P('col'), may hold values from 0 to 31, as said below
- adj_values: bfloat16 [128, 24, 128, 128], P(('row', 'col')), as said below
- adj_index: int32 [128, 24], P(('row', 'col')), may hold values from 0 to 23, as said below
- w_msg: bfloat16 [512, 512], replicated, may hold values from -0.25 to 0.25
- gate_scale: float32 [512], replicated, may hold values from 0.5 to 1.5
- cotangent: bfloat16 [98304, 512], P(('row', 'col')), may hold values from -0.078125 to 0.078125
Outputs:
- side_out: bfloat16 [98304, 512], P(('row', 'col'))
- grad_down: float32 [5120, 512], P('row')
- grad_msg: float32 [512, 512], P('row')
- grad_gate: float32 [512], P('row')
The draws below stay inside these ranges and needn't reach their ends.
Inputs may be any that keep to these rules, and one draw needn't show every extreme that they name: `owner_of`: each row owner receives exactly 768 documents of each column group; one device sends at most 72 documents to one owner, and 72 is reached in every column group. `adj_index`: entry e of a device lies in its block row e // 4; the first entry of each block row is the diagonal block of the row group. Within a row group the adjacency is symmetric: summed block (I, J) is the transpose of summed block (J, I). `adj_values`: blocks of the same pair in transposed positions are transposes of each other; diagonal blocks are symmetric.
All inputs are finite; a program needn't handle non-finite values.
Results may differ from the reference program's by a relative error of at most 0.0072.
Values may be sent and summed in bfloat16 or wider, within the bound.
No kernel may reach another device: no remote copies, remote signals or barrier semaphores. Data moves between devices by JAX's collectives and lax.ppermute only.
A program may use at most 128 MiB of HBM per device.

```python
import jax
import jax.numpy as jnp
from jax import lax

DL = 5120
H = 512
TPD = 2
BLOCK = 128
MATCH = 3
NODES_DEV = 768
NODES = 98304
GROUP = 3072
RB = 6
GB = 24
NBL = 24
N_ROW = 32
N_COL = 4


def match_tables(key):
    sub_keys = jax.random.split(key, N_ROW * MATCH)

    def single(subkey):
        ordering = jax.random.permutation(subkey, GB).astype(jnp.int32)
        left_side = ordering[0::2]
        right_side = ordering[1::2]
        pair_ids = jnp.arange(GB // 2, dtype=jnp.int32)
        partner = jnp.zeros((GB,), jnp.int32).at[left_side].set(right_side).at[right_side].set(left_side)
        pair_of = jnp.zeros((GB,), jnp.int32).at[left_side].set(pair_ids).at[right_side].set(pair_ids)
        flipped = jnp.zeros((GB,), jnp.int32).at[right_side].set(1)
        return (partner, pair_of, flipped)
    partner, pair_of, flipped = jax.vmap(single)(sub_keys)
    return (partner.reshape(N_ROW, MATCH, GB), pair_of.reshape(N_ROW, MATCH, GB), flipped.reshape(N_ROW, MATCH, GB))


def draw_adj_index(key, part):
    partner, pair_of, flipped = match_tables(key)
    diagonal = jnp.broadcast_to(jnp.arange(GB, dtype=jnp.int32)[None, :, None], (N_ROW, GB, 1))
    partner_blocks = partner.transpose(0, 2, 1)
    assembled = jnp.concatenate([diagonal, partner_blocks], axis=2)
    return assembled.reshape(N_ROW * N_COL, NBL).astype(jnp.int32)


def draw_adj_values(key, part):
    partner, pair_of, flipped = match_tables(key)
    key = jax.random.fold_in(key, 11)
    diag_key, pair_key = jax.random.split(key)
    block_scale = (BLOCK * (MATCH + 1)) ** (-0.5)
    diag_shape = (N_ROW, GB, BLOCK, BLOCK)
    pair_shape = (N_ROW, MATCH, GB // 2, BLOCK, BLOCK)
    diag_raw = jax.random.normal(diag_key, diag_shape, jnp.float32)
    pair_raw = jax.random.normal(pair_key, pair_shape, jnp.float32)
    diagonal = (diag_raw + diag_raw.transpose(0, 1, 3, 2)) * (block_scale * 0.7071)
    pair_raw = pair_raw * block_scale
    picked = jax.vmap(jax.vmap(lambda blocks_all, which: blocks_all[which]))(pair_raw, pair_of)
    oriented = jnp.where(flipped[..., None, None] > 0, picked.transpose(0, 1, 2, 4, 3), picked)
    partner_blocks = oriented.transpose(0, 2, 1, 3, 4)
    assembled = jnp.concatenate([diagonal[:, :, None], partner_blocks], axis=2)
    return assembled.reshape(N_ROW * N_COL, NBL, BLOCK, BLOCK).astype(jnp.bfloat16)


def draw_owner_of(key, part):
    key = jax.random.fold_in(key, 3)
    col_keys = jax.random.split(key, N_COL)
    share = NODES_DEV // N_ROW

    def column(col_key):
        pattern_key, shuffle_key = jax.random.split(col_key)
        offset_rank = jax.random.permutation(pattern_key, N_ROW).astype(jnp.int32)
        per_offset = jnp.where(offset_rank < N_ROW // 4, 3 * share, jnp.where(offset_rank < N_ROW // 2, share, 0))
        source_ids = jnp.arange(N_ROW, dtype=jnp.int32)[:, None]
        dest_ids = jnp.arange(N_ROW, dtype=jnp.int32)[None, :]
        counts = per_offset[(dest_ids - source_ids) % N_ROW]
        bounds = jnp.cumsum(counts, axis=1)
        slot_ids = jnp.arange(NODES_DEV, dtype=jnp.int32)
        dest_of = jnp.sum((bounds[:, None, :] <= slot_ids[None, :, None]).astype(jnp.int32), axis=2)
        shuffle_keys = jax.random.split(shuffle_key, N_ROW)
        shuffled = jax.vmap(lambda subkey, listing: listing[jax.random.permutation(subkey, NODES_DEV)])(shuffle_keys, dest_of)
        return shuffled.reshape(-1)
    return jax.vmap(column)(col_keys).astype(jnp.int32)


def raised(result, rng, source, target, blocks, factor):
    def block_of(dim):
        return (jnp.arange(result.shape[dim]) // (result.shape[dim] // blocks)).reshape((-1,) + (1,) * (result.ndim - 1 - dim))

    near = jax.random.permutation(rng, blocks)[block_of(target)]
    second = (block_of(target) + blocks // 2) % blocks
    return jnp.where((block_of(source) == near) | (block_of(source) == second), factor * result, result)


def block_levels(rng, extent, shards, smallest, top_value):
    level = 1.0
    for axis_at, blocks in shards:
        heights = jax.random.uniform(jax.random.fold_in(jax.random.fold_in(rng, 6), axis_at), (blocks,), jnp.float32, smallest / len(shards), top_value / len(shards))
        level = level * jnp.repeat(jnp.exp(heights), extent[axis_at] // blocks).reshape((-1,) + (1,) * (len(extent) - 1 - axis_at))
    return level


def centred(own_key, shape, spread, reach, cuts=(), kind=jnp.bfloat16):
    result = jax.random.normal(own_key, shape, jnp.float32) * spread
    if len(cuts) > 0:
        result = block_levels(own_key, shape, cuts, -0.22, 0.18) * result
    return jnp.clip(result, min=-reach, max=reach).astype(kind)


def noise_with(own_key, extent, spread, most, cuts, heavy, kind=jnp.bfloat16):
    drawn = spread * jax.random.normal(own_key, extent, jnp.float32)
    if cuts:
        drawn = drawn * block_levels(own_key, extent, cuts, -0.22, 0.18)
    return jnp.clip(raised(drawn, jax.random.fold_in(own_key, 3), *heavy), -most, most).astype(kind)


def setup_inputs(seed: int = 0) -> dict:
    arg_keys = jax.random.split(jax.random.key(seed), 9)
    doc_taps = noise_with(arg_keys[0], (NODES, TPD, DL), 1.0, 24.0, ((0, 128),), (0, 2, 128, 5.5))
    w_down = centred(arg_keys[1], (DL, H), DL ** -0.5, 0.078125)
    owner_of = draw_owner_of(jax.random.fold_in(arg_keys[8], 71), 0)
    adj_values = draw_adj_values(jax.random.fold_in(arg_keys[8], 71), 0)
    adj_index = draw_adj_index(jax.random.fold_in(arg_keys[8], 71), 0)
    w_msg = centred(arg_keys[5], (H, H), H ** -0.5, 0.25)
    gate_scale = jnp.clip(jax.random.uniform(arg_keys[6], (H,), jnp.float32, 0.5, 1.5), 0.5, 1.5)
    cotangent = noise_with(arg_keys[7], (NODES, H), NODES ** -0.5, 0.078125, ((0, 128),), (0, 1, 128, 5.5))
    return {"doc_taps": doc_taps, "w_down": w_down, "owner_of": owner_of, "adj_values": adj_values, "adj_index": adj_index, "w_msg": w_msg, "gate_scale": gate_scale, "cotangent": cotangent}


def dense_tile(values, index):
    row_ids = jnp.arange(NBL, dtype=jnp.int32) // (MATCH + 1)
    layout = jnp.zeros((RB, GB, BLOCK, BLOCK), jnp.float32)
    layout = layout.at[row_ids, index.astype(jnp.int32)].add(values.astype(jnp.float32))
    return layout.transpose(0, 2, 1, 3).reshape(RB * BLOCK, GB * BLOCK).astype(jnp.bfloat16)


def relay_order(owner_of):
    columns_list = []
    for column in range(N_COL):
        ordering = jnp.argsort(owner_of[column], stable=True).astype(jnp.int32)
        source_row = ordering // NODES_DEV
        position = ordering % NODES_DEV
        global_row = (source_row * N_COL + column) * NODES_DEV + position
        columns_list.append(global_row.reshape(N_ROW, NODES_DEV))
    return jnp.stack(columns_list, axis=1).reshape(NODES).astype(jnp.int32)


def reference(doc_taps, w_down, owner_of, adj_values, adj_index, w_msg, gate_scale, cotangent):
    pooled = (jnp.sum(doc_taps.astype(jnp.float32), axis=1) / TPD).astype(jnp.bfloat16)
    side = jnp.dot(pooled, w_down, preferred_element_type=jnp.float32).astype(jnp.bfloat16)
    mapping = relay_order(owner_of)
    owned = side[mapping]
    group_vals = adj_values.reshape(N_ROW, N_COL, NBL, BLOCK, BLOCK)
    group_index = adj_index.reshape(N_ROW, N_COL, NBL)

    def forward_group(packed):
        values, index, features = packed
        pieces = []
        for column in range(N_COL):
            tile_now = dense_tile(values[column], index[column])
            pieces.append(jnp.dot(tile_now, features, preferred_element_type=jnp.float32))
        return jnp.concatenate(pieces, axis=0)

    aggregate = lax.map(forward_group, (group_vals, group_index, owned.reshape(N_ROW, GROUP, H)))
    aggregate = aggregate.reshape(NODES, H).astype(jnp.bfloat16)
    message = jnp.dot(aggregate, w_msg, preferred_element_type=jnp.float32)
    squash = jax.nn.sigmoid(message)
    activated = message * squash
    side_out = (owned.astype(jnp.float32) + gate_scale * activated).astype(jnp.bfloat16)
    upstream = cotangent.astype(jnp.float32)
    message_grad = (upstream * gate_scale * squash * (1.0 + message * (1.0 - squash))).astype(jnp.bfloat16)
    grad_gate = jnp.sum(upstream * activated, axis=0)
    grad_msg = jnp.dot(aggregate.T, message_grad, preferred_element_type=jnp.float32)
    aggregate_grad = jnp.dot(message_grad, w_msg.T, preferred_element_type=jnp.float32).astype(jnp.bfloat16)

    def backward_group(packed):
        values, index, grads_here = packed
        total = jnp.zeros((GROUP, H), jnp.float32)
        for column in range(N_COL):
            tile_now = dense_tile(values[column], index[column])
            rows_here = grads_here[column * NODES_DEV:(column + 1) * NODES_DEV]
            total = total + jnp.dot(tile_now.T, rows_here, preferred_element_type=jnp.float32)
        return total

    returned = lax.map(backward_group, (group_vals, group_index, aggregate_grad.reshape(N_ROW, GROUP, H)))
    owned_grad = (upstream + returned.reshape(NODES, H)).astype(jnp.bfloat16)
    side_grad = jnp.zeros_like(owned_grad).at[mapping].set(owned_grad)
    grad_down = jnp.dot(pooled.T, side_grad, preferred_element_type=jnp.float32)
    return side_out, grad_down, grad_msg, grad_gate
```

```python
import jax
import jax.numpy as jnp
import numpy as np
from jax import lax
from jax.experimental import pallas as pl
from jax.experimental.pallas import tpu as pltpu
from jax.sharding import Mesh
from jax.sharding import PartitionSpec as P

ROWS = ("z", "x", "core")
BF16 = jnp.bfloat16
F32 = jnp.float32
SLOTS = 72


def iota(shape, dim):
    return lax.broadcasted_iota(jnp.int32, shape, dim)


def one_hot(mask):
    return jnp.where(mask, 1.0, 0.0).astype(BF16)


def params(mib):
    return pltpu.CompilerParams(vmem_limit_bytes=mib * 1024 * 1024)


def cost(flops, moved, special=0):
    return pl.CostEstimate(flops=int(flops), bytes_accessed=int(moved), transcendentals=int(special))


def whole(*shape):
    return pl.BlockSpec(shape, lambda i: (0,) * len(shape))


def pool_tiles(pick, x_ref, pooled_ref):
    tiles = x_ref.shape[1] // 16
    for group in range(x_ref.shape[0] // 16):
        docs = pl.ds(group * 16, 16)
        block = jnp.concatenate(
            [x_ref[docs, t * 16:(t + 1) * 16, :].reshape(256, 128) for t in range(tiles)], axis=1
        )
        mean = jnp.dot(pick[...], block, preferred_element_type=F32).astype(BF16)
        for j in range(8):
            for t in range(tiles):
                at = (t * 8 + j) * 128
                pooled_ref[docs, at:at + 128] = mean[j * 16:(j + 1) * 16, t * 128:(t + 1) * 128]


def pack_rows(slot, side, out_ref):
    docs = side.shape[0]
    step = out_ref.shape[0] // 6
    for part in range(6):
        rows = iota((step, docs), 0) + part * step
        chosen = one_hot(rows == slot)
        out_ref[part * step:(part + 1) * step, :] = jnp.dot(
            chosen, side, preferred_element_type=F32
        ).astype(BF16)


def pool_kernel(owner_ref, x_ref, w_ref, pooled_ref, out_ref, slot_ref, pick, side):
    at = pl.program_id(0)
    step = x_ref.shape[0]
    docs = side.shape[0]

    @pl.when(at == 0)
    def _():
        out_row, in_row = iota((128, 256), 0), iota((128, 256), 1)
        same_doc = out_row % 16 == in_row // 16
        same_tile = out_row // 16 == (in_row % 16) // 2
        pick[...] = jnp.where(same_doc & same_tile, 0.5, 0.0).astype(BF16)

    pool_tiles(pick, x_ref, pooled_ref)
    side[pl.ds(pl.multiple_of(at * step, step), step), :] = jnp.dot(
        pooled_ref[...], w_ref[...], preferred_element_type=F32
    ).astype(BF16)

    @pl.when(at == pl.num_programs(0) - 1)
    def _():
        first = pl.multiple_of(lax.axis_index(ROWS) * docs, 128)
        dest = owner_ref[:, pl.ds(first, docs)]
        hit = iota((32, docs), 0) == dest
        earlier = one_hot(iota((docs, docs), 0) < iota((docs, docs), 1))
        before = jnp.dot(one_hot(hit), earlier, preferred_element_type=F32)
        rank = jnp.sum(jnp.where(hit, before, 0.0), axis=0, keepdims=True)
        slot = dest * SLOTS + rank.astype(jnp.int32)
        slot_ref[...] = slot
        pack_rows(slot, side[...], out_ref)


def pool_and_pack(owner_of, doc_taps, w_down, wide, slots):
    docs, tokens, depth = doc_taps.shape
    tiles = depth // 128
    taps = doc_taps.reshape(docs, tokens, tiles, 128).transpose(0, 2, 1, 3)
    taps = taps.reshape(docs, tokens * tiles, 128)
    step = 128
    return pl.pallas_call(
        pool_kernel,
        grid=(docs // step,),
        in_specs=[
            whole(*owner_of.shape),
            pl.BlockSpec((step, tokens * tiles, 128), lambda i: (i, 0, 0)),
            whole(depth, wide),
        ],
        out_specs=[
            pl.BlockSpec((step, depth), lambda i: (i, 0)),
            whole(slots, wide),
            whole(1, docs),
        ],
        out_shape=[
            jax.ShapeDtypeStruct((docs, depth), BF16),
            jax.ShapeDtypeStruct((slots, wide), BF16),
            jax.ShapeDtypeStruct((1, docs), jnp.int32),
        ],
        scratch_shapes=[pltpu.VMEM((128, 256), BF16), pltpu.VMEM((docs, wide), BF16)],
        compiler_params=params(56),
        cost_estimate=cost(6e9, 28e6),
    )(owner_of, taps, w_down)


def project_kernel(slot_ref, pooled_ref, w_ref, out_ref, total):
    at = pl.program_id(0)
    term = jnp.dot(pooled_ref[...], w_ref[...], preferred_element_type=F32)

    @pl.when(at == 0)
    def _():
        total[...] = term

    @pl.when(at > 0)
    def _():
        total[...] += term

    @pl.when(at == pl.num_programs(0) - 1)
    def _():
        pack_rows(slot_ref[...], total[...].astype(BF16), out_ref)


def project_and_pack(slot, pooled, w_down, wide, chunk, slots):
    docs, depth = pooled.shape
    step = depth // 5
    return pl.pallas_call(
        project_kernel,
        grid=(5,),
        in_specs=[
            whole(1, docs),
            pl.BlockSpec((docs, step), lambda i: (0, i)),
            pl.BlockSpec((step, wide), lambda i: (i, chunk)),
        ],
        out_specs=whole(slots, wide),
        out_shape=jax.ShapeDtypeStruct((slots, wide), BF16),
        scratch_shapes=[pltpu.VMEM((docs, wide), F32)],
        compiler_params=params(24),
        cost_estimate=cost(3e9, 12e6),
    )(slot, pooled, w_down)


def turn_kernel(pooled_ref, mine_ref, theirs_ref):
    turned = pooled_ref[...].T
    rows = mine_ref.shape[2]
    cols = mine_ref.shape[0]
    core = lax.axis_index("core")
    for this in range(2):
        @pl.when(core == this)
        def _():
            for out_ref, which in ((mine_ref, this), (theirs_ref, 1 - this)):
                for chip in range(mine_ref.shape[1]):
                    for col in range(cols):
                        at = ((chip * 2 + which) * cols + col) * rows
                        out_ref[col, chip] = turned[at:at + rows, :]


def turn(pooled, chips, cols):
    docs, depth = pooled.shape
    rows = depth // (2 * chips * cols)
    pair = 4 * cols * rows
    out = jax.ShapeDtypeStruct((cols, chips, rows, docs), BF16)
    return pl.pallas_call(
        turn_kernel,
        grid=(chips // 2,),
        in_specs=[pl.BlockSpec((docs, pair), lambda i: (0, i))],
        out_specs=[pl.BlockSpec((cols, 2, rows, docs), lambda i: (0, i, 0, 0))] * 2,
        out_shape=[out, out],
        compiler_params=params(24),
        cost_estimate=cost(1e9, 16e6),
    )(pooled)


def take_kernel(place_ref, table_ref, out_ref):
    step, depth = out_ref.shape[0], table_ref.shape[0]
    if place_ref.shape[0] == 1:
        mask = iota((step, depth), 0) + pl.program_id(0) * step == place_ref[...]
    else:
        mask = iota((step, depth), 1) == place_ref[...]
    out_ref[...] = jnp.dot(one_hot(mask), table_ref[...], preferred_element_type=F32).astype(BF16)


def take(place, table, count):
    depth, width = table.shape
    step = count // 3
    if place.shape[0] == 1:
        place_spec = whole(1, depth)
    else:
        place_spec = pl.BlockSpec((step, 1), lambda i: (i, 0))
    return pl.pallas_call(
        take_kernel,
        grid=(3,),
        in_specs=[place_spec, whole(depth, width)],
        out_specs=pl.BlockSpec((step, width), lambda i: (i, 0)),
        out_shape=jax.ShapeDtypeStruct((count, width), BF16),
        compiler_params=params(20),
        cost_estimate=cost(2 * count * depth * width, 2e6),
    )(place, table)


def gather_col(part):
    up = [(c, (c + 1) % 4) for c in range(4)]
    down = [(c, (c + 3) % 4) for c in range(4)]
    half = part.shape[0] // 2
    before = lax.ppermute(part, "col", up)
    after = lax.ppermute(part, "col", down)
    low = lax.ppermute(before[:half], "col", up)
    high = lax.ppermute(after[half:], "col", down)
    return part, after, low, high, before


def stage(parts, table):
    at = 0
    for part in parts:
        table[at:at + part.shape[0], :] = part[...]
        at += part.shape[0]


def block_row(index_ref, values_ref, table, row, per_row):
    total = None
    for k in range(per_row):
        entry = row * per_row + k
        at = pl.multiple_of(index_ref[entry] * 128, 128)
        term = jnp.dot(values_ref[entry], table[pl.ds(at, 128), :], preferred_element_type=F32)
        total = term if total is None else total + term
    return total


def product_kernel(index_ref, values_ref, *refs):
    parts, (out_ref, table) = refs[:5], refs[5:]
    stage(parts, table)
    rows = out_ref.shape[0] // 128
    per_row = values_ref.shape[0] // rows
    for row in range(rows):
        out_ref[row * 128:(row + 1) * 128, :] = block_row(
            index_ref, values_ref, table, row, per_row
        ).astype(BF16)


def product(index, values, parts):
    nodes, width = parts[0].shape
    vmem = pl.BlockSpec(memory_space=pltpu.VMEM)
    return pl.pallas_call(
        product_kernel,
        in_specs=[pl.BlockSpec(memory_space=pltpu.SMEM)] + [vmem] * 6,
        out_specs=vmem,
        out_shape=jax.ShapeDtypeStruct((nodes, width), BF16),
        scratch_shapes=[pltpu.VMEM((4 * nodes, width), BF16)],
        compiler_params=params(16),
        cost_estimate=cost(2e8, 3e6),
    )(index, values, *parts)


def layer_kernel(index_ref, values_ref, *refs):
    parts = refs[:5]
    (first_ref, owned_ref, cot_ref, w_ref, wt_ref, gate_ref) = refs[5:11]
    (side_out_ref, agg_ref, mgrad_ref, agrad0_ref, agrad1_ref, gpart_ref, table) = refs[11:]
    at = pl.program_id(0)

    @pl.when(at == 0)
    def _():
        stage(parts, table)

    step = cot_ref.shape[0]
    wide = first_ref.shape[1]
    nodes = step * pl.num_programs(0)
    per_row = values_ref.shape[0] * 128 // nodes
    rows = step // 128
    agg_ref[:, :wide] = first_ref[...]
    for row in range(rows):
        agg_ref[row * 128:(row + 1) * 128, wide:] = block_row(
            index_ref, values_ref, table, at * rows + row, per_row
        ).astype(BF16)
    message = jnp.dot(agg_ref[...], w_ref[...], preferred_element_type=F32)
    squash = jax.nn.sigmoid(message)
    activated = message * squash
    gate = gate_ref[...]
    upstream = cot_ref[...].astype(F32)
    owned = jnp.concatenate(
        [owned_ref[...], parts[0][pl.ds(pl.multiple_of(at * step, step), step), :]], axis=1
    )
    side_out_ref[...] = (owned.astype(F32) + gate * activated).astype(BF16)
    mgrad = (upstream * gate * squash * (1.0 + message * (1.0 - squash))).astype(BF16)
    mgrad_ref[...] = mgrad
    agrad = jnp.dot(mgrad, wt_ref[...], preferred_element_type=F32).astype(BF16)
    agrad0_ref[...] = agrad[:, :wide]
    agrad1_ref[...] = agrad[:, wide:]
    part = jnp.sum(upstream * activated, axis=0, keepdims=True)

    @pl.when(at == 0)
    def _():
        gpart_ref[...] = part

    @pl.when(at > 0)
    def _():
        gpart_ref[...] += part


def layer(index, values, parts, first, owned, cotangent, w_msg, gate):
    nodes, width = cotangent.shape
    wide = width // 2
    step = 256
    rows = lambda size: pl.BlockSpec((step, size), lambda i: (i, 0))
    shape = lambda size: jax.ShapeDtypeStruct((nodes, size), BF16)
    return pl.pallas_call(
        layer_kernel,
        grid=(nodes // step,),
        in_specs=[pl.BlockSpec(memory_space=pltpu.SMEM), whole(*values.shape)]
        + [whole(*part.shape) for part in parts]
        + [rows(wide), rows(wide), rows(width), whole(width, width), whole(width, width),
           whole(1, width)],
        out_specs=[rows(width), rows(width), rows(width), rows(wide), rows(wide), whole(1, width)],
        out_shape=[shape(width), shape(width), shape(width), shape(wide), shape(wide),
                   jax.ShapeDtypeStruct((1, width), F32)],
        scratch_shapes=[pltpu.VMEM((4 * nodes, wide), BF16)],
        compiler_params=params(32),
        cost_estimate=cost(12e8, 8e6, nodes * width),
    )(index, values, *parts, first, owned, cotangent, w_msg, w_msg.T, gate)


def back_kernel(index_ref, values_ref, *refs):
    parts = refs[:5]
    cot_ref, place_ref, out_ref, table, grad = refs[5:]
    nodes = cot_ref.shape[0]
    per_row = values_ref.shape[0] * 128 // nodes

    @pl.when(pl.program_id(0) == 0)
    def _():
        stage(parts, table)
        for row in range(nodes // 128):
            at = slice(row * 128, (row + 1) * 128)
            total = block_row(index_ref, values_ref, table, row, per_row)
            grad[at, :] = (cot_ref[at, :].astype(F32) + total).astype(BF16)

    mask = iota((out_ref.shape[0], nodes), 1) == place_ref[...]
    out_ref[...] = jnp.dot(one_hot(mask), grad[...], preferred_element_type=F32).astype(BF16)


def back(index, values, parts, cotangent, chunk, place, slots):
    nodes, wide = parts[0].shape
    step = slots // 6
    return pl.pallas_call(
        back_kernel,
        grid=(6,),
        in_specs=[pl.BlockSpec(memory_space=pltpu.SMEM), whole(*values.shape)]
        + [whole(*part.shape) for part in parts]
        + [pl.BlockSpec((nodes, wide), lambda i: (0, chunk)),
           pl.BlockSpec((step, 1), lambda i: (i, 0))],
        out_specs=pl.BlockSpec((step, wide), lambda i: (i, 0)),
        out_shape=jax.ShapeDtypeStruct((slots, wide), BF16),
        scratch_shapes=[pltpu.VMEM((4 * nodes, wide), BF16), pltpu.VMEM((nodes, wide), BF16)],
        compiler_params=params(24),
        cost_estimate=cost(2 * slots * nodes * wide, 5e6),
    )(index, values, *parts, cotangent, place)


def relay(rows):
    slots, width = rows.shape
    size = lax.axis_size(ROWS)
    moved = lax.all_to_all(
        rows.reshape(size, slots // size, width), ROWS, split_axis=0, concat_axis=0, tiled=True
    )
    return moved.reshape(slots, width)


def col_pieces(part):
    return [lax.ppermute(part, "col", [(c, c ^ step) for c in range(4)]) for step in (1, 2, 3)]


def shards(doc_taps, w_down, owner_of, adj_values, adj_index, w_msg, gate_scale, cotangent):
    docs = doc_taps.shape[0]
    depth, width = w_down.shape
    wide = width // 2
    row_size, cols = lax.axis_size(ROWS), lax.axis_size("col")
    my_row, my_col = lax.axis_index(ROWS), lax.axis_index("col")
    slots = row_size * SLOTS
    chips = row_size // 2
    share = depth // row_size
    piece = share // cols
    values = adj_values[0]
    blocks = docs // 128
    index = (adj_index[0] // blocks - my_col) % cols * blocks + adj_index[0] % blocks
    gate = gate_scale.reshape(1, width)

    pooled, packed, slot = pool_and_pack(owner_of, doc_taps, w_down, wide, slots)
    incoming0 = relay(packed)
    incoming1 = relay(project_and_pack(slot, pooled, w_down, wide, 1, slots))

    owners = owner_of[0]
    counts = jnp.sum((owners.reshape(row_size, docs) == my_row).astype(jnp.int32), axis=1)
    lower = jnp.arange(row_size)[None, :] < jnp.arange(row_size)[:, None]
    starts = jnp.sum(jnp.where(lower, counts[None, :], 0), axis=1)
    in_slot = jnp.arange(SLOTS, dtype=jnp.int32)[None, :]
    position = jnp.where(in_slot < counts[:, None], starts[:, None] + in_slot, -1).reshape(slots)
    pos_row, pos_col = position.reshape(1, slots), position.reshape(slots, 1)

    owned0 = take(pos_row, incoming0, docs)
    parts0 = gather_col(owned0)
    owned1 = take(pos_row, incoming1, docs)
    parts1 = gather_col(owned1)
    first = product(index, values, parts0)
    side_out, aggregate, message_grad, agrad0, agrad1, gate_part = layer(
        index, values, parts1, first, owned0, cotangent, w_msg, gate
    )

    mine, theirs = turn(pooled, chips, cols)
    mine = mine.reshape(depth // 2, docs)
    swap = [(0, 1), (1, 0)]
    other = lax.ppermute(theirs.reshape(depth // 2, docs), "core", swap)

    msg_part = lax.dot_general(
        aggregate, message_grad, (((0,), (0,)), ((), ())), preferred_element_type=F32
    )
    msg_share = width // row_size
    gate_rows = jnp.pad(
        gate_part.reshape(row_size, 1, msg_share), ((0, 0), (0, 7), (0, width - msg_share))
    )
    small = jnp.concatenate([msg_part.reshape(row_size, msg_share, width), gate_rows], axis=1)
    small = lax.all_to_all(small, ROWS, split_axis=0, concat_axis=0, tiled=True)

    slot_col = slot.reshape(docs, 1)
    downs = []
    for chunk, agrad in enumerate((agrad0, agrad1)):
        gparts = gather_col(agrad)
        back_in = relay(back(index, values, gparts, cotangent, chunk, pos_col, slots))
        side_grad = take(slot_col, back_in, docs)
        other_grad = lax.ppermute(side_grad, "core", swap)
        down_part = jnp.dot(mine, side_grad, preferred_element_type=F32) + jnp.dot(
            other, other_grad, preferred_element_type=F32
        )
        by_col = lax.all_to_all(
            down_part.astype(BF16).reshape(cols, chips * piece, wide),
            "col", split_axis=0, concat_axis=0, tiled=True,
        )
        by_col = jnp.sum(by_col.astype(F32), axis=0).astype(BF16)
        by_chip = lax.all_to_all(
            by_col.reshape(chips, piece, wide), ("z", "x"), split_axis=0, concat_axis=0, tiled=True
        )
        downs.append(jnp.sum(by_chip.astype(F32), axis=0))

    down = jnp.concatenate(downs, axis=1)
    found = [down] + col_pieces(down)
    rows = []
    for col in range(cols):
        row = found[0]
        for step in (1, 2, 3):
            row = jnp.where(my_col ^ step == col, found[step], row)
        rows.append(row)
    grad_down = jnp.concatenate(rows, axis=0)

    small_sum = jnp.sum(small, axis=0)
    near, far, cross = col_pieces(small_sum)
    small_sum = (small_sum + near) + (far + cross)
    grad_msg = small_sum[:msg_share]
    grad_gate = small_sum[msg_share, :msg_share]
    return side_out, grad_down, grad_msg, grad_gate


def solution(mesh):
    rows, cols = mesh.devices.shape
    z = 4
    x = rows // (2 * z)
    split = Mesh(mesh.devices.reshape(z, x, 2, cols), ("z", "x", "core", "col"))
    each = ROWS + ("col",)
    placed = (
        P(each, None, None),
        P(),
        P("col", None),
        P(each, None, None, None),
        P(each, None),
        P(),
        P(),
        P(each, None),
    )
    return jax.shard_map(
        shards,
        mesh=split,
        in_specs=placed,
        out_specs=(P(each, None), P(ROWS, None), P(ROWS, None), P(ROWS)),
        check_vma=False,
    )
```

```python
import functools

import jax
import jax.numpy as jnp
import numpy as np
from jax import lax
from jax.experimental import pallas as pl
from jax.experimental.pallas import tpu as pltpu
from jax.sharding import Mesh
from jax.sharding import PartitionSpec as P

ROWS = ("z", "x", "core")
BF16 = jnp.bfloat16
F32 = jnp.float32
SLOTS = 72


def iota(shape, dim):
    return lax.broadcasted_iota(jnp.int32, shape, dim)


def one_hot(mask):
    return jnp.where(mask, 1.0, 0.0).astype(BF16)


def params(mib=60):
    return pltpu.CompilerParams(vmem_limit_bytes=mib * 1024 * 1024)


def cost(flops, moved, special=0):
    return pl.CostEstimate(flops=int(flops), bytes_accessed=int(moved), transcendentals=int(special))


def whole(*shape):
    return pl.BlockSpec(shape, lambda i: (0,) * len(shape))


def bf16(*shape):
    return jax.ShapeDtypeStruct(shape, BF16)


def pool_tiles(pick, x_ref, pooled_ref):
    tiles = x_ref.shape[1] // 16
    for group in range(x_ref.shape[0] // 16):
        docs = pl.ds(group * 16, 16)
        block = jnp.concatenate(
            [x_ref[docs, t * 16:(t + 1) * 16, :].reshape(256, 128) for t in range(tiles)], axis=1
        )
        mean = jnp.dot(pick[...], block, preferred_element_type=F32).astype(BF16)
        for j in range(8):
            for t in range(tiles):
                at = (t * 8 + j) * 128
                pooled_ref[docs, at:at + 128] = mean[j * 16:(j + 1) * 16, t * 128:(t + 1) * 128]


def project_block(x_ref, w_hbm, first, pick, pooled, side, w_ref, w_sem):
    at = pl.program_id(0)
    step = x_ref.shape[0]
    load = pltpu.make_async_copy(w_hbm.at[:, pl.ds(first, w_ref.shape[1])], w_ref, w_sem)

    @pl.when(at == 0)
    def _():
        load.start()
        out_row, in_row = iota((128, 256), 0), iota((128, 256), 1)
        same_doc = out_row % 16 == in_row // 16
        same_tile = out_row // 16 == (in_row % 16) // 2
        pick[...] = jnp.where(same_doc & same_tile, 0.5, 0.0).astype(BF16)

    pool_tiles(pick, x_ref, pooled)

    @pl.when(at == 0)
    def _():
        load.wait()

    side[pl.ds(pl.multiple_of(at * step, step), step), :] = jnp.dot(
        pooled[...], w_ref[...], preferred_element_type=F32
    ).astype(BF16)


def pool_kernel(owner_ref, x_ref, w_hbm, out_ref, slot_ref,
                pick, pooled, side, w_ref, w_sem, chosen):
    at = pl.program_id(0)
    docs = side.shape[0]
    share = out_ref.shape[0] // 6

    @pl.when(at == 0)
    def _():
        first = pl.multiple_of(lax.axis_index(ROWS) * docs, 128)
        dest = owner_ref[:, pl.ds(first, docs)]
        hit = iota((32, docs), 0) == dest
        earlier = one_hot(iota((docs, docs), 0) < iota((docs, docs), 1))
        before = jnp.dot(one_hot(hit), earlier, preferred_element_type=F32)
        rank = jnp.sum(jnp.where(hit, before, 0.0), axis=0, keepdims=True)
        slot_ref[...] = dest * SLOTS + rank.astype(jnp.int32)

    project_block(x_ref, w_hbm, 0, pick, pooled, side, w_ref, w_sem)
    rows = iota((share, docs), 0) + at * share
    chosen[pl.ds(pl.multiple_of(at * share, 16), share), :] = one_hot(rows == slot_ref[...])

    @pl.when(at == pl.num_programs(0) - 1)
    def _():
        for part in range(6):
            rows = slice(part * share, (part + 1) * share)
            out_ref[rows, :] = jnp.dot(
                chosen[rows, :], side[...], preferred_element_type=F32
            ).astype(BF16)


def turn_kernel(slot_ref, x_ref, w_hbm, out_ref, mine_ref, theirs_ref,
                pick, pooled, side, w_ref, w_sem):
    first = w_hbm.shape[1] - w_ref.shape[1]
    project_block(x_ref, w_hbm, first, pick, pooled, side, w_ref, w_sem)
    rows = mine_ref.shape[1]
    core = lax.axis_index("core")
    for pair in range(mine_ref.shape[0] // 2):
        turned = pooled[:, pair * 4 * rows:(pair + 1) * 4 * rows].T
        for this in range(2):
            @pl.when(core == this)
            def _():
                for turned_ref, which in ((mine_ref, this), (theirs_ref, 1 - this)):
                    for chip in range(2):
                        at = (chip * 2 + which) * rows
                        turned_ref[pair * 2 + chip] = turned[at:at + rows, :]

    @pl.when(pl.program_id(0) == pl.num_programs(0) - 1)
    def _():
        step = out_ref.shape[0] // 6
        for part in range(6):
            rows = iota((step, side.shape[0]), 0) + part * step
            out_ref[part * step:(part + 1) * step, :] = jnp.dot(
                one_hot(rows == slot_ref[...]), side[...], preferred_element_type=F32
            ).astype(BF16)


def taps_by_tile(doc_taps):
    docs, tokens, depth = doc_taps.shape
    tiles = depth // 128
    taps = doc_taps.reshape(docs, tokens, tiles, 128).transpose(0, 2, 1, 3)
    return taps.reshape(docs, tokens * tiles, 128)


def pool_scratch(step, docs, depth, wide):
    return [
        pltpu.VMEM((128, 256), BF16),
        pltpu.VMEM((step, depth), BF16),
        pltpu.VMEM((docs, wide), BF16),
        pltpu.VMEM((depth, wide), BF16),
        pltpu.SemaphoreType.DMA,
    ]


def pool_and_pack(owner_of, taps, w_down, wide, slots):
    docs, rows, _ = taps.shape
    step = docs // 6
    return pl.pallas_call(
        pool_kernel,
        grid=(6,),
        in_specs=[
            whole(*owner_of.shape),
            pl.BlockSpec((step, rows, 128), lambda i: (i, 0, 0)),
            pl.BlockSpec(memory_space=pl.ANY),
        ],
        out_specs=[whole(slots, wide), whole(1, docs)],
        out_shape=[bf16(slots, wide), jax.ShapeDtypeStruct((1, docs), jnp.int32)],
        scratch_shapes=pool_scratch(step, docs, w_down.shape[0], wide)
        + [pltpu.VMEM((slots, docs), BF16)],
        compiler_params=params(),
        cost_estimate=cost(6e9, 20e6),
    )(owner_of, taps, w_down)


def pool_and_turn(slot, taps, w_down, wide, slots, chips):
    docs, rows, _ = taps.shape
    depth = w_down.shape[0]
    step = docs // 6
    turned = pl.BlockSpec((chips, depth // (2 * chips), step), lambda i: (0, 0, i))
    shape = bf16(chips, depth // (2 * chips), docs)
    return pl.pallas_call(
        turn_kernel,
        grid=(6,),
        in_specs=[
            whole(1, docs),
            pl.BlockSpec((step, rows, 128), lambda i: (i, 0, 0)),
            pl.BlockSpec(memory_space=pl.ANY),
        ],
        out_specs=[whole(slots, wide), turned, turned],
        out_shape=[bf16(slots, wide), shape, shape],
        scratch_shapes=pool_scratch(step, docs, depth, wide),
        compiler_params=params(),
        cost_estimate=cost(6e9, 28e6),
    )(slot, taps, w_down)


def take_kernel(waited, place_ref, table_ref, *out_refs):
    at = pl.program_id(0)
    out_refs = out_refs[waited:]
    depth = table_ref.shape[0]
    step = out_refs[0].shape[0]
    if place_ref.shape[0] == 1:
        mask = iota((step, depth), 0) + at * step == place_ref[...]
    else:
        mask = iota((step, depth), 1) == place_ref[...]
    rows = jnp.dot(one_hot(mask), table_ref[...], preferred_element_type=F32).astype(BF16)
    if len(out_refs) == 1:
        out_refs[0][...] = rows
    else:
        for i, out_ref in enumerate(out_refs):
            @pl.when(at == i)
            def _():
                out_ref[...] = rows


def take(place, table, count, halves=False, after=()):
    depth, width = table.shape
    step = count // 2
    if place.shape[0] == 1:
        place_spec = whole(1, depth)
    else:
        place_spec = pl.BlockSpec((step, 1), lambda i: (i, 0))
    if halves:
        out_specs, out_shape = [whole(step, width)] * 2, [bf16(step, width)] * 2
    else:
        out_specs, out_shape = pl.BlockSpec((step, width), lambda i: (i, 0)), bf16(count, width)
    return pl.pallas_call(
        functools.partial(take_kernel, len(after)),
        grid=(2,),
        in_specs=[place_spec, whole(depth, width)]
        + [pl.BlockSpec(memory_space=pl.ANY) for _ in after],
        out_specs=out_specs,
        out_shape=out_shape,
        compiler_params=params(24),
        cost_estimate=cost(2 * count * depth * width, 2e6),
    )(place, table, *after)


def shift(part, by):
    return lax.ppermute(part, "col", [(c, (c + by) % 4) for c in range(4)])


def gather_ring(low, high):
    before_low, after_high = shift(low, 1), shift(high, 3)
    before_high, after_low = shift(high, 1), shift(low, 3)
    far_low, far_high = shift(before_low, 1), shift(after_high, 3)
    return low, high, after_low, after_high, far_low, far_high, before_low, before_high


def stage(parts, table):
    at = 0
    for part in parts:
        table[at:at + part.shape[0], :] = part[...]
        at += part.shape[0]


def block_row(index_ref, values_ref, table, row, per_row):
    total = None
    for k in range(per_row):
        entry = row * per_row + k
        at = pl.multiple_of(index_ref[entry] * 128, 128)
        term = jnp.dot(values_ref[entry], table[pl.ds(at, 128), :], preferred_element_type=F32)
        total = term if total is None else total + term
    return total


def product_kernel(index_ref, values_ref, *refs):
    parts, (out_ref, table) = refs[:-2], refs[-2:]
    stage(parts, table)
    rows = out_ref.shape[0] // 128
    per_row = values_ref.shape[0] // rows
    for row in range(rows):
        out_ref[row * 128:(row + 1) * 128, :] = block_row(
            index_ref, values_ref, table, row, per_row
        ).astype(BF16)


def product(index, values, parts, nodes):
    width = parts[0].shape[1]
    vmem = pl.BlockSpec(memory_space=pltpu.VMEM)
    return pl.pallas_call(
        product_kernel,
        in_specs=[pl.BlockSpec(memory_space=pltpu.SMEM), vmem] + [vmem] * len(parts),
        out_specs=vmem,
        out_shape=bf16(nodes, width),
        scratch_shapes=[pltpu.VMEM((4 * nodes, width), BF16)],
        compiler_params=params(),
        cost_estimate=cost(2e8, 3e6),
    )(index, values, *parts)


def layer_kernel(index_ref, values_ref, *refs):
    parts = refs[:8]
    (first_ref, low_in_ref, high_in_ref, cot_ref, w_ref, wt_ref, gate_ref) = refs[8:15]
    (side_out_ref, agg_ref, mgrad_ref, low_ref, high_ref, next_low_ref, next_high_ref,
     gpart_ref, table) = refs[15:]
    at = pl.program_id(0)

    @pl.when(at == 0)
    def _():
        stage(parts, table)

    step = cot_ref.shape[0]
    wide = first_ref.shape[1]
    lead = low_ref.shape[1]
    nodes = step * pl.num_programs(0)
    per_row = values_ref.shape[0] * 128 // nodes
    rows = step // 128
    agg_ref[:, :wide] = first_ref[...]
    for row in range(rows):
        agg_ref[row * 128:(row + 1) * 128, wide:] = block_row(
            index_ref, values_ref, table, at * rows + row, per_row
        ).astype(BF16)
    gate = gate_ref[...]
    part = None
    for third in range(rows):
        here = slice(third * 128, (third + 1) * 128)
        message = jnp.dot(agg_ref[here, :], w_ref[...], preferred_element_type=F32)
        squash = jax.nn.sigmoid(message)
        activated = message * squash
        upstream = cot_ref[here, :].astype(F32)
        at_row = pl.multiple_of(at * step + third * 128, 128)
        lead_in = jnp.where(at == 0, low_in_ref[here, :], high_in_ref[here, :])
        owned = jnp.concatenate([lead_in, table[pl.ds(at_row, 128), :]], axis=1)
        side_out_ref[here, :] = (owned.astype(F32) + gate * activated).astype(BF16)
        mgrad_ref[here, :] = (
            upstream * gate * squash * (1.0 + message * (1.0 - squash))
        ).astype(BF16)
        term = jnp.sum(upstream * activated, axis=0, keepdims=True)
        part = term if part is None else part + term
    agrad = jnp.dot(mgrad_ref[...], wt_ref[...], preferred_element_type=F32).astype(BF16)

    @pl.when(at == 0)
    def _():
        low_ref[...] = agrad[:, :lead]
        next_low_ref[...] = agrad[:, lead:]
        gpart_ref[...] = part

    @pl.when(at == 1)
    def _():
        high_ref[...] = agrad[:, :lead]
        next_high_ref[...] = agrad[:, lead:]
        gpart_ref[...] += part


def layer(index, values, parts, first, owned, cotangent, w_msg, gate, lead):
    nodes, width = cotangent.shape
    wide = first.shape[1]
    step = nodes // 2
    rows = lambda size: pl.BlockSpec((step, size), lambda i: (i, 0))
    return pl.pallas_call(
        layer_kernel,
        grid=(2,),
        in_specs=[pl.BlockSpec(memory_space=pltpu.SMEM), whole(*values.shape)]
        + [whole(*part.shape) for part in parts]
        + [rows(wide), whole(step, wide), whole(step, wide), rows(width), whole(width, width), whole(width, width),
           whole(1, width)],
        out_specs=[rows(width), rows(width), rows(width), whole(step, lead), whole(step, lead),
                   whole(step, width - lead), whole(step, width - lead), whole(1, width)],
        out_shape=[bf16(nodes, width), bf16(nodes, width), bf16(nodes, width), bf16(step, lead),
                   bf16(step, lead), bf16(step, width - lead), bf16(step, width - lead),
                   jax.ShapeDtypeStruct((1, width), F32)],
        scratch_shapes=[pltpu.VMEM((4 * nodes, width - wide), BF16)],
        compiler_params=params(),
        cost_estimate=cost(12e8, 8e6, nodes * width),
    )(index, values, *parts, first, *owned, cotangent, w_msg, w_msg.T, gate)


def back_kernel(first, index_ref, values_ref, *refs):
    parts, (cot_ref, place_ref), (out_ref, table, grad) = refs[:8], refs[8:10], refs[-3:]
    nodes = cot_ref.shape[0]
    per_row = values_ref.shape[0] * 128 // nodes

    @pl.when(pl.program_id(0) == 0)
    def _():
        stage(parts, table)
        for row in range(nodes // 128):
            at = slice(row * 128, (row + 1) * 128)
            total = block_row(index_ref, values_ref, table, row, per_row)
            upstream = cot_ref[at, first:first + total.shape[1]].astype(F32)
            grad[at, :] = (upstream + total).astype(BF16)

    mask = iota((out_ref.shape[0], nodes), 1) == place_ref[...]
    out_ref[...] = jnp.dot(one_hot(mask), grad[...], preferred_element_type=F32).astype(BF16)


def back(index, values, parts, cotangent, first, place, slots, after=()):
    nodes = cotangent.shape[0]
    wide = parts[0].shape[1]
    step = slots // 4
    return pl.pallas_call(
        functools.partial(back_kernel, first),
        grid=(4,),
        in_specs=[pl.BlockSpec(memory_space=pltpu.SMEM), whole(*values.shape)]
        + [whole(*part.shape) for part in parts]
        + [whole(*cotangent.shape), pl.BlockSpec((step, 1), lambda i: (i, 0))]
        + [pl.BlockSpec(memory_space=pl.ANY) for _ in after],
        out_specs=pl.BlockSpec((step, wide), lambda i: (i, 0)),
        out_shape=bf16(slots, wide),
        scratch_shapes=[pltpu.VMEM((4 * nodes, wide), BF16), pltpu.VMEM((nodes, wide), BF16)],
        compiler_params=params(),
        cost_estimate=cost(2 * slots * nodes * wide, 5e6),
    )(index, values, *parts, cotangent, place, *after)


def small_kernel(agg_ref, mgrad_ref, gate_ref, after_ref, mine_ref, theirs_ref):
    msg = lax.dot_general(
        agg_ref[...], mgrad_ref[...], (((0,), (0,)), ((), ())), preferred_element_type=F32
    )
    chips, rows, width = mine_ref.shape
    share = width // (2 * chips)
    tail = jnp.concatenate([gate_ref[...], jnp.zeros((rows - share - 1, width), F32)], axis=0)
    core = lax.axis_index("core")
    for this in range(2):
        @pl.when(core == this)
        def _():
            for out_ref, which in ((mine_ref, this), (theirs_ref, 1 - this)):
                for chip in range(chips):
                    at = (chip * 2 + which) * share
                    out_ref[chip, :share, :] = msg[at:at + share, :]
                    out_ref[chip, share:, :] = tail


def small_sums(aggregate, message_grad, gate_part, chips, after):
    width = aggregate.shape[1]
    vmem = pl.BlockSpec(memory_space=pltpu.VMEM)
    out = jax.ShapeDtypeStruct((chips, 24, width), F32)
    return pl.pallas_call(
        small_kernel,
        in_specs=[vmem] * 3 + [pl.BlockSpec(memory_space=pl.ANY)],
        out_specs=[vmem] * 2,
        out_shape=[out, out],
        compiler_params=params(),
        cost_estimate=cost(4e8, 4e6),
    )(aggregate, message_grad, gate_part, after)


def down_rows(mine_ref, other_ref, grad_ref, other_grad_ref):
    docs = mine_ref.shape[2]
    rows = mine_ref.shape[0] * mine_ref.shape[1]
    return jnp.dot(
        mine_ref[...].reshape(rows, docs), grad_ref[...], preferred_element_type=F32
    ) + jnp.dot(
        other_ref[...].reshape(rows, docs), other_grad_ref[...], preferred_element_type=F32
    )


def tiles_of(array):
    return [array[:, at:at + 128] for at in range(0, array.shape[1], 128)]


def two_terms(row):
    high = row.astype(BF16).astype(F32)
    return [high, row - high, jnp.zeros((6, 128), F32)]


def down_by_col_kernel(mine_ref, other_ref, grad_ref, other_grad_ref, small_ref,
                       other_small_ref, *out_refs):
    total = down_rows(mine_ref, other_ref, grad_ref, other_grad_ref)
    small = small_ref[...] + other_small_ref[...]
    chips = small.shape[0]
    msg = (small.shape[1] - 8) // 4
    piece = total.shape[0] // (4 * chips)
    blocks = []
    for chip in range(chips):
        for col in range(4):
            at = (chip * 4 + col) * piece
            gate = small[chip, 4 * msg:4 * msg + 1, col * 128:(col + 1) * 128]
            cells = (
                tiles_of(total[at:at + piece, :])
                + tiles_of(small[chip, col * msg:(col + 1) * msg, :])
                + two_terms(gate)
            )
            blocks.append(jnp.concatenate(cells, axis=0).astype(BF16))
    my_col = lax.axis_index("col")
    for first in range(4):
        @pl.when(my_col == first)
        def _():
            for k, out_ref in enumerate(out_refs):
                for chip in range(chips):
                    out_ref[chip] = blocks[chip * 4 + (first + k) % 4]


def lead_kernel(*refs):
    total = sum([ref[...].astype(F32) for ref in refs[1:4]], refs[0][...].astype(F32))
    out_ref = refs[4]
    at = total.shape[1] - 8
    for chip in range(total.shape[0]):
        gate = total[chip, at:at + 1, :] + total[chip, at + 1:at + 2, :]
        cells = [total[chip, :at, :]] + two_terms(gate)
        out_ref[chip] = jnp.concatenate(cells, axis=0).astype(BF16)


def lead_sum(pieces):
    vmem = pl.BlockSpec(memory_space=pltpu.VMEM)
    return pl.pallas_call(
        lead_kernel,
        in_specs=[vmem] * 4,
        out_specs=vmem,
        out_shape=bf16(*pieces[0].shape),
        compiler_params=params(24),
        cost_estimate=cost(1e6, 1e6),
    )(*pieces)


def down_by_chip_kernel(mine_ref, other_ref, grad_ref, other_grad_ref, led_ref, out_ref):
    total = down_rows(mine_ref, other_ref, grad_ref, other_grad_ref)
    chips, share, _ = mine_ref.shape
    led = out_ref.shape[1] - led_ref.shape[1]
    for chip in range(chips):
        cells = tiles_of(total[chip * share:(chip + 1) * share, :])
        out_ref[chip, :led, :] = jnp.concatenate(cells, axis=0).astype(BF16)
        out_ref[chip, led:, :] = led_ref[chip]


def down_specs(mine, grad):
    chips, share, docs = mine.shape
    rows = pl.BlockSpec((chips // 4, share, docs), lambda i: (i, 0, 0))
    return [rows, rows, whole(*grad.shape), whole(*grad.shape)]


def down_by_col(mine, other, grad, other_grad, small, other_small, cols):
    chips, share, docs = mine.shape
    rows = share // cols * grad.shape[1] // 128 + 24
    by_chip = pl.BlockSpec((chips // 4,) + small.shape[1:], lambda i: (i, 0, 0))
    return pl.pallas_call(
        down_by_col_kernel,
        grid=(4,),
        in_specs=down_specs(mine, grad) + [by_chip, by_chip],
        out_specs=[pl.BlockSpec((chips // 4, rows, 128), lambda i: (i, 0, 0))] * cols,
        out_shape=[bf16(chips, rows, 128)] * cols,
        compiler_params=params(),
        cost_estimate=cost(2e9, 10e6),
    )(mine, other, grad, other_grad, small, other_small)


def down_by_chip(mine, other, grad, other_grad, led):
    chips, share, docs = mine.shape
    rows = share * grad.shape[1] // 128 + led.shape[1]
    by_chip = lambda size: pl.BlockSpec((chips // 4, size, 128), lambda i: (i, 0, 0))
    return pl.pallas_call(
        down_by_chip_kernel,
        grid=(4,),
        in_specs=down_specs(mine, grad) + [by_chip(led.shape[1])],
        out_specs=by_chip(rows),
        out_shape=bf16(chips, rows, 128),
        compiler_params=params(),
        cost_estimate=cost(2e9, 12e6),
    )(mine, other, grad, other_grad, led)


def fold_kernel(parts_ref, out_ref):
    total = jnp.sum(parts_ref[...].astype(F32), axis=0)
    at = total.shape[0] - 8
    gate = total[at:at + 1, :] + total[at + 1:at + 2, :]
    out_ref[...] = jnp.concatenate([total[:at, :]] + two_terms(gate), axis=0).astype(BF16)


def fold(parts):
    chips, rows, width = parts.shape
    vmem = pl.BlockSpec(memory_space=pltpu.VMEM)
    return pl.pallas_call(
        fold_kernel,
        in_specs=[vmem],
        out_specs=vmem,
        out_shape=bf16(rows, width),
        compiler_params=params(24),
        cost_estimate=cost(1e6, 2e6),
    )(parts)


def finish_kernel(lead, *refs):
    found, (down_ref, msg_ref, gate_ref) = refs[:4], refs[4:]
    share, width = down_ref.shape
    msg = msg_ref.shape[0]
    piece = share // 4
    my_col = lax.axis_index("col")
    own, near, far, cross = (ref[...].astype(F32) for ref in found)
    total = (own + near) + (far + cross)
    at = 0
    for lane in range(lead, width, 128):
        down_ref[:, lane:lane + 128] = total[at:at + share, :]
        at += share

    def from_col(col):
        step = my_col ^ col
        part = own[at:, :]
        for i, other in enumerate((near, far, cross)):
            part = jnp.where(step == i + 1, other[at:, :], part)
        return part

    for col in range(4):
        part = from_col(col)
        row = 0
        for lane in range(0, lead, 128):
            down_ref[col * piece:(col + 1) * piece, lane:lane + 128] = part[row:row + piece, :]
            row += piece
        for lane in range(0, width, 128):
            msg_ref[col * msg // 4:(col + 1) * msg // 4, lane:lane + 128] = (
                part[row:row + msg // 4, :]
            )
            row += msg // 4
    first = lax.axis_index(ROWS) * msg
    gate = from_col(first // 128)[-8:, :]
    spread = jnp.broadcast_to(gate[0:1, :] + gate[1:2, :], (8, 128))
    gate_ref[...] = pltpu.roll(spread, (128 - first % 128) % 128, 1)[:1, :msg]


def finish(found, share, msg, width, lead):
    vmem = pl.BlockSpec(memory_space=pltpu.VMEM)
    shape = lambda *dims: jax.ShapeDtypeStruct(dims, F32)
    return pl.pallas_call(
        functools.partial(finish_kernel, lead),
        in_specs=[vmem] * 4,
        out_specs=[vmem] * 3,
        out_shape=[shape(share, width), shape(msg, width), shape(1, msg)],
        compiler_params=params(24),
        cost_estimate=cost(1e6, 1e6),
    )(*found)


def relay(rows):
    slots, width = rows.shape
    size = lax.axis_size(ROWS)
    moved = lax.all_to_all(
        rows.reshape(size, slots // size, width), ROWS, split_axis=0, concat_axis=0, tiled=True
    )
    return moved.reshape(slots, width)


def shards(doc_taps, w_down, owner_of, adj_values, adj_index, w_msg, gate_scale, cotangent):
    docs = doc_taps.shape[0]
    depth, width = w_down.shape
    wide = width // 2
    lead = width // 4
    row_size, cols = lax.axis_size(ROWS), lax.axis_size("col")
    my_row, my_col = lax.axis_index(ROWS), lax.axis_index("col")
    slots = row_size * SLOTS
    chips = row_size // 2
    values = adj_values[0]
    blocks = docs // 128
    index = (adj_index[0] // blocks - my_col) % cols * blocks + adj_index[0] % blocks
    gate = gate_scale.reshape(1, width)
    swap = lambda array: lax.ppermute(array, "core", [(0, 1), (1, 0)])

    taps = taps_by_tile(doc_taps)
    packed0, slot = pool_and_pack(owner_of, taps, w_down, wide, slots)
    incoming0 = relay(packed0)
    packed1, mine, theirs = pool_and_turn(slot, taps, w_down, width - wide, slots, chips)
    other = swap(theirs)
    incoming1 = relay(packed1)

    owners = owner_of[0]
    counts = jnp.sum((owners.reshape(row_size, docs) == my_row).astype(jnp.int32), axis=1)
    lower = jnp.arange(row_size)[None, :] < jnp.arange(row_size)[:, None]
    starts = jnp.sum(jnp.where(lower, counts[None, :], 0), axis=1)
    in_slot = jnp.arange(SLOTS, dtype=jnp.int32)[None, :]
    position = jnp.where(in_slot < counts[:, None], starts[:, None] + in_slot, -1).reshape(slots)
    pos_row, pos_col = position.reshape(1, slots), position.reshape(slots, 1)

    owned0 = take(pos_row, incoming0, docs, halves=True)
    parts0 = gather_ring(*owned0)
    owned1 = take(pos_row, incoming1, docs, halves=True, after=parts0[4:6])
    first = product(index, values, parts0, docs)
    side_out, aggregate, message_grad, low, high, next_low, next_high, gate_part = layer(
        index, values, gather_ring(*owned1), first, owned0, cotangent, w_msg, gate, lead
    )

    slot_col = slot.reshape(docs, 1)
    next_parts = gather_ring(next_low, next_high)
    packed_back0 = back(index, values, gather_ring(low, high), cotangent, 0, pos_col, slots,
                        after=(next_parts[2], next_parts[7]))
    returned0 = relay(packed_back0)
    packed_back1 = back(index, values, next_parts, cotangent, lead, pos_col, slots)
    returned1 = relay(packed_back1)

    small, other_small = small_sums(aggregate, message_grad, gate_part, chips, packed_back0)
    other_small = swap(other_small)
    grad0 = take(slot_col, returned0, docs)
    pieces = down_by_col(mine, other, grad0, swap(grad0), small, other_small, cols)
    led = lead_sum([pieces[0]] + [shift(pieces[k], k) for k in range(1, cols)])
    grad1 = take(slot_col, returned1, docs, after=(led,))
    down = down_by_chip(mine, other, grad1, swap(grad1), led)
    down = lax.all_to_all(down, ("z", "x"), split_axis=0, concat_axis=0, tiled=True)
    own = fold(down)
    found = [own] + [
        lax.ppermute(own, "col", [(c, c ^ step) for c in range(4)]) for step in (1, 2, 3)
    ]
    grad_down, grad_msg, grad_gate = finish(
        found, depth // row_size, width // row_size, width, lead
    )
    return side_out, grad_down, grad_msg, grad_gate.reshape(width // row_size)


def solution(mesh):
    rows, cols = mesh.devices.shape
    z = 4
    x = rows // (2 * z)
    split = Mesh(mesh.devices.reshape(z, x, 2, cols), ("z", "x", "core", "col"))
    each = ROWS + ("col",)
    placed = (
        P(each, None, None),
        P(),
        P("col", None),
        P(each, None, None, None),
        P(each, None),
        P(),
        P(),
        P(each, None),
    )
    return jax.shard_map(
        shards,
        mesh=split,
        in_specs=placed,
        out_specs=(P(each, None), P(ROWS, None), P(ROWS, None), P(ROWS)),
        check_vma=False,
    )
```

```python
import functools

import jax
import jax.numpy as jnp
import numpy as np
from jax import lax
from jax.experimental import pallas as pl
from jax.experimental.pallas import tpu as pltpu
from jax.sharding import Mesh
from jax.sharding import PartitionSpec as P

ROWS = ("z", "x", "core")
BF16 = jnp.bfloat16
F32 = jnp.float32
SLOTS = 72


def iota(shape, dim):
    return lax.broadcasted_iota(jnp.int32, shape, dim)


def one_hot(mask):
    return jnp.where(mask, 1.0, 0.0).astype(BF16)


def params(mib=60):
    return pltpu.CompilerParams(vmem_limit_bytes=mib * 1024 * 1024)


def cost(flops, moved, special=0):
    return pl.CostEstimate(flops=int(flops), bytes_accessed=int(moved), transcendentals=int(special))


def whole(*shape):
    return pl.BlockSpec(shape, lambda i: (0,) * len(shape))


def bf16(*shape):
    return jax.ShapeDtypeStruct(shape, BF16)


def pool_tiles(pick, x_ref, pooled_ref, together):
    tiles = x_ref.shape[1] // 16
    for group in range(0, x_ref.shape[0] // 16, together):
        block = jnp.concatenate(
            [
                x_ref[(group + g) * 16:(group + g + 1) * 16, t * 16:(t + 1) * 16, :].reshape(256, 128)
                for g in range(together)
                for t in range(tiles)
            ],
            axis=1,
        )
        mean = jnp.dot(pick[...], block, preferred_element_type=F32).astype(BF16)
        for g in range(together):
            docs = slice((group + g) * 16, (group + g + 1) * 16)
            for j in range(8):
                for t in range(tiles):
                    at, lane = (t * 8 + j) * 128, (g * tiles + t) * 128
                    pooled_ref[docs, at:at + 128] = mean[j * 16:(j + 1) * 16, lane:lane + 128]


def pool_tiles_mixed(pick, wide_rows, x_ref, pooled_ref):
    rows = x_ref.shape[1]
    for group in range(0, x_ref.shape[0] // 16, 2):
        pool_tiles(pick, x_ref.at[group * 16:(group + 1) * 16], pooled_ref.at[group * 16:(group + 1) * 16], 1)
        docs = slice((group + 1) * 16, (group + 2) * 16)
        wide_rows[...] = x_ref[docs].reshape(16 * rows, 128).astype(F32)
        for tile in range(rows // 2):
            first = wide_rows[pl.ds(2 * tile, 16, stride=rows), :]
            second = wide_rows[pl.ds(2 * tile + 1, 16, stride=rows), :]
            pooled_ref[docs, tile * 128:(tile + 1) * 128] = ((first + second) * 0.5).astype(BF16)


def project_block(x_ref, w_hbm, first, pick, pooled, side, w_ref, w_sem, wide_rows=None):
    at = pl.program_id(0)
    step = x_ref.shape[0]
    load = pltpu.make_async_copy(w_hbm.at[:, pl.ds(first, w_ref.shape[1])], w_ref, w_sem)

    @pl.when(at == 0)
    def _():
        load.start()
        out_row, in_row = iota((128, 256), 0), iota((128, 256), 1)
        same_doc = out_row % 16 == in_row // 16
        same_tile = out_row // 16 == (in_row % 16) // 2
        pick[...] = jnp.where(same_doc & same_tile, 0.5, 0.0).astype(BF16)

    if wide_rows is None:
        pool_tiles(pick, x_ref, pooled, 4)
    else:
        pool_tiles_mixed(pick, wide_rows, x_ref, pooled)

    @pl.when(at == 0)
    def _():
        load.wait()

    side[pl.ds(pl.multiple_of(at * step, step), step), :] = jnp.dot(
        pooled[...], w_ref[...], preferred_element_type=F32
    ).astype(BF16)


def pool_kernel(owner_ref, x_ref, w_hbm, out_ref, slot_ref,
                pick, pooled, side, w_ref, w_sem, chosen):
    at = pl.program_id(0)
    docs = side.shape[0]
    share = out_ref.shape[0] // 6

    @pl.when(at == 0)
    def _():
        first = pl.multiple_of(lax.axis_index(ROWS) * docs, 128)
        dest = owner_ref[:, pl.ds(first, docs)]
        hit = iota((32, docs), 0) == dest
        earlier = one_hot(iota((docs, docs), 0) < iota((docs, docs), 1))
        before = jnp.dot(one_hot(hit), earlier, preferred_element_type=F32)
        rank = jnp.sum(jnp.where(hit, before, 0.0), axis=0, keepdims=True)
        slot_ref[...] = dest * SLOTS + rank.astype(jnp.int32)

    project_block(x_ref, w_hbm, 0, pick, pooled, side, w_ref, w_sem)
    rows = iota((share, docs), 0) + at * share
    chosen[pl.ds(pl.multiple_of(at * share, 16), share), :] = one_hot(rows == slot_ref[...])

    @pl.when(at == pl.num_programs(0) - 1)
    def _():
        for part in range(6):
            rows = slice(part * share, (part + 1) * share)
            out_ref[rows, :] = jnp.dot(
                chosen[rows, :], side[...], preferred_element_type=F32
            ).astype(BF16)


def turn_kernel(slot_ref, x_ref, w_hbm, out_ref, mine_ref, theirs_ref,
                pick, pooled, side, w_ref, w_sem, wide_rows):
    first = w_hbm.shape[1] - w_ref.shape[1]
    project_block(x_ref, w_hbm, first, pick, pooled, side, w_ref, w_sem, wide_rows)
    rows = mine_ref.shape[1]
    core = lax.axis_index("core")
    for pair in range(mine_ref.shape[0] // 2):
        turned = pooled[:, pair * 4 * rows:(pair + 1) * 4 * rows].T
        for this in range(2):
            @pl.when(core == this)
            def _():
                for turned_ref, which in ((mine_ref, this), (theirs_ref, 1 - this)):
                    for chip in range(2):
                        at = (chip * 2 + which) * rows
                        turned_ref[pair * 2 + chip] = turned[at:at + rows, :]

    @pl.when(pl.program_id(0) == pl.num_programs(0) - 1)
    def _():
        step = out_ref.shape[0] // 6
        for part in range(6):
            rows = iota((step, side.shape[0]), 0) + part * step
            out_ref[part * step:(part + 1) * step, :] = jnp.dot(
                one_hot(rows == slot_ref[...]), side[...], preferred_element_type=F32
            ).astype(BF16)


def taps_by_tile(doc_taps):
    docs, tokens, depth = doc_taps.shape
    tiles = depth // 128
    taps = doc_taps.reshape(docs, tokens, tiles, 128).transpose(0, 2, 1, 3)
    return taps.reshape(docs, tokens * tiles, 128)


def pool_scratch(step, docs, depth, wide):
    return [
        pltpu.VMEM((128, 256), BF16),
        pltpu.VMEM((step, depth), BF16),
        pltpu.VMEM((docs, wide), BF16),
        pltpu.VMEM((depth, wide), BF16),
        pltpu.SemaphoreType.DMA,
    ]


def pool_and_pack(owner_of, taps, w_down, wide, slots):
    docs, rows, _ = taps.shape
    step = docs // 6
    return pl.pallas_call(
        pool_kernel,
        grid=(6,),
        in_specs=[
            whole(*owner_of.shape),
            pl.BlockSpec((step, rows, 128), lambda i: (i, 0, 0)),
            pl.BlockSpec(memory_space=pl.ANY),
        ],
        out_specs=[whole(slots, wide), whole(1, docs)],
        out_shape=[bf16(slots, wide), jax.ShapeDtypeStruct((1, docs), jnp.int32)],
        scratch_shapes=pool_scratch(step, docs, w_down.shape[0], wide)
        + [pltpu.VMEM((slots, docs), BF16)],
        compiler_params=params(),
        cost_estimate=cost(6e9, 20e6),
    )(owner_of, taps, w_down)


def pool_and_turn(slot, taps, w_down, wide, slots, chips):
    docs, rows, _ = taps.shape
    depth = w_down.shape[0]
    step = docs // 6
    turned = pl.BlockSpec((chips, depth // (2 * chips), step), lambda i: (0, 0, i))
    shape = bf16(chips, depth // (2 * chips), docs)
    return pl.pallas_call(
        turn_kernel,
        grid=(6,),
        in_specs=[
            whole(1, docs),
            pl.BlockSpec((step, rows, 128), lambda i: (i, 0, 0)),
            pl.BlockSpec(memory_space=pl.ANY),
        ],
        out_specs=[whole(slots, wide), turned, turned],
        out_shape=[bf16(slots, wide), shape, shape],
        scratch_shapes=pool_scratch(step, docs, depth, wide)
        + [pltpu.VMEM((16 * rows, 128), F32)],
        compiler_params=params(),
        cost_estimate=cost(6e9, 28e6),
    )(slot, taps, w_down)


def take_kernel(waited, place_ref, table_ref, *out_refs):
    at = pl.program_id(0)
    out_refs = out_refs[waited:]
    depth = table_ref.shape[0]
    step = out_refs[0].shape[0]
    if place_ref.shape[0] == 1:
        mask = iota((step, depth), 0) + at * step == place_ref[...]
    else:
        mask = iota((step, depth), 1) == place_ref[...]
    rows = jnp.dot(one_hot(mask), table_ref[...], preferred_element_type=F32).astype(BF16)
    if len(out_refs) == 1:
        out_refs[0][...] = rows
    else:
        for i, out_ref in enumerate(out_refs):
            @pl.when(at == i)
            def _():
                out_ref[...] = rows


def take(place, table, count, halves=False, after=()):
    depth, width = table.shape
    step = count // 2
    if place.shape[0] == 1:
        place_spec = whole(1, depth)
    else:
        place_spec = pl.BlockSpec((step, 1), lambda i: (i, 0))
    if halves:
        out_specs, out_shape = [whole(step, width)] * 2, [bf16(step, width)] * 2
    else:
        out_specs, out_shape = pl.BlockSpec((step, width), lambda i: (i, 0)), bf16(count, width)
    return pl.pallas_call(
        functools.partial(take_kernel, len(after)),
        grid=(2,),
        in_specs=[place_spec, whole(depth, width)]
        + [pl.BlockSpec(memory_space=pl.ANY) for _ in after],
        out_specs=out_specs,
        out_shape=out_shape,
        compiler_params=params(24),
        cost_estimate=cost(2 * count * depth * width, 2e6),
    )(place, table, *after)


def shift(part, by):
    return lax.ppermute(part, "col", [(c, (c + by) % 4) for c in range(4)])


def gather_ring(low, high):
    before_low, after_high = shift(low, 1), shift(high, 3)
    before_high, after_low = shift(high, 1), shift(low, 3)
    far_low, far_high = shift(before_low, 1), shift(after_high, 3)
    return low, high, after_low, after_high, far_low, far_high, before_low, before_high


def stage(parts, table):
    at = 0
    for part in parts:
        table[at:at + part.shape[0], :] = part[...]
        at += part.shape[0]


def block_row(index_ref, values_ref, table, row, per_row):
    entries = [row * per_row + k for k in range(per_row)]
    at = [pl.multiple_of(index_ref[entry] * 128, 128) for entry in entries]
    blocks = jnp.concatenate([values_ref[entry] for entry in entries], axis=1)
    picked = jnp.concatenate([table[pl.ds(first, 128), :] for first in at], axis=0)
    return jnp.dot(blocks, picked, preferred_element_type=F32)


def product_kernel(index_ref, values_ref, *refs):
    parts, (out_ref, table) = refs[:-2], refs[-2:]
    stage(parts, table)
    rows = out_ref.shape[0] // 128
    per_row = values_ref.shape[0] // rows
    for row in range(rows):
        out_ref[row * 128:(row + 1) * 128, :] = block_row(
            index_ref, values_ref, table, row, per_row
        ).astype(BF16)


def product(index, values, parts, nodes):
    width = parts[0].shape[1]
    vmem = pl.BlockSpec(memory_space=pltpu.VMEM)
    return pl.pallas_call(
        product_kernel,
        in_specs=[pl.BlockSpec(memory_space=pltpu.SMEM), vmem] + [vmem] * len(parts),
        out_specs=vmem,
        out_shape=bf16(nodes, width),
        scratch_shapes=[pltpu.VMEM((4 * nodes, width), BF16)],
        compiler_params=params(),
        cost_estimate=cost(2e8, 3e6),
    )(index, values, *parts)


def layer_kernel(index_ref, values_ref, *refs):
    parts = refs[:8]
    (first_ref, low_in_ref, high_in_ref, cot_ref, w_ref, wt_ref, gate_ref) = refs[8:15]
    (side_out_ref, agg_ref, mgrad_ref, low_ref, high_ref, gpart_ref, table) = refs[15:]
    at = pl.program_id(0)

    @pl.when(at == 0)
    def _():
        stage(parts, table)

    step = cot_ref.shape[0]
    wide = first_ref.shape[1]
    nodes = step * pl.num_programs(0)
    per_row = values_ref.shape[0] * 128 // nodes
    rows = step // 128
    agg_ref[:, :wide] = first_ref[...]
    for row in range(rows):
        agg_ref[row * 128:(row + 1) * 128, wide:] = block_row(
            index_ref, values_ref, table, at * rows + row, per_row
        ).astype(BF16)
    gate = gate_ref[...]
    part = None
    for third in range(rows):
        here = slice(third * 128, (third + 1) * 128)
        message = jnp.dot(agg_ref[here, :], w_ref[...], preferred_element_type=F32)
        squash = jax.nn.sigmoid(message)
        activated = message * squash
        upstream = cot_ref[here, :].astype(F32)
        at_row = pl.multiple_of(at * step + third * 128, 128)
        lead_in = jnp.where(at == 0, low_in_ref[here, :], high_in_ref[here, :])
        owned = jnp.concatenate([lead_in, table[pl.ds(at_row, 128), :]], axis=1)
        side_out_ref[here, :] = (owned.astype(F32) + gate * activated).astype(BF16)
        mgrad_ref[here, :] = (
            upstream * gate * squash * (1.0 + message * (1.0 - squash))
        ).astype(BF16)
        term = jnp.sum(upstream * activated, axis=0, keepdims=True)
        part = term if part is None else part + term
    agrad = jnp.dot(mgrad_ref[...], wt_ref[...], preferred_element_type=F32).astype(BF16)

    @pl.when(at == 0)
    def _():
        low_ref[...] = agrad
        gpart_ref[...] = part

    @pl.when(at == 1)
    def _():
        high_ref[...] = agrad
        gpart_ref[...] += part


def layer(index, values, parts, first, owned, cotangent, w_msg, gate):
    nodes, width = cotangent.shape
    wide = first.shape[1]
    step = nodes // 2
    rows = lambda size: pl.BlockSpec((step, size), lambda i: (i, 0))
    return pl.pallas_call(
        layer_kernel,
        grid=(2,),
        in_specs=[pl.BlockSpec(memory_space=pltpu.SMEM), whole(*values.shape)]
        + [whole(*part.shape) for part in parts]
        + [rows(wide), whole(step, wide), whole(step, wide), rows(width), whole(width, width), whole(width, width),
           whole(1, width)],
        out_specs=[rows(width), rows(width), rows(width), whole(step, width), whole(step, width),
                   whole(1, width)],
        out_shape=[bf16(nodes, width), bf16(nodes, width), bf16(nodes, width), bf16(step, width),
                   bf16(step, width),
                   jax.ShapeDtypeStruct((1, width), F32)],
        scratch_shapes=[pltpu.VMEM((4 * nodes, width - wide), BF16)],
        compiler_params=params(),
        cost_estimate=cost(12e8, 8e6, nodes * width),
    )(index, values, *parts, first, *owned, cotangent, w_msg, w_msg.T, gate)


def back_kernel(index_ref, values_ref, *refs):
    parts, (cot_ref, place_ref), (out_ref, table, grad) = refs[:8], refs[8:10], refs[-3:]
    nodes = cot_ref.shape[0]
    per_row = values_ref.shape[0] * 128 // nodes

    @pl.when(pl.program_id(0) == 0)
    def _():
        stage(parts, table)
        for row in range(nodes // 128):
            at = slice(row * 128, (row + 1) * 128)
            total = block_row(index_ref, values_ref, table, row, per_row)
            upstream = cot_ref[at, :].astype(F32)
            grad[at, :] = (upstream + total).astype(BF16)

    mask = iota((out_ref.shape[0], nodes), 1) == place_ref[...]
    out_ref[...] = jnp.dot(one_hot(mask), grad[...], preferred_element_type=F32).astype(BF16)


def back(index, values, parts, cotangent, place, slots):
    nodes = cotangent.shape[0]
    wide = parts[0].shape[1]
    step = slots // 4
    return pl.pallas_call(
        back_kernel,
        grid=(4,),
        in_specs=[pl.BlockSpec(memory_space=pltpu.SMEM), whole(*values.shape)]
        + [whole(*part.shape) for part in parts]
        + [whole(*cotangent.shape), pl.BlockSpec((step, 1), lambda i: (i, 0))],
        out_specs=pl.BlockSpec((step, wide), lambda i: (i, 0)),
        out_shape=bf16(slots, wide),
        scratch_shapes=[pltpu.VMEM((4 * nodes, wide), BF16), pltpu.VMEM((nodes, wide), BF16)],
        compiler_params=params(),
        cost_estimate=cost(2 * slots * nodes * wide, 5e6),
    )(index, values, *parts, cotangent, place)


def small_kernel(agg_ref, mgrad_ref, gate_ref, after_ref, mine_ref, theirs_ref):
    msg = lax.dot_general(
        agg_ref[...], mgrad_ref[...], (((0,), (0,)), ((), ())), preferred_element_type=F32
    )
    chips, rows, width = mine_ref.shape
    share = width // (2 * chips)
    tail = jnp.concatenate([gate_ref[...], jnp.zeros((rows - share - 1, width), F32)], axis=0)
    core = lax.axis_index("core")
    for this in range(2):
        @pl.when(core == this)
        def _():
            for out_ref, which in ((mine_ref, this), (theirs_ref, 1 - this)):
                for chip in range(chips):
                    at = (chip * 2 + which) * share
                    out_ref[chip, :share, :] = msg[at:at + share, :]
                    out_ref[chip, share:, :] = tail


def small_sums(aggregate, message_grad, gate_part, chips, after):
    width = aggregate.shape[1]
    vmem = pl.BlockSpec(memory_space=pltpu.VMEM)
    out = jax.ShapeDtypeStruct((chips, 24, width), F32)
    return pl.pallas_call(
        small_kernel,
        in_specs=[vmem] * 3 + [pl.BlockSpec(memory_space=pl.ANY)],
        out_specs=[vmem] * 2,
        out_shape=[out, out],
        compiler_params=params(),
        cost_estimate=cost(4e8, 4e6),
    )(aggregate, message_grad, gate_part, after)


def down_rows(mine_ref, other_ref, grad_ref, other_grad_ref):
    docs = mine_ref.shape[2]
    rows = mine_ref.shape[0] * mine_ref.shape[1]
    left = jnp.concatenate(
        [mine_ref[...].reshape(rows, docs), other_ref[...].reshape(rows, docs)], axis=1
    )
    right = jnp.concatenate([grad_ref[...], other_grad_ref[...]], axis=0)
    return jnp.dot(left, right, preferred_element_type=F32)


def tiles_of(array):
    return [array[:, at:at + 128] for at in range(0, array.shape[1], 128)]


def two_terms(row):
    high = row.astype(BF16).astype(F32)
    return [high, row - high, jnp.zeros((14, 128), F32)]


def small_by_col_kernel(small_ref, other_small_ref, *out_refs):
    small = small_ref[...] + other_small_ref[...]
    chips = small.shape[0]
    msg = (small.shape[1] - 8) // 4
    blocks = []
    for chip in range(chips):
        for col in range(4):
            gate = small[chip, 4 * msg:4 * msg + 1, col * 128:(col + 1) * 128]
            cells = tiles_of(small[chip, col * msg:(col + 1) * msg, :]) + two_terms(gate)
            blocks.append(jnp.concatenate(cells, axis=0).astype(BF16))
    my_col = lax.axis_index("col")
    for first in range(4):
        @pl.when(my_col == first)
        def _():
            for k, out_ref in enumerate(out_refs):
                for chip in range(chips):
                    out_ref[chip] = blocks[chip * 4 + (first + k) % 4]


def small_by_col(small, other_small, cols):
    vmem = pl.BlockSpec(memory_space=pltpu.VMEM)
    return pl.pallas_call(
        small_by_col_kernel,
        in_specs=[vmem] * 2,
        out_specs=[vmem] * cols,
        out_shape=[bf16(small.shape[0], 32, 128)] * cols,
        compiler_params=params(),
        cost_estimate=cost(1e6, 2e6),
    )(small, other_small)


def lead_kernel(*refs):
    total = sum([ref[...].astype(F32) for ref in refs[1:4]], refs[0][...].astype(F32))
    out_ref = refs[4]
    at = total.shape[1] - 16
    for chip in range(total.shape[0]):
        gate = total[chip, at:at + 1, :] + total[chip, at + 1:at + 2, :]
        cells = [total[chip, :at, :]] + two_terms(gate)
        out_ref[chip] = jnp.concatenate(cells, axis=0).astype(BF16)


def lead_sum(pieces):
    vmem = pl.BlockSpec(memory_space=pltpu.VMEM)
    return pl.pallas_call(
        lead_kernel,
        in_specs=[vmem] * 4,
        out_specs=vmem,
        out_shape=bf16(*pieces[0].shape),
        compiler_params=params(24),
        cost_estimate=cost(1e6, 1e6),
    )(*pieces)


def down_by_chip_kernel(mine_ref, other_ref, grad_ref, other_grad_ref, led_ref, out_ref):
    total = down_rows(mine_ref, other_ref, grad_ref, other_grad_ref)
    chips, share, _ = mine_ref.shape
    led = out_ref.shape[1] - led_ref.shape[1]
    for chip in range(chips):
        cells = tiles_of(total[chip * share:(chip + 1) * share, :])
        out_ref[chip, :led, :] = jnp.concatenate(cells, axis=0).astype(BF16)
        out_ref[chip, led:, :] = led_ref[chip]


def down_specs(mine, grad):
    chips, share, docs = mine.shape
    rows = pl.BlockSpec((chips // 4, share, docs), lambda i: (i, 0, 0))
    return [rows, rows, whole(*grad.shape), whole(*grad.shape)]


def down_by_chip(mine, other, grad, other_grad, led):
    chips, share, docs = mine.shape
    rows = share * grad.shape[1] // 128 + led.shape[1]
    by_chip = lambda size: pl.BlockSpec((chips // 4, size, 128), lambda i: (i, 0, 0))
    return pl.pallas_call(
        down_by_chip_kernel,
        grid=(4,),
        in_specs=down_specs(mine, grad) + [by_chip(led.shape[1])],
        out_specs=by_chip(rows),
        out_shape=bf16(chips, rows, 128),
        compiler_params=params(),
        cost_estimate=cost(2e9, 12e6),
    )(mine, other, grad, other_grad, led)


def fold_kernel(parts_ref, out_ref):
    total = jnp.sum(parts_ref[...].astype(F32), axis=0)
    at = total.shape[0] - 16
    gate = total[at:at + 1, :] + total[at + 1:at + 2, :]
    out_ref[...] = jnp.concatenate([total[:at, :]] + two_terms(gate), axis=0).astype(BF16)


def fold(parts):
    chips, rows, width = parts.shape
    vmem = pl.BlockSpec(memory_space=pltpu.VMEM)
    return pl.pallas_call(
        fold_kernel,
        in_specs=[vmem],
        out_specs=vmem,
        out_shape=bf16(rows, width),
        compiler_params=params(24),
        cost_estimate=cost(1e6, 2e6),
    )(parts)


def finish_kernel(*refs):
    found, (down_ref, msg_ref, gate_ref) = refs[:4], refs[4:]
    share, width = down_ref.shape
    msg = msg_ref.shape[0]
    my_col = lax.axis_index("col")
    own, near, far, cross = (ref[...].astype(F32) for ref in found)
    total = (own + near) + (far + cross)
    at = 0
    for lane in range(0, width, 128):
        down_ref[:, lane:lane + 128] = total[at:at + share, :]
        at += share

    def from_col(col):
        step = my_col ^ col
        part = own[at:, :]
        for i, other in enumerate((near, far, cross)):
            part = jnp.where(step == i + 1, other[at:, :], part)
        return part

    for col in range(4):
        part = from_col(col)
        row = 0
        for lane in range(0, width, 128):
            msg_ref[col * msg // 4:(col + 1) * msg // 4, lane:lane + 128] = (
                part[row:row + msg // 4, :]
            )
            row += msg // 4
    first = lax.axis_index(ROWS) * msg
    gate = from_col(first // 128)[-16:, :]
    spread = jnp.broadcast_to(gate[0:1, :] + gate[1:2, :], (8, 128))
    gate_ref[...] = pltpu.roll(spread, (128 - first % 128) % 128, 1)[:1, :msg]


def finish(found, share, msg, width):
    vmem = pl.BlockSpec(memory_space=pltpu.VMEM)
    shape = lambda *dims: jax.ShapeDtypeStruct(dims, F32)
    return pl.pallas_call(
        finish_kernel,
        in_specs=[vmem] * 4,
        out_specs=[vmem] * 3,
        out_shape=[shape(share, width), shape(msg, width), shape(1, msg)],
        compiler_params=params(24),
        cost_estimate=cost(1e6, 1e6),
    )(*found)


def relay(rows):
    slots, width = rows.shape
    size = lax.axis_size(ROWS)
    moved = lax.all_to_all(
        rows.reshape(size, slots // size, width), ROWS, split_axis=0, concat_axis=0, tiled=True
    )
    return moved.reshape(slots, width)


def shards(doc_taps, w_down, owner_of, adj_values, adj_index, w_msg, gate_scale, cotangent):
    docs = doc_taps.shape[0]
    depth, width = w_down.shape
    wide = width // 2
    row_size, cols = lax.axis_size(ROWS), lax.axis_size("col")
    my_row, my_col = lax.axis_index(ROWS), lax.axis_index("col")
    slots = row_size * SLOTS
    chips = row_size // 2
    values = adj_values[0]
    blocks = docs // 128
    index = (adj_index[0] // blocks - my_col) % cols * blocks + adj_index[0] % blocks
    gate = gate_scale.reshape(1, width)
    swap = lambda array: lax.ppermute(array, "core", [(0, 1), (1, 0)])

    taps = taps_by_tile(doc_taps)
    packed0, slot = pool_and_pack(owner_of, taps, w_down, wide, slots)
    incoming0 = relay(packed0)
    packed1, mine, theirs = pool_and_turn(slot, taps, w_down, width - wide, slots, chips)
    other = swap(theirs)
    incoming1 = relay(packed1)

    owners = owner_of[0]
    counts = jnp.sum((owners.reshape(row_size, docs) == my_row).astype(jnp.int32), axis=1)
    lower = jnp.arange(row_size)[None, :] < jnp.arange(row_size)[:, None]
    starts = jnp.sum(jnp.where(lower, counts[None, :], 0), axis=1)
    in_slot = jnp.arange(SLOTS, dtype=jnp.int32)[None, :]
    position = jnp.where(in_slot < counts[:, None], starts[:, None] + in_slot, -1).reshape(slots)
    pos_row, pos_col = position.reshape(1, slots), position.reshape(slots, 1)

    owned0 = take(pos_row, incoming0, docs, halves=True)
    parts0 = gather_ring(*owned0)
    owned1 = take(pos_row, incoming1, docs, halves=True, after=parts0[4:6])
    first = product(index, values, parts0, docs)
    side_out, aggregate, message_grad, low, high, gate_part = layer(
        index, values, gather_ring(*owned1), first, owned0, cotangent, w_msg, gate
    )

    packed_back = back(index, values, gather_ring(low, high), cotangent, pos_col, slots)
    returned = relay(packed_back)

    small, other_small = small_sums(aggregate, message_grad, gate_part, chips, packed_back)
    pieces = small_by_col(small, swap(other_small), cols)
    led = lead_sum([pieces[0]] + [shift(pieces[k], k) for k in range(1, cols)])
    grad = take(slot.reshape(docs, 1), returned, docs, after=(led,))
    down = down_by_chip(mine, other, grad, swap(grad), led)
    down = lax.all_to_all(down, ("z", "x"), split_axis=0, concat_axis=0, tiled=True)
    own = fold(down)
    found = [own] + [
        lax.ppermute(own, "col", [(c, c ^ step) for c in range(4)]) for step in (1, 2, 3)
    ]
    grad_down, grad_msg, grad_gate = finish(found, depth // row_size, width // row_size, width)
    return side_out, grad_down, grad_msg, grad_gate.reshape(width // row_size)


def solution(mesh):
    rows, cols = mesh.devices.shape
    z = 4
    x = rows // (2 * z)
    split = Mesh(mesh.devices.reshape(z, x, 2, cols), ("z", "x", "core", "col"))
    each = ROWS + ("col",)
    placed = (
        P(each, None, None),
        P(),
        P("col", None),
        P(each, None, None, None),
        P(each, None),
        P(),
        P(),
        P(each, None),
    )
    return jax.shard_map(
        shards,
        mesh=split,
        in_specs=placed,
        out_specs=(P(each, None), P(ROWS, None), P(ROWS, None), P(ROWS)),
        check_vma=False,
    )
```

```python
import functools

import jax
import jax.numpy as jnp
import numpy as np
from jax import lax
from jax.experimental import pallas as pl
from jax.experimental.pallas import tpu as pltpu
from jax.sharding import Mesh
from jax.sharding import PartitionSpec as P

ROWS = ("z", "x", "core")
BF16 = jnp.bfloat16
F32 = jnp.float32
SLOTS = 72


def iota(shape, dim):
    return lax.broadcasted_iota(jnp.int32, shape, dim)


def one_hot(mask):
    return jnp.where(mask, 1.0, 0.0).astype(BF16)


def params(mib=60):
    return pltpu.CompilerParams(vmem_limit_bytes=mib * 1024 * 1024)


def cost(flops, moved, special=0):
    return pl.CostEstimate(flops=int(flops), bytes_accessed=int(moved), transcendentals=int(special))


def whole(*shape):
    return pl.BlockSpec(shape, lambda i: (0,) * len(shape))


def bf16(*shape):
    return jax.ShapeDtypeStruct(shape, BF16)


STREAMS = 4


def pool_tiles(pick, x_refs, pooled_ref):
    tiles = x_refs[0].shape[1] // 16
    docs = x_refs[0].shape[0]
    for stream, x_ref in enumerate(x_refs):
        block = jnp.concatenate(
            [
                x_ref[at:at + 16, t * 16:(t + 1) * 16, :].reshape(256, 128)
                for at in range(0, docs, 16)
                for t in range(tiles)
            ],
            axis=1,
        )
        mean = jnp.dot(pick[...], block, preferred_element_type=F32).astype(BF16)
        for group in range(docs // 16):
            first = stream * docs + group * 16
            for j in range(8):
                for t in range(tiles):
                    at, lane = (t * 8 + j) * 128, (group * tiles + t) * 128
                    pooled_ref[first:first + 16, at:at + 128] = (
                        mean[j * 16:(j + 1) * 16, lane:lane + 128]
                    )


def set_pick(pick):
    out_row, in_row = iota((128, 256), 0), iota((128, 256), 1)
    same_doc = out_row % 16 == in_row // 16
    same_tile = out_row // 16 == (in_row % 16) // 2
    pick[...] = jnp.where(same_doc & same_tile, 0.5, 0.0).astype(BF16)


def pool_kernel(owner_ref, *refs):
    x_refs, (w_hbm, out_ref, slot_ref) = refs[:STREAMS], refs[STREAMS:STREAMS + 3]
    pick, pooled, side, w_ref, w_sem, chosen = refs[STREAMS + 3:]
    at = pl.program_id(0)
    steps = pl.num_programs(0)
    docs = side.shape[0]
    step = STREAMS * x_refs[0].shape[0]
    share = out_ref.shape[0] // 6
    load = pltpu.make_async_copy(w_hbm, w_ref, w_sem)

    @pl.when(at == 0)
    def _():
        load.start()
        set_pick(pick)
        first = pl.multiple_of(lax.axis_index(ROWS) * docs, 128)
        dest = owner_ref[:, pl.ds(first, docs)]
        hit = iota((32, docs), 0) == dest
        earlier = one_hot(iota((docs, docs), 0) < iota((docs, docs), 1))
        before = jnp.dot(one_hot(hit), earlier, preferred_element_type=F32)
        rank = jnp.sum(jnp.where(hit, before, 0.0), axis=0, keepdims=True)
        slot_ref[...] = dest * SLOTS + rank.astype(jnp.int32)

    pool_tiles(pick, x_refs, pooled.at[pl.ds(pl.multiple_of(at * step, step), step)])
    rows = iota((share, docs), 0) + at * share
    chosen[pl.ds(pl.multiple_of(at * share, 16), share), :] = one_hot(rows == slot_ref[...])

    @pl.when(at == steps - 1)
    def _():
        load.wait()
        for part in range(2):
            rows = slice(part * docs // 2, (part + 1) * docs // 2)
            side[rows, :] = jnp.dot(
                pooled[rows, :], w_ref[...], preferred_element_type=F32
            ).astype(BF16)
        for part in range(6):
            rows = slice(part * share, (part + 1) * share)
            out_ref[rows, :] = jnp.dot(
                chosen[rows, :], side[...], preferred_element_type=F32
            ).astype(BF16)


def turn_kernel(*refs):
    x_refs, (mine_ref, theirs_ref, done_ref, pick, pooled) = refs[:STREAMS], refs[STREAMS + 1:]

    @pl.when(pl.program_id(0) == 0)
    def _():
        set_pick(pick)
        done_ref[...] = jnp.zeros_like(done_ref)

    pool_tiles(pick, x_refs, pooled)
    rows = mine_ref.shape[1]
    core = lax.axis_index("core")
    for pair in range(mine_ref.shape[0] // 2):
        turned = pooled[:, pair * 4 * rows:(pair + 1) * 4 * rows].T
        for this in range(2):
            @pl.when(core == this)
            def _():
                for turned_ref, which in ((mine_ref, this), (theirs_ref, 1 - this)):
                    for chip in range(2):
                        at = (chip * 2 + which) * rows
                        turned_ref[pair * 2 + chip] = turned[at:at + rows, :]


def taps_by_tile(doc_taps):
    docs, tokens, depth = doc_taps.shape
    tiles = depth // 128
    taps = doc_taps.reshape(docs, tokens, tiles, 128).transpose(0, 2, 1, 3)
    return taps.reshape(docs, tokens * tiles, 128)


def streams(step, rows):
    def spec(stream):
        return pl.BlockSpec((step // STREAMS, rows, 128), lambda i: (i * STREAMS + stream, 0, 0))

    return [spec(stream) for stream in range(STREAMS)]


def pool_and_pack(owner_of, taps, w_down, slots):
    docs, rows, _ = taps.shape
    depth, width = w_down.shape
    return pl.pallas_call(
        pool_kernel,
        grid=(6,),
        in_specs=[
            whole(*owner_of.shape),
            *streams(docs // 6, rows),
            pl.BlockSpec(memory_space=pl.ANY),
        ],
        out_specs=[whole(slots, width), whole(1, docs)],
        out_shape=[bf16(slots, width), jax.ShapeDtypeStruct((1, docs), jnp.int32)],
        scratch_shapes=[
            pltpu.VMEM((128, 256), BF16),
            pltpu.VMEM((docs, depth), BF16),
            pltpu.VMEM((docs, width), BF16),
            pltpu.VMEM((depth, width), BF16),
            pltpu.SemaphoreType.DMA,
            pltpu.VMEM((slots, docs), BF16),
        ],
        compiler_params=params(),
        cost_estimate=cost(8e9, 23e6),
    )(owner_of, *[taps] * STREAMS, w_down)


def pool_and_turn(taps, depth, chips, after):
    docs, rows, _ = taps.shape
    step = docs // 6
    turned = pl.BlockSpec((chips, depth // (2 * chips), step), lambda i: (0, 0, i))
    return pl.pallas_call(
        turn_kernel,
        grid=(6,),
        in_specs=streams(step, rows) + [pl.BlockSpec(memory_space=pl.ANY)],
        out_specs=[turned, turned, whole(8, 128)],
        out_shape=[bf16(chips, depth // (2 * chips), docs)] * 2
        + [jax.ShapeDtypeStruct((8, 128), F32)],
        scratch_shapes=[pltpu.VMEM((128, 256), BF16), pltpu.VMEM((step, depth), BF16)],
        compiler_params=params(),
        cost_estimate=cost(2e9, 24e6),
    )(*[taps] * STREAMS, after)


def take_kernel(waited, place_ref, table_ref, *out_refs):
    at = pl.program_id(0)
    out_refs = out_refs[waited:]
    depth = table_ref.shape[0]
    step = out_refs[0].shape[0]
    if place_ref.shape[0] == 1:
        mask = iota((step, depth), 0) + at * step == place_ref[...]
    else:
        mask = iota((step, depth), 1) == place_ref[...]
    rows = jnp.dot(one_hot(mask), table_ref[...], preferred_element_type=F32).astype(BF16)
    if len(out_refs) == 1:
        out_refs[0][...] = rows
    else:
        for i, out_ref in enumerate(out_refs):
            @pl.when(at == i)
            def _():
                out_ref[...] = rows


def take(place, table, count, halves=False, after=()):
    depth, width = table.shape
    step = count // 2
    if place.shape[0] == 1:
        place_spec = whole(1, depth)
    else:
        place_spec = pl.BlockSpec((step, 1), lambda i: (i, 0))
    if halves:
        out_specs, out_shape = [whole(step, width)] * 2, [bf16(step, width)] * 2
    else:
        out_specs, out_shape = pl.BlockSpec((step, width), lambda i: (i, 0)), bf16(count, width)
    return pl.pallas_call(
        functools.partial(take_kernel, len(after)),
        grid=(2,),
        in_specs=[place_spec, whole(depth, width)]
        + [pl.BlockSpec(memory_space=pl.ANY) for _ in after],
        out_specs=out_specs,
        out_shape=out_shape,
        compiler_params=params(24),
        cost_estimate=cost(2 * count * depth * width, 2e6),
    )(place, table, *after)


def shift(part, by):
    return lax.ppermute(part, "col", [(c, (c + by) % 4) for c in range(4)])


def gather_ring(low, high):
    before_low, after_high = shift(low, 1), shift(high, 3)
    before_high, after_low = shift(high, 1), shift(low, 3)
    far_low, far_high = shift(before_low, 1), shift(after_high, 3)
    return low, high, after_low, after_high, far_low, far_high, before_low, before_high


def stage(parts, table):
    at = 0
    for part in parts:
        table[at:at + part.shape[0], :] = part[...]
        at += part.shape[0]


def block_row(index_ref, values_ref, table, row, per_row):
    entries = [row * per_row + k for k in range(per_row)]
    at = [pl.multiple_of(index_ref[entry] * 128, 128) for entry in entries]
    blocks = jnp.concatenate([values_ref[entry] for entry in entries], axis=1)
    picked = jnp.concatenate([table[pl.ds(first, 128), :] for first in at], axis=0)
    return jnp.dot(blocks, picked, preferred_element_type=F32)


def layer_kernel(index_ref, values_ref, *refs):
    parts = refs[:8]
    (cot_ref, w_ref, gate_ref) = refs[8:11]
    (side_out_ref, agg_ref, mgrad_ref, low_ref, high_ref, gpart_ref, table) = refs[11:]
    at = pl.program_id(0)

    @pl.when(at == 0)
    def _():
        stage(parts, table)

    step = cot_ref.shape[0]
    nodes = step * pl.num_programs(0)
    per_row = values_ref.shape[0] * 128 // nodes
    rows = step // 128
    for row in range(rows):
        agg_ref[row * 128:(row + 1) * 128, :] = block_row(
            index_ref, values_ref, table, at * rows + row, per_row
        ).astype(BF16)
    gate = gate_ref[...]
    part = None
    for third in range(rows):
        here = slice(third * 128, (third + 1) * 128)
        message = jnp.dot(agg_ref[here, :], w_ref[...], preferred_element_type=F32)
        squash = jax.nn.sigmoid(message)
        activated = message * squash
        upstream = cot_ref[here, :].astype(F32)
        at_row = pl.multiple_of(at * step + third * 128, 128)
        owned = table[pl.ds(at_row, 128), :]
        side_out_ref[here, :] = (owned.astype(F32) + gate * activated).astype(BF16)
        mgrad_ref[here, :] = (
            upstream * gate * squash * (1.0 + message * (1.0 - squash))
        ).astype(BF16)
        term = jnp.sum(upstream * activated, axis=0, keepdims=True)
        part = term if part is None else part + term
    agrad = lax.dot_general(
        mgrad_ref[...], w_ref[...], (((1,), (1,)), ((), ())), preferred_element_type=F32
    ).astype(BF16)

    @pl.when(at == 0)
    def _():
        low_ref[...] = agrad
        gpart_ref[...] = part

    @pl.when(at == 1)
    def _():
        high_ref[...] = agrad
        gpart_ref[...] += part


def layer(index, values, parts, cotangent, w_msg, gate):
    nodes, width = cotangent.shape
    step = nodes // 2
    rows = lambda size: pl.BlockSpec((step, size), lambda i: (i, 0))
    return pl.pallas_call(
        layer_kernel,
        grid=(2,),
        in_specs=[pl.BlockSpec(memory_space=pltpu.SMEM), whole(*values.shape)]
        + [whole(*part.shape) for part in parts]
        + [rows(width), whole(width, width), whole(1, width)],
        out_specs=[rows(width), rows(width), rows(width), whole(step, width), whole(step, width),
                   whole(1, width)],
        out_shape=[bf16(nodes, width), bf16(nodes, width), bf16(nodes, width), bf16(step, width),
                   bf16(step, width),
                   jax.ShapeDtypeStruct((1, width), F32)],
        scratch_shapes=[pltpu.VMEM((4 * nodes, width), BF16)],
        compiler_params=params(),
        cost_estimate=cost(12e8, 8e6, nodes * width),
    )(index, values, *parts, cotangent, w_msg, gate)


def back_kernel(index_ref, values_ref, *refs):
    parts, (cot_ref, place_ref), (out_ref, table, grad) = refs[:8], refs[8:10], refs[-3:]
    nodes = cot_ref.shape[0]
    per_row = values_ref.shape[0] * 128 // nodes

    @pl.when(pl.program_id(0) == 0)
    def _():
        stage(parts, table)
        for row in range(nodes // 128):
            at = slice(row * 128, (row + 1) * 128)
            total = block_row(index_ref, values_ref, table, row, per_row)
            upstream = cot_ref[at, :].astype(F32)
            grad[at, :] = (upstream + total).astype(BF16)

    mask = iota((out_ref.shape[0], nodes), 1) == place_ref[...]
    out_ref[...] = jnp.dot(one_hot(mask), grad[...], preferred_element_type=F32).astype(BF16)


def back(index, values, parts, cotangent, place, slots):
    nodes = cotangent.shape[0]
    wide = parts[0].shape[1]
    step = slots // 4
    return pl.pallas_call(
        back_kernel,
        grid=(4,),
        in_specs=[pl.BlockSpec(memory_space=pltpu.SMEM), whole(*values.shape)]
        + [whole(*part.shape) for part in parts]
        + [whole(*cotangent.shape), pl.BlockSpec((step, 1), lambda i: (i, 0))],
        out_specs=pl.BlockSpec((step, wide), lambda i: (i, 0)),
        out_shape=bf16(slots, wide),
        scratch_shapes=[pltpu.VMEM((4 * nodes, wide), BF16), pltpu.VMEM((nodes, wide), BF16)],
        compiler_params=params(),
        cost_estimate=cost(2 * slots * nodes * wide, 5e6),
    )(index, values, *parts, cotangent, place)


def small_kernel(agg_ref, mgrad_ref, gate_ref, after_ref, mine_ref, theirs_ref):
    msg = lax.dot_general(
        agg_ref[...], mgrad_ref[...], (((0,), (0,)), ((), ())), preferred_element_type=F32
    )
    chips, rows, width = mine_ref.shape
    share = width // (2 * chips)
    tail = jnp.concatenate([gate_ref[...], jnp.zeros((rows - share - 1, width), F32)], axis=0)
    core = lax.axis_index("core")
    for this in range(2):
        @pl.when(core == this)
        def _():
            for out_ref, which in ((mine_ref, this), (theirs_ref, 1 - this)):
                for chip in range(chips):
                    at = (chip * 2 + which) * share
                    out_ref[chip, :share, :] = msg[at:at + share, :]
                    out_ref[chip, share:, :] = tail


def small_sums(aggregate, message_grad, gate_part, chips, after):
    width = aggregate.shape[1]
    vmem = pl.BlockSpec(memory_space=pltpu.VMEM)
    out = jax.ShapeDtypeStruct((chips, 24, width), F32)
    return pl.pallas_call(
        small_kernel,
        in_specs=[vmem] * 3 + [pl.BlockSpec(memory_space=pl.ANY)],
        out_specs=[vmem] * 2,
        out_shape=[out, out],
        compiler_params=params(24),
        cost_estimate=cost(4e8, 4e6),
    )(aggregate, message_grad, gate_part, after)


def down_rows(mine_ref, other_ref, grad_ref, other_grad_ref):
    docs = mine_ref.shape[2]
    rows = mine_ref.shape[0] * mine_ref.shape[1]
    left = jnp.concatenate(
        [mine_ref[...].reshape(rows, docs), other_ref[...].reshape(rows, docs)], axis=1
    )
    right = jnp.concatenate([grad_ref[...], other_grad_ref[...]], axis=0)
    return jnp.dot(left, right, preferred_element_type=F32)


def tiles_of(array):
    return [array[:, at:at + 128] for at in range(0, array.shape[1], 128)]


def two_terms(row):
    high = row.astype(BF16).astype(F32)
    return [high, row - high, jnp.zeros((14, 128), F32)]


def small_by_col_kernel(small_ref, other_small_ref, *out_refs):
    small = small_ref[...] + other_small_ref[...]
    chips = small.shape[0]
    msg = (small.shape[1] - 8) // 4
    blocks = []
    for chip in range(chips):
        for col in range(4):
            gate = small[chip, 4 * msg:4 * msg + 1, col * 128:(col + 1) * 128]
            cells = tiles_of(small[chip, col * msg:(col + 1) * msg, :]) + two_terms(gate)
            blocks.append(jnp.concatenate(cells, axis=0).astype(BF16))
    my_col = lax.axis_index("col")
    for first in range(4):
        @pl.when(my_col == first)
        def _():
            for k, out_ref in enumerate(out_refs):
                for chip in range(chips):
                    out_ref[chip] = blocks[chip * 4 + (first + k) % 4]


def small_by_col(small, other_small, cols):
    vmem = pl.BlockSpec(memory_space=pltpu.VMEM)
    return pl.pallas_call(
        small_by_col_kernel,
        in_specs=[vmem] * 2,
        out_specs=[vmem] * cols,
        out_shape=[bf16(small.shape[0], 32, 128)] * cols,
        compiler_params=params(24),
        cost_estimate=cost(1e6, 2e6),
    )(small, other_small)


def lead_kernel(*refs):
    total = sum([ref[...].astype(F32) for ref in refs[1:4]], refs[0][...].astype(F32))
    out_ref = refs[4]
    at = total.shape[1] - 16
    for chip in range(total.shape[0]):
        gate = total[chip, at:at + 1, :] + total[chip, at + 1:at + 2, :]
        cells = [total[chip, :at, :]] + two_terms(gate)
        out_ref[chip] = jnp.concatenate(cells, axis=0).astype(BF16)


def lead_sum(pieces):
    vmem = pl.BlockSpec(memory_space=pltpu.VMEM)
    return pl.pallas_call(
        lead_kernel,
        in_specs=[vmem] * 4,
        out_specs=vmem,
        out_shape=bf16(*pieces[0].shape),
        compiler_params=params(24),
        cost_estimate=cost(1e6, 1e6),
    )(*pieces)


def down_by_chip_kernel(mine_ref, other_ref, grad_ref, other_grad_ref, led_ref, out_ref):
    total = down_rows(mine_ref, other_ref, grad_ref, other_grad_ref)
    chips, share, _ = mine_ref.shape
    led = out_ref.shape[1] - led_ref.shape[1]
    for chip in range(chips):
        cells = tiles_of(total[chip * share:(chip + 1) * share, :])
        out_ref[chip, :led, :] = jnp.concatenate(cells, axis=0).astype(BF16)
        out_ref[chip, led:, :] = led_ref[chip]


def down_specs(mine, grad):
    chips, share, docs = mine.shape
    rows = pl.BlockSpec((chips // 4, share, docs), lambda i: (i, 0, 0))
    return [rows, rows, whole(*grad.shape), whole(*grad.shape)]


def down_by_chip(mine, other, grad, other_grad, led):
    chips, share, docs = mine.shape
    rows = share * grad.shape[1] // 128 + led.shape[1]
    by_chip = lambda size: pl.BlockSpec((chips // 4, size, 128), lambda i: (i, 0, 0))
    return pl.pallas_call(
        down_by_chip_kernel,
        grid=(4,),
        in_specs=down_specs(mine, grad) + [by_chip(led.shape[1])],
        out_specs=by_chip(rows),
        out_shape=bf16(chips, rows, 128),
        compiler_params=params(40),
        cost_estimate=cost(2e9, 12e6),
    )(mine, other, grad, other_grad, led)


def fold_kernel(parts_ref, out_ref):
    total = jnp.sum(parts_ref[...].astype(F32), axis=0)
    at = total.shape[0] - 16
    gate = total[at:at + 1, :] + total[at + 1:at + 2, :]
    out_ref[...] = jnp.concatenate([total[:at, :]] + two_terms(gate), axis=0).astype(BF16)


def fold(parts):
    chips, rows, width = parts.shape
    vmem = pl.BlockSpec(memory_space=pltpu.VMEM)
    return pl.pallas_call(
        fold_kernel,
        in_specs=[vmem],
        out_specs=vmem,
        out_shape=bf16(rows, width),
        compiler_params=params(24),
        cost_estimate=cost(1e6, 2e6),
    )(parts)


def finish_kernel(*refs):
    found, (down_ref, msg_ref, gate_ref) = refs[:4], refs[4:]
    share, width = down_ref.shape
    msg = msg_ref.shape[0]
    my_col = lax.axis_index("col")
    own, near, far, cross = (ref[...].astype(F32) for ref in found)
    total = (own + near) + (far + cross)
    at = 0
    for lane in range(0, width, 128):
        down_ref[:, lane:lane + 128] = total[at:at + share, :]
        at += share

    def from_col(col):
        step = my_col ^ col
        part = own[at:, :]
        for i, other in enumerate((near, far, cross)):
            part = jnp.where(step == i + 1, other[at:, :], part)
        return part

    for col in range(4):
        part = from_col(col)
        row = 0
        for lane in range(0, width, 128):
            msg_ref[col * msg // 4:(col + 1) * msg // 4, lane:lane + 128] = (
                part[row:row + msg // 4, :]
            )
            row += msg // 4
    first = lax.axis_index(ROWS) * msg
    gate = from_col(first // 128)[-16:, :]
    spread = jnp.broadcast_to(gate[0:1, :] + gate[1:2, :], (8, 128))
    gate_ref[...] = pltpu.roll(spread, (128 - first % 128) % 128, 1)[:1, :msg]


def finish(found, share, msg, width):
    vmem = pl.BlockSpec(memory_space=pltpu.VMEM)
    shape = lambda *dims: jax.ShapeDtypeStruct(dims, F32)
    return pl.pallas_call(
        finish_kernel,
        in_specs=[vmem] * 4,
        out_specs=[vmem] * 3,
        out_shape=[shape(share, width), shape(msg, width), shape(1, msg)],
        compiler_params=params(24),
        cost_estimate=cost(1e6, 1e6),
    )(*found)


def relay(rows):
    slots, width = rows.shape
    size = lax.axis_size(ROWS)
    moved = lax.all_to_all(
        rows.reshape(size, slots // size, width), ROWS, split_axis=0, concat_axis=0, tiled=True
    )
    return moved.reshape(slots, width)


def shards(doc_taps, w_down, owner_of, adj_values, adj_index, w_msg, gate_scale, cotangent):
    docs = doc_taps.shape[0]
    depth, width = w_down.shape
    row_size, cols = lax.axis_size(ROWS), lax.axis_size("col")
    my_row, my_col = lax.axis_index(ROWS), lax.axis_index("col")
    slots = row_size * SLOTS
    chips = row_size // 2
    values = adj_values[0]
    blocks = docs // 128
    index = (adj_index[0] // blocks - my_col) % cols * blocks + adj_index[0] % blocks
    gate = gate_scale.reshape(1, width)
    swap = lambda array: lax.ppermute(array, "core", [(0, 1), (1, 0)])

    taps = taps_by_tile(doc_taps)
    packed, slot = pool_and_pack(owner_of, taps, w_down, slots)
    incoming = relay(packed)
    mine, theirs, turned = pool_and_turn(taps, depth, chips, slot)
    other = swap(theirs)

    owners = owner_of[0]
    counts = jnp.sum((owners.reshape(row_size, docs) == my_row).astype(jnp.int32), axis=1)
    lower = jnp.arange(row_size)[None, :] < jnp.arange(row_size)[:, None]
    starts = jnp.sum(jnp.where(lower, counts[None, :], 0), axis=1)
    in_slot = jnp.arange(SLOTS, dtype=jnp.int32)[None, :]
    position = jnp.where(in_slot < counts[:, None], starts[:, None] + in_slot, -1).reshape(slots)
    pos_row, pos_col = position.reshape(1, slots), position.reshape(slots, 1)

    owned = take(pos_row, incoming, docs, halves=True, after=(turned,))
    side_out, aggregate, message_grad, low, high, gate_part = layer(
        index, values, gather_ring(*owned), cotangent, w_msg, gate
    )

    packed_back = back(index, values, gather_ring(low, high), cotangent, pos_col, slots)
    returned = relay(packed_back)

    small, other_small = small_sums(aggregate, message_grad, gate_part, chips, packed_back)
    pieces = small_by_col(small, swap(other_small), cols)
    led = lead_sum([pieces[0]] + [shift(pieces[k], k) for k in range(1, cols)])
    grad = take(slot.reshape(docs, 1), returned, docs, after=(led,))
    down = down_by_chip(mine, other, grad, swap(grad), led)
    down = lax.all_to_all(down, ("z", "x"), split_axis=0, concat_axis=0, tiled=True)
    own = fold(down)
    found = [own] + [
        lax.ppermute(own, "col", [(c, c ^ step) for c in range(4)]) for step in (1, 2, 3)
    ]
    grad_down, grad_msg, grad_gate = finish(found, depth // row_size, width // row_size, width)
    return side_out, grad_down, grad_msg, grad_gate.reshape(width // row_size)


def solution(mesh):
    rows, cols = mesh.devices.shape
    z = 4
    x = rows // (2 * z)
    split = Mesh(mesh.devices.reshape(z, x, 2, cols), ("z", "x", "core", "col"))
    each = ROWS + ("col",)
    placed = (
        P(each, None, None),
        P(),
        P("col", None),
        P(each, None, None, None),
        P(each, None),
        P(),
        P(),
        P(each, None),
    )
    return jax.shard_map(
        shards,
        mesh=split,
        in_specs=placed,
        out_specs=(P(each, None), P(ROWS, None), P(ROWS, None), P(ROWS)),
        check_vma=False,
    )
```

```python
import functools

import jax
import jax.numpy as jnp
import numpy as np
from jax import lax
from jax.experimental import pallas as pl
from jax.experimental.pallas import tpu as pltpu
from jax.sharding import Mesh
from jax.sharding import PartitionSpec as P

ROWS = ("z", "x", "core")
BF16 = jnp.bfloat16
F32 = jnp.float32
SLOTS = 72


def iota(shape, dim):
    return lax.broadcasted_iota(jnp.int32, shape, dim)


def one_hot(mask):
    return jnp.where(mask, 1.0, 0.0).astype(BF16)


def params(mib=60):
    return pltpu.CompilerParams(vmem_limit_bytes=mib * 1024 * 1024)


def cost(flops, moved, special=0):
    return pl.CostEstimate(flops=int(flops), bytes_accessed=int(moved), transcendentals=int(special))


def whole(*shape):
    return pl.BlockSpec(shape, lambda i: (0,) * len(shape))


def bf16(*shape):
    return jax.ShapeDtypeStruct(shape, BF16)


STREAMS = 4


def pool_tiles(pick, x_refs, pooled_ref):
    tiles = x_refs[0].shape[1] // 16
    docs = x_refs[0].shape[0]
    for stream, x_ref in enumerate(x_refs):
        block = jnp.concatenate(
            [
                x_ref[at:at + 16, t * 16:(t + 1) * 16, :].reshape(256, 128)
                for at in range(0, docs, 16)
                for t in range(tiles)
            ],
            axis=1,
        )
        mean = jnp.dot(pick[...], block, preferred_element_type=F32).astype(BF16)
        for group in range(docs // 16):
            first = stream * docs + group * 16
            for j in range(8):
                for t in range(tiles):
                    at, lane = (t * 8 + j) * 128, (group * tiles + t) * 128
                    pooled_ref[first:first + 16, at:at + 128] = (
                        mean[j * 16:(j + 1) * 16, lane:lane + 128]
                    )


def set_pick(pick):
    out_row, in_row = iota((128, 256), 0), iota((128, 256), 1)
    same_doc = out_row % 16 == in_row // 16
    same_tile = out_row // 16 == (in_row % 16) // 2
    pick[...] = jnp.where(same_doc & same_tile, 0.5, 0.0).astype(BF16)


def pool_kernel(owner_ref, *refs):
    x_refs, (w_hbm, out_ref, slot_ref) = refs[:STREAMS], refs[STREAMS:STREAMS + 3]
    pick, pooled, side, w_ref, w_sem, chosen = refs[STREAMS + 3:]
    at = pl.program_id(0)
    steps = pl.num_programs(0)
    docs = side.shape[0]
    step = STREAMS * x_refs[0].shape[0]
    share = out_ref.shape[0] // 6
    load = pltpu.make_async_copy(w_hbm, w_ref, w_sem)

    @pl.when(at == 0)
    def _():
        load.start()
        set_pick(pick)
        first = pl.multiple_of(lax.axis_index(ROWS) * docs, 128)
        dest = owner_ref[:, pl.ds(first, docs)]
        hit = iota((32, docs), 0) == dest
        earlier = one_hot(iota((docs, docs), 0) < iota((docs, docs), 1))
        before = jnp.dot(one_hot(hit), earlier, preferred_element_type=F32)
        rank = jnp.sum(jnp.where(hit, before, 0.0), axis=0, keepdims=True)
        slot_ref[...] = dest * SLOTS + rank.astype(jnp.int32)

    pool_tiles(pick, x_refs, pooled.at[pl.ds(pl.multiple_of(at * step, step), step)])
    rows = iota((share, docs), 0) + at * share
    chosen[pl.ds(pl.multiple_of(at * share, 16), share), :] = one_hot(rows == slot_ref[...])

    @pl.when(at == 1)
    def _():
        load.wait()

    @pl.when(at % 2 == 1)
    def _():
        rows = pl.ds(pl.multiple_of((at - 1) * step, step), 2 * step)
        side[rows, :] = jnp.dot(
            pooled[rows, :], w_ref[...], preferred_element_type=F32
        ).astype(BF16)

    @pl.when(at == steps - 1)
    def _():
        for part in range(6):
            rows = slice(part * share, (part + 1) * share)
            out_ref[rows, :] = jnp.dot(
                chosen[rows, :], side[...], preferred_element_type=F32
            ).astype(BF16)


def turn_kernel(*refs):
    x_refs, (mine_ref, theirs_ref, done_ref, pick, pooled) = refs[:STREAMS], refs[STREAMS + 1:]

    @pl.when(pl.program_id(0) == 0)
    def _():
        set_pick(pick)
        done_ref[...] = jnp.zeros_like(done_ref)

    pool_tiles(pick, x_refs, pooled)
    rows = mine_ref.shape[1]
    core = lax.axis_index("core")
    for pair in range(mine_ref.shape[0] // 2):
        turned = pooled[:, pair * 4 * rows:(pair + 1) * 4 * rows].T
        for this in range(2):
            @pl.when(core == this)
            def _():
                for turned_ref, which in ((mine_ref, this), (theirs_ref, 1 - this)):
                    for chip in range(2):
                        at = (chip * 2 + which) * rows
                        turned_ref[pair * 2 + chip] = turned[at:at + rows, :]


def taps_by_tile(doc_taps):
    docs, tokens, depth = doc_taps.shape
    tiles = depth // 128
    taps = doc_taps.reshape(docs, tokens, tiles, 128).transpose(0, 2, 1, 3)
    return taps.reshape(docs, tokens * tiles, 128)


def streams(step, rows):
    def spec(stream):
        return pl.BlockSpec((step // STREAMS, rows, 128), lambda i: (i * STREAMS + stream, 0, 0))

    return [spec(stream) for stream in range(STREAMS)]


def pool_and_pack(owner_of, taps, w_down, slots):
    docs, rows, _ = taps.shape
    depth, width = w_down.shape
    return pl.pallas_call(
        pool_kernel,
        grid=(6,),
        in_specs=[
            whole(*owner_of.shape),
            *streams(docs // 6, rows),
            pl.BlockSpec(memory_space=pl.ANY),
        ],
        out_specs=[whole(slots, width), whole(1, docs)],
        out_shape=[bf16(slots, width), jax.ShapeDtypeStruct((1, docs), jnp.int32)],
        scratch_shapes=[
            pltpu.VMEM((128, 256), BF16),
            pltpu.VMEM((docs, depth), BF16),
            pltpu.VMEM((docs, width), BF16),
            pltpu.VMEM((depth, width), BF16),
            pltpu.SemaphoreType.DMA,
            pltpu.VMEM((slots, docs), BF16),
        ],
        compiler_params=params(),
        cost_estimate=cost(8e9, 23e6),
    )(owner_of, *[taps] * STREAMS, w_down)


def pool_and_turn(taps, depth, chips, after):
    docs, rows, _ = taps.shape
    step = docs // 6
    turned = pl.BlockSpec((chips, depth // (2 * chips), step), lambda i: (0, 0, i))
    return pl.pallas_call(
        turn_kernel,
        grid=(6,),
        in_specs=streams(step, rows) + [pl.BlockSpec(memory_space=pl.ANY)],
        out_specs=[turned, turned, whole(8, 128)],
        out_shape=[bf16(chips, depth // (2 * chips), docs)] * 2
        + [jax.ShapeDtypeStruct((8, 128), F32)],
        scratch_shapes=[pltpu.VMEM((128, 256), BF16), pltpu.VMEM((step, depth), BF16)],
        compiler_params=params(),
        cost_estimate=cost(2e9, 24e6),
    )(*[taps] * STREAMS, after)


def take_kernel(waited, place_ref, table_ref, *out_refs):
    at = pl.program_id(0)
    out_refs = out_refs[waited:]
    depth = table_ref.shape[0]
    step = out_refs[0].shape[0]
    if place_ref.shape[0] == 1:
        mask = iota((step, depth), 0) + at * step == place_ref[...]
    else:
        mask = iota((step, depth), 1) == place_ref[...]
    rows = jnp.dot(one_hot(mask), table_ref[...], preferred_element_type=F32).astype(BF16)
    if len(out_refs) == 1:
        out_refs[0][...] = rows
    else:
        for i, out_ref in enumerate(out_refs):
            @pl.when(at == i)
            def _():
                out_ref[...] = rows


def take(place, table, count, halves=False, after=()):
    depth, width = table.shape
    step = count // 2
    if place.shape[0] == 1:
        place_spec = whole(1, depth)
    else:
        place_spec = pl.BlockSpec((step, 1), lambda i: (i, 0))
    if halves:
        out_specs, out_shape = [whole(step, width)] * 2, [bf16(step, width)] * 2
    else:
        out_specs, out_shape = pl.BlockSpec((step, width), lambda i: (i, 0)), bf16(count, width)
    return pl.pallas_call(
        functools.partial(take_kernel, len(after)),
        grid=(2,),
        in_specs=[place_spec, whole(depth, width)]
        + [pl.BlockSpec(memory_space=pl.ANY) for _ in after],
        out_specs=out_specs,
        out_shape=out_shape,
        compiler_params=params(24),
        cost_estimate=cost(2 * count * depth * width, 2e6),
    )(place, table, *after)


def shift(part, by):
    return lax.ppermute(part, "col", [(c, (c + by) % 4) for c in range(4)])


def gather_ring(low, high):
    before_low, after_high = shift(low, 1), shift(high, 3)
    before_high, after_low = shift(high, 1), shift(low, 3)
    far_low, far_high = shift(before_low, 1), shift(after_high, 3)
    return low, high, after_low, after_high, far_low, far_high, before_low, before_high


def stage(parts, table):
    at = 0
    for part in parts:
        table[at:at + part.shape[0], :] = part[...]
        at += part.shape[0]


def block_row(index_ref, values_ref, table, row, per_row):
    entries = [row * per_row + k for k in range(per_row)]
    at = [pl.multiple_of(index_ref[entry] * 128, 128) for entry in entries]
    blocks = jnp.concatenate([values_ref[entry] for entry in entries], axis=1)
    picked = jnp.concatenate([table[pl.ds(first, 128), :] for first in at], axis=0)
    return jnp.dot(blocks, picked, preferred_element_type=F32)


def layer_kernel(index_ref, values_ref, *refs):
    parts = refs[:8]
    (cot_ref, w_ref, gate_ref) = refs[8:11]
    (side_out_ref, agg_ref, mgrad_ref, low_ref, high_ref, gpart_ref, table) = refs[11:]
    at = pl.program_id(0)

    @pl.when(at == 0)
    def _():
        stage(parts, table)

    step = cot_ref.shape[0]
    nodes = step * pl.num_programs(0)
    per_row = values_ref.shape[0] * 128 // nodes
    rows = step // 128
    for row in range(rows):
        agg_ref[row * 128:(row + 1) * 128, :] = block_row(
            index_ref, values_ref, table, at * rows + row, per_row
        ).astype(BF16)
    gate = gate_ref[...]
    part = None
    for third in range(rows):
        here = slice(third * 128, (third + 1) * 128)
        message = jnp.dot(agg_ref[here, :], w_ref[...], preferred_element_type=F32)
        squash = jax.nn.sigmoid(message)
        activated = message * squash
        upstream = cot_ref[here, :].astype(F32)
        at_row = pl.multiple_of(at * step + third * 128, 128)
        owned = table[pl.ds(at_row, 128), :]
        side_out_ref[here, :] = (owned.astype(F32) + gate * activated).astype(BF16)
        mgrad_ref[here, :] = (
            upstream * gate * squash * (1.0 + message * (1.0 - squash))
        ).astype(BF16)
        term = jnp.sum(upstream * activated, axis=0, keepdims=True)
        part = term if part is None else part + term
    agrad = lax.dot_general(
        mgrad_ref[...], w_ref[...], (((1,), (1,)), ((), ())), preferred_element_type=F32
    ).astype(BF16)

    @pl.when(at == 0)
    def _():
        low_ref[...] = agrad
        gpart_ref[...] = part

    @pl.when(at == 1)
    def _():
        high_ref[...] = agrad
        gpart_ref[...] += part


def layer(index, values, parts, cotangent, w_msg, gate):
    nodes, width = cotangent.shape
    step = nodes // 2
    rows = lambda size: pl.BlockSpec((step, size), lambda i: (i, 0))
    return pl.pallas_call(
        layer_kernel,
        grid=(2,),
        in_specs=[pl.BlockSpec(memory_space=pltpu.SMEM), whole(*values.shape)]
        + [whole(*part.shape) for part in parts]
        + [rows(width), whole(width, width), whole(1, width)],
        out_specs=[rows(width), rows(width), rows(width), whole(step, width), whole(step, width),
                   whole(1, width)],
        out_shape=[bf16(nodes, width), bf16(nodes, width), bf16(nodes, width), bf16(step, width),
                   bf16(step, width),
                   jax.ShapeDtypeStruct((1, width), F32)],
        scratch_shapes=[pltpu.VMEM((4 * nodes, width), BF16)],
        compiler_params=params(40),
        cost_estimate=cost(12e8, 8e6, nodes * width),
    )(index, values, *parts, cotangent, w_msg, gate)


def back_kernel(index_ref, values_ref, *refs):
    parts, (cot_ref, place_ref), (out_ref, table, grad) = refs[:8], refs[8:10], refs[-3:]
    nodes = cot_ref.shape[0]
    per_row = values_ref.shape[0] * 128 // nodes

    @pl.when(pl.program_id(0) == 0)
    def _():
        stage(parts, table)
        for row in range(nodes // 128):
            at = slice(row * 128, (row + 1) * 128)
            total = block_row(index_ref, values_ref, table, row, per_row)
            upstream = cot_ref[at, :].astype(F32)
            grad[at, :] = (upstream + total).astype(BF16)

    mask = iota((out_ref.shape[0], nodes), 1) == place_ref[...]
    out_ref[...] = jnp.dot(one_hot(mask), grad[...], preferred_element_type=F32).astype(BF16)


def back(index, values, parts, cotangent, place, slots):
    nodes = cotangent.shape[0]
    wide = parts[0].shape[1]
    step = slots // 4
    return pl.pallas_call(
        back_kernel,
        grid=(4,),
        in_specs=[pl.BlockSpec(memory_space=pltpu.SMEM), whole(*values.shape)]
        + [whole(*part.shape) for part in parts]
        + [whole(*cotangent.shape), pl.BlockSpec((step, 1), lambda i: (i, 0))],
        out_specs=pl.BlockSpec((step, wide), lambda i: (i, 0)),
        out_shape=bf16(slots, wide),
        scratch_shapes=[pltpu.VMEM((4 * nodes, wide), BF16), pltpu.VMEM((nodes, wide), BF16)],
        compiler_params=params(40),
        cost_estimate=cost(2 * slots * nodes * wide, 5e6),
    )(index, values, *parts, cotangent, place)


def small_kernel(agg_ref, mgrad_ref, gate_ref, after_ref, mine_ref, theirs_ref):
    msg = lax.dot_general(
        agg_ref[...], mgrad_ref[...], (((0,), (0,)), ((), ())), preferred_element_type=F32
    )
    chips, rows, width = mine_ref.shape
    share = width // (2 * chips)
    tail = jnp.concatenate([gate_ref[...], jnp.zeros((rows - share - 1, width), F32)], axis=0)
    core = lax.axis_index("core")
    for this in range(2):
        @pl.when(core == this)
        def _():
            for out_ref, which in ((mine_ref, this), (theirs_ref, 1 - this)):
                for chip in range(chips):
                    at = (chip * 2 + which) * share
                    out_ref[chip, :share, :] = msg[at:at + share, :]
                    out_ref[chip, share:, :] = tail


def small_sums(aggregate, message_grad, gate_part, chips, after):
    width = aggregate.shape[1]
    vmem = pl.BlockSpec(memory_space=pltpu.VMEM)
    out = jax.ShapeDtypeStruct((chips, 24, width), F32)
    return pl.pallas_call(
        small_kernel,
        in_specs=[vmem] * 3 + [pl.BlockSpec(memory_space=pl.ANY)],
        out_specs=[vmem] * 2,
        out_shape=[out, out],
        compiler_params=params(24),
        cost_estimate=cost(4e8, 4e6),
    )(aggregate, message_grad, gate_part, after)


def down_rows(mine_ref, other_ref, grad_ref, other_grad_ref):
    docs = mine_ref.shape[2]
    rows = mine_ref.shape[0] * mine_ref.shape[1]
    left = jnp.concatenate(
        [mine_ref[...].reshape(rows, docs), other_ref[...].reshape(rows, docs)], axis=1
    )
    right = jnp.concatenate([grad_ref[...], other_grad_ref[...]], axis=0)
    return jnp.dot(left, right, preferred_element_type=F32)


def tiles_of(array):
    return [array[:, at:at + 128] for at in range(0, array.shape[1], 128)]


def two_terms(row):
    high = row.astype(BF16).astype(F32)
    return [high, row - high, jnp.zeros((14, 128), F32)]


def small_by_col_kernel(small_ref, other_small_ref, *out_refs):
    small = small_ref[...] + other_small_ref[...]
    chips = small.shape[0]
    msg = (small.shape[1] - 8) // 4
    blocks = []
    for chip in range(chips):
        for col in range(4):
            gate = small[chip, 4 * msg:4 * msg + 1, col * 128:(col + 1) * 128]
            cells = tiles_of(small[chip, col * msg:(col + 1) * msg, :]) + two_terms(gate)
            blocks.append(jnp.concatenate(cells, axis=0).astype(BF16))
    my_col = lax.axis_index("col")
    for first in range(4):
        @pl.when(my_col == first)
        def _():
            for k, out_ref in enumerate(out_refs):
                for chip in range(chips):
                    out_ref[chip] = blocks[chip * 4 + (first + k) % 4]


def small_by_col(small, other_small, cols):
    vmem = pl.BlockSpec(memory_space=pltpu.VMEM)
    return pl.pallas_call(
        small_by_col_kernel,
        in_specs=[vmem] * 2,
        out_specs=[vmem] * cols,
        out_shape=[bf16(small.shape[0], 32, 128)] * cols,
        compiler_params=params(24),
        cost_estimate=cost(1e6, 2e6),
    )(small, other_small)


def lead_kernel(*refs):
    total = sum([ref[...].astype(F32) for ref in refs[1:4]], refs[0][...].astype(F32))
    out_ref = refs[4]
    at = total.shape[1] - 16
    for chip in range(total.shape[0]):
        gate = total[chip, at:at + 1, :] + total[chip, at + 1:at + 2, :]
        cells = [total[chip, :at, :]] + two_terms(gate)
        out_ref[chip] = jnp.concatenate(cells, axis=0).astype(BF16)


def lead_sum(pieces):
    vmem = pl.BlockSpec(memory_space=pltpu.VMEM)
    return pl.pallas_call(
        lead_kernel,
        in_specs=[vmem] * 4,
        out_specs=vmem,
        out_shape=bf16(*pieces[0].shape),
        compiler_params=params(24),
        cost_estimate=cost(1e6, 1e6),
    )(*pieces)


def down_by_chip_kernel(mine_ref, other_ref, grad_ref, other_grad_ref, led_ref, out_ref):
    total = down_rows(mine_ref, other_ref, grad_ref, other_grad_ref)
    chips, share, _ = mine_ref.shape
    led = out_ref.shape[1] - led_ref.shape[1]
    for chip in range(chips):
        cells = tiles_of(total[chip * share:(chip + 1) * share, :])
        out_ref[chip, :led, :] = jnp.concatenate(cells, axis=0).astype(BF16)
        out_ref[chip, led:, :] = led_ref[chip]


def down_specs(mine, grad):
    chips, share, docs = mine.shape
    rows = pl.BlockSpec((chips // 4, share, docs), lambda i: (i, 0, 0))
    return [rows, rows, whole(*grad.shape), whole(*grad.shape)]


def down_by_chip(mine, other, grad, other_grad, led):
    chips, share, docs = mine.shape
    rows = share * grad.shape[1] // 128 + led.shape[1]
    by_chip = lambda size: pl.BlockSpec((chips // 4, size, 128), lambda i: (i, 0, 0))
    return pl.pallas_call(
        down_by_chip_kernel,
        grid=(4,),
        in_specs=down_specs(mine, grad) + [by_chip(led.shape[1])],
        out_specs=by_chip(rows),
        out_shape=bf16(chips, rows, 128),
        compiler_params=params(40),
        cost_estimate=cost(2e9, 12e6),
    )(mine, other, grad, other_grad, led)


def fold_kernel(parts_ref, out_ref):
    total = jnp.sum(parts_ref[...].astype(F32), axis=0)
    at = total.shape[0] - 16
    gate = total[at:at + 1, :] + total[at + 1:at + 2, :]
    out_ref[...] = jnp.concatenate([total[:at, :]] + two_terms(gate), axis=0).astype(BF16)


def fold(parts):
    chips, rows, width = parts.shape
    vmem = pl.BlockSpec(memory_space=pltpu.VMEM)
    return pl.pallas_call(
        fold_kernel,
        in_specs=[vmem],
        out_specs=vmem,
        out_shape=bf16(rows, width),
        compiler_params=params(24),
        cost_estimate=cost(1e6, 2e6),
    )(parts)


def finish_kernel(*refs):
    found, (down_ref, msg_ref, gate_ref) = refs[:4], refs[4:]
    share, width = down_ref.shape
    msg = msg_ref.shape[0]
    my_col = lax.axis_index("col")
    own, near, far, cross = (ref[...].astype(F32) for ref in found)
    total = (own + near) + (far + cross)
    at = 0
    for lane in range(0, width, 128):
        down_ref[:, lane:lane + 128] = total[at:at + share, :]
        at += share

    def from_col(col):
        step = my_col ^ col
        part = own[at:, :]
        for i, other in enumerate((near, far, cross)):
            part = jnp.where(step == i + 1, other[at:, :], part)
        return part

    for col in range(4):
        part = from_col(col)
        row = 0
        for lane in range(0, width, 128):
            msg_ref[col * msg // 4:(col + 1) * msg // 4, lane:lane + 128] = (
                part[row:row + msg // 4, :]
            )
            row += msg // 4
    first = lax.axis_index(ROWS) * msg
    gate = from_col(first // 128)[-16:, :]
    spread = jnp.broadcast_to(gate[0:1, :] + gate[1:2, :], (8, 128))
    gate_ref[...] = pltpu.roll(spread, (128 - first % 128) % 128, 1)[:1, :msg]


def finish(found, share, msg, width):
    vmem = pl.BlockSpec(memory_space=pltpu.VMEM)
    shape = lambda *dims: jax.ShapeDtypeStruct(dims, F32)
    return pl.pallas_call(
        finish_kernel,
        in_specs=[vmem] * 4,
        out_specs=[vmem] * 3,
        out_shape=[shape(share, width), shape(msg, width), shape(1, msg)],
        compiler_params=params(24),
        cost_estimate=cost(1e6, 1e6),
    )(*found)


def relay(rows):
    slots, width = rows.shape
    size = lax.axis_size(ROWS)
    moved = lax.all_to_all(
        rows.reshape(size, slots // size, width), ROWS, split_axis=0, concat_axis=0, tiled=True
    )
    return moved.reshape(slots, width)


def shards(doc_taps, w_down, owner_of, adj_values, adj_index, w_msg, gate_scale, cotangent):
    docs = doc_taps.shape[0]
    depth, width = w_down.shape
    row_size, cols = lax.axis_size(ROWS), lax.axis_size("col")
    my_row, my_col = lax.axis_index(ROWS), lax.axis_index("col")
    slots = row_size * SLOTS
    chips = row_size // 2
    values = adj_values[0]
    blocks = docs // 128
    index = (adj_index[0] // blocks - my_col) % cols * blocks + adj_index[0] % blocks
    gate = gate_scale.reshape(1, width)
    swap = lambda array: lax.ppermute(array, "core", [(0, 1), (1, 0)])

    taps = taps_by_tile(doc_taps)
    packed, slot = pool_and_pack(owner_of, taps, w_down, slots)
    incoming = relay(packed)
    mine, theirs, turned = pool_and_turn(taps, depth, chips, slot)
    other = swap(theirs)

    owners = owner_of[0]
    counts = jnp.sum((owners.reshape(row_size, docs) == my_row).astype(jnp.int32), axis=1)
    lower = jnp.arange(row_size)[None, :] < jnp.arange(row_size)[:, None]
    starts = jnp.sum(jnp.where(lower, counts[None, :], 0), axis=1)
    in_slot = jnp.arange(SLOTS, dtype=jnp.int32)[None, :]
    position = jnp.where(in_slot < counts[:, None], starts[:, None] + in_slot, -1).reshape(slots)
    pos_row, pos_col = position.reshape(1, slots), position.reshape(slots, 1)

    owned = take(pos_row, incoming, docs, halves=True, after=(turned,))
    side_out, aggregate, message_grad, low, high, gate_part = layer(
        index, values, gather_ring(*owned), cotangent, w_msg, gate
    )

    packed_back = back(index, values, gather_ring(low, high), cotangent, pos_col, slots)
    returned = relay(packed_back)

    small, other_small = small_sums(aggregate, message_grad, gate_part, chips, packed_back)
    pieces = small_by_col(small, swap(other_small), cols)
    led = lead_sum([pieces[0]] + [shift(pieces[k], k) for k in range(1, cols)])
    grad = take(slot.reshape(docs, 1), returned, docs, after=(led,))
    down = down_by_chip(mine, other, grad, swap(grad), led)
    down = lax.all_to_all(down, ("z", "x"), split_axis=0, concat_axis=0, tiled=True)
    own = fold(down)
    found = [own] + [
        lax.ppermute(own, "col", [(c, c ^ step) for c in range(4)]) for step in (1, 2, 3)
    ]
    grad_down, grad_msg, grad_gate = finish(found, depth // row_size, width // row_size, width)
    return side_out, grad_down, grad_msg, grad_gate.reshape(width // row_size)


def solution(mesh):
    rows, cols = mesh.devices.shape
    z = 4
    x = rows // (2 * z)
    split = Mesh(mesh.devices.reshape(z, x, 2, cols), ("z", "x", "core", "col"))
    each = ROWS + ("col",)
    placed = (
        P(each, None, None),
        P(),
        P("col", None),
        P(each, None, None, None),
        P(each, None),
        P(),
        P(),
        P(each, None),
    )
    return jax.shard_map(
        shards,
        mesh=split,
        in_specs=placed,
        out_specs=(P(each, None), P(ROWS, None), P(ROWS, None), P(ROWS)),
        check_vma=False,
    )
```

```python
import functools

import jax
import jax.numpy as jnp
import numpy as np
from jax import lax
from jax.experimental import pallas as pl
from jax.experimental.pallas import tpu as pltpu
from jax.sharding import Mesh
from jax.sharding import PartitionSpec as P

ROWS = ("z", "x", "core")
BF16 = jnp.bfloat16
F32 = jnp.float32
SLOTS = 72


def iota(shape, dim):
    return lax.broadcasted_iota(jnp.int32, shape, dim)


def one_hot(mask):
    return jnp.where(mask, 1.0, 0.0).astype(BF16)


def params(mib=60):
    return pltpu.CompilerParams(vmem_limit_bytes=mib * 1024 * 1024)


def cost(flops, moved, special=0):
    return pl.CostEstimate(flops=int(flops), bytes_accessed=int(moved), transcendentals=int(special))


def whole(*shape):
    return pl.BlockSpec(shape, lambda i: (0,) * len(shape))


def bf16(*shape):
    return jax.ShapeDtypeStruct(shape, BF16)


STREAMS = 4


def pool_tiles(pick, x_refs, pooled_ref):
    tiles = x_refs[0].shape[1] // 16
    docs = x_refs[0].shape[0]
    for stream, x_ref in enumerate(x_refs):
        block = jnp.concatenate(
            [
                x_ref[at:at + 16, t * 16:(t + 1) * 16, :].reshape(256, 128)
                for at in range(0, docs, 16)
                for t in range(tiles)
            ],
            axis=1,
        )
        mean = jnp.dot(pick[...], block, preferred_element_type=F32).astype(BF16)
        for group in range(docs // 16):
            first = stream * docs + group * 16
            for j in range(8):
                for t in range(tiles):
                    at, lane = (t * 8 + j) * 128, (group * tiles + t) * 128
                    pooled_ref[first:first + 16, at:at + 128] = (
                        mean[j * 16:(j + 1) * 16, lane:lane + 128]
                    )


def set_pick(pick):
    out_row, in_row = iota((128, 256), 0), iota((128, 256), 1)
    same_doc = out_row % 16 == in_row // 16
    same_tile = out_row // 16 == (in_row % 16) // 2
    pick[...] = jnp.where(same_doc & same_tile, 0.5, 0.0).astype(BF16)


def pool_kernel(owner_ref, *refs):
    x_refs, (w_hbm, out_ref, slot_ref) = refs[:STREAMS], refs[STREAMS:STREAMS + 3]
    pick, pooled, side, w_ref, w_sem, chosen = refs[STREAMS + 3:]
    at = pl.program_id(0)
    steps = pl.num_programs(0)
    docs = side.shape[0]
    step = STREAMS * x_refs[0].shape[0]
    share = out_ref.shape[0] // 6
    load = pltpu.make_async_copy(w_hbm, w_ref, w_sem)

    @pl.when(at == 0)
    def _():
        load.start()
        set_pick(pick)
        first = pl.multiple_of(lax.axis_index(ROWS) * docs, 128)
        dest = owner_ref[:, pl.ds(first, docs)]
        hit = iota((32, docs), 0) == dest
        earlier = one_hot(iota((docs, docs), 0) < iota((docs, docs), 1))
        before = jnp.dot(one_hot(hit), earlier, preferred_element_type=F32)
        rank = jnp.sum(jnp.where(hit, before, 0.0), axis=0, keepdims=True)
        slot_ref[...] = dest * SLOTS + rank.astype(jnp.int32)

    pool_tiles(pick, x_refs, pooled.at[pl.ds(pl.multiple_of(at * step, step), step)])
    rows = iota((share, docs), 0) + at * share
    chosen[pl.ds(pl.multiple_of(at * share, 16), share), :] = one_hot(rows == slot_ref[...])

    @pl.when(at == steps - 1)
    def _():
        load.wait()
        side[...] = jnp.dot(pooled[...], w_ref[...], preferred_element_type=F32).astype(BF16)
        for part in range(6):
            rows = slice(part * share, (part + 1) * share)
            out_ref[rows, :] = jnp.dot(
                chosen[rows, :], side[...], preferred_element_type=F32
            ).astype(BF16)


def turn_kernel(*refs):
    x_refs, (mine_ref, theirs_ref, done_ref, pick, pooled) = refs[:STREAMS], refs[STREAMS + 1:]

    @pl.when(pl.program_id(0) == 0)
    def _():
        set_pick(pick)
        done_ref[...] = jnp.zeros_like(done_ref)

    pool_tiles(pick, x_refs, pooled)
    rows = mine_ref.shape[1]
    core = lax.axis_index("core")
    for pair in range(mine_ref.shape[0] // 2):
        turned = pooled[:, pair * 4 * rows:(pair + 1) * 4 * rows].T
        for this in range(2):
            @pl.when(core == this)
            def _():
                for turned_ref, which in ((mine_ref, this), (theirs_ref, 1 - this)):
                    for chip in range(2):
                        at = (chip * 2 + which) * rows
                        turned_ref[pair * 2 + chip] = turned[at:at + rows, :]


def taps_by_tile(doc_taps):
    docs, tokens, depth = doc_taps.shape
    tiles = depth // 128
    taps = doc_taps.reshape(docs, tokens, tiles, 128).transpose(0, 2, 1, 3)
    return taps.reshape(docs, tokens * tiles, 128)


def streams(step, rows):
    def spec(stream):
        return pl.BlockSpec((step // STREAMS, rows, 128), lambda i: (i * STREAMS + stream, 0, 0))

    return [spec(stream) for stream in range(STREAMS)]


def pool_and_pack(owner_of, taps, w_down, slots):
    docs, rows, _ = taps.shape
    depth, width = w_down.shape
    return pl.pallas_call(
        pool_kernel,
        grid=(6,),
        in_specs=[
            whole(*owner_of.shape),
            *streams(docs // 6, rows),
            pl.BlockSpec(memory_space=pl.ANY),
        ],
        out_specs=[whole(slots, width), whole(1, docs)],
        out_shape=[bf16(slots, width), jax.ShapeDtypeStruct((1, docs), jnp.int32)],
        scratch_shapes=[
            pltpu.VMEM((128, 256), BF16),
            pltpu.VMEM((docs, depth), BF16),
            pltpu.VMEM((docs, width), BF16),
            pltpu.VMEM((depth, width), BF16),
            pltpu.SemaphoreType.DMA,
            pltpu.VMEM((slots, docs), BF16),
        ],
        compiler_params=params(),
        cost_estimate=cost(8e9, 23e6),
    )(owner_of, *[taps] * STREAMS, w_down)


def pool_and_turn(taps, depth, chips, after, slots):
    docs, rows, _ = taps.shape
    step = docs // 6
    turned = pl.BlockSpec((chips, depth // (2 * chips), step), lambda i: (0, 0, i))
    return pl.pallas_call(
        turn_kernel,
        grid=(6,),
        in_specs=streams(step, rows) + [pl.BlockSpec(memory_space=pl.ANY)],
        out_specs=[turned, turned, whole(1, slots)],
        out_shape=[bf16(chips, depth // (2 * chips), docs)] * 2
        + [jax.ShapeDtypeStruct((1, slots), jnp.int32)],
        scratch_shapes=[pltpu.VMEM((128, 256), BF16), pltpu.VMEM((step, depth), BF16)],
        compiler_params=params(),
        cost_estimate=cost(2e9, 24e6),
    )(*[taps] * STREAMS, after)


def take_kernel(waited, place_ref, table_ref, *out_refs):
    at = pl.program_id(0)
    out_refs = out_refs[waited:]
    depth = table_ref.shape[0]
    step = out_refs[0].shape[0]
    if place_ref.shape[0] == 1:
        mask = iota((step, depth), 0) + at * step == place_ref[...]
    else:
        mask = iota((step, depth), 1) == place_ref[...]
    rows = jnp.dot(one_hot(mask), table_ref[...], preferred_element_type=F32).astype(BF16)
    if len(out_refs) == 1:
        out_refs[0][...] = rows
    else:
        for i, out_ref in enumerate(out_refs):
            @pl.when(at == i)
            def _():
                out_ref[...] = rows


def take(place, table, count, halves=False, after=()):
    depth, width = table.shape
    step = count // 2
    if place.shape[0] == 1:
        place_spec = whole(1, depth)
    else:
        place_spec = pl.BlockSpec((step, 1), lambda i: (i, 0))
    if halves:
        out_specs, out_shape = [whole(step, width)] * 2, [bf16(step, width)] * 2
    else:
        out_specs, out_shape = pl.BlockSpec((step, width), lambda i: (i, 0)), bf16(count, width)
    return pl.pallas_call(
        functools.partial(take_kernel, len(after)),
        grid=(2,),
        in_specs=[place_spec, whole(depth, width)]
        + [pl.BlockSpec(memory_space=pl.ANY) for _ in after],
        out_specs=out_specs,
        out_shape=out_shape,
        compiler_params=params(24),
        cost_estimate=cost(2 * count * depth * width, 2e6),
    )(place, table, *after)


def shift(part, by):
    return lax.ppermute(part, "col", [(c, (c + by) % 4) for c in range(4)])


def gather_ring(low, high):
    before_low, after_high = shift(low, 1), shift(high, 3)
    before_high, after_low = shift(high, 1), shift(low, 3)
    far_low, far_high = shift(before_low, 1), shift(after_high, 3)
    return low, high, after_low, after_high, far_low, far_high, before_low, before_high


def stage(parts, table):
    at = 0
    for part in parts:
        table[at:at + part.shape[0], :] = part[...]
        at += part.shape[0]


def block_row(index_ref, values_ref, table, row, per_row):
    entries = [row * per_row + k for k in range(per_row)]
    at = [pl.multiple_of(index_ref[entry] * 128, 128) for entry in entries]
    blocks = jnp.concatenate([values_ref[entry] for entry in entries], axis=1)
    picked = jnp.concatenate([table[pl.ds(first, 128), :] for first in at], axis=0)
    return jnp.dot(blocks, picked, preferred_element_type=F32)


def layer_kernel(index_ref, values_ref, *refs):
    parts = refs[:8]
    (cot_ref, w_ref, gate_ref) = refs[8:11]
    (side_out_ref, agg_ref, mgrad_ref, low_ref, high_ref, gpart_ref, table) = refs[11:]
    at = pl.program_id(0)

    @pl.when(at == 0)
    def _():
        stage(parts, table)

    step = cot_ref.shape[0]
    nodes = step * pl.num_programs(0)
    per_row = values_ref.shape[0] * 128 // nodes
    rows = step // 128
    for row in range(rows):
        agg_ref[row * 128:(row + 1) * 128, :] = block_row(
            index_ref, values_ref, table, at * rows + row, per_row
        ).astype(BF16)
    gate = gate_ref[...]
    part = None
    for third in range(rows):
        here = slice(third * 128, (third + 1) * 128)
        message = jnp.dot(agg_ref[here, :], w_ref[...], preferred_element_type=F32)
        squash = jax.nn.sigmoid(message)
        activated = message * squash
        upstream = cot_ref[here, :].astype(F32)
        at_row = pl.multiple_of(at * step + third * 128, 128)
        owned = table[pl.ds(at_row, 128), :]
        side_out_ref[here, :] = (owned.astype(F32) + gate * activated).astype(BF16)
        mgrad_ref[here, :] = (
            upstream * gate * squash * (1.0 + message * (1.0 - squash))
        ).astype(BF16)
        term = jnp.sum(upstream * activated, axis=0, keepdims=True)
        part = term if part is None else part + term
    agrad = lax.dot_general(
        mgrad_ref[...], w_ref[...], (((1,), (1,)), ((), ())), preferred_element_type=F32
    ).astype(BF16)

    @pl.when(at == 0)
    def _():
        low_ref[...] = agrad
        gpart_ref[...] = part

    @pl.when(at == 1)
    def _():
        high_ref[...] = agrad
        gpart_ref[...] += part


def layer(index, values, parts, cotangent, w_msg, gate):
    nodes, width = cotangent.shape
    step = nodes // 2
    rows = lambda size: pl.BlockSpec((step, size), lambda i: (i, 0))
    return pl.pallas_call(
        layer_kernel,
        grid=(2,),
        in_specs=[pl.BlockSpec(memory_space=pltpu.SMEM), whole(*values.shape)]
        + [whole(*part.shape) for part in parts]
        + [rows(width), whole(width, width), whole(1, width)],
        out_specs=[rows(width), rows(width), rows(width), whole(step, width), whole(step, width),
                   whole(1, width)],
        out_shape=[bf16(nodes, width), bf16(nodes, width), bf16(nodes, width), bf16(step, width),
                   bf16(step, width),
                   jax.ShapeDtypeStruct((1, width), F32)],
        scratch_shapes=[pltpu.VMEM((4 * nodes, width), BF16)],
        compiler_params=params(),
        cost_estimate=cost(12e8, 8e6, nodes * width),
    )(index, values, *parts, cotangent, w_msg, gate)


def back_kernel(index_ref, values_ref, *refs):
    parts, (cot_ref, place_ref), (out_ref, table, grad) = refs[:8], refs[8:10], refs[-3:]
    nodes = cot_ref.shape[0]
    per_row = values_ref.shape[0] * 128 // nodes

    @pl.when(pl.program_id(0) == 0)
    def _():
        stage(parts, table)
        for row in range(nodes // 128):
            at = slice(row * 128, (row + 1) * 128)
            total = block_row(index_ref, values_ref, table, row, per_row)
            upstream = cot_ref[at, :].astype(F32)
            grad[at, :] = (upstream + total).astype(BF16)

    mask = iota((out_ref.shape[0], nodes), 1) == place_ref[...]
    out_ref[...] = jnp.dot(one_hot(mask), grad[...], preferred_element_type=F32).astype(BF16)


def back(index, values, parts, cotangent, place, slots):
    nodes = cotangent.shape[0]
    wide = parts[0].shape[1]
    step = slots // 4
    return pl.pallas_call(
        back_kernel,
        grid=(4,),
        in_specs=[pl.BlockSpec(memory_space=pltpu.SMEM), whole(*values.shape)]
        + [whole(*part.shape) for part in parts]
        + [whole(*cotangent.shape), pl.BlockSpec((step, 1), lambda i: (i, 0))],
        out_specs=pl.BlockSpec((step, wide), lambda i: (i, 0)),
        out_shape=bf16(slots, wide),
        scratch_shapes=[pltpu.VMEM((4 * nodes, wide), BF16), pltpu.VMEM((nodes, wide), BF16)],
        compiler_params=params(40),
        cost_estimate=cost(2 * slots * nodes * wide, 5e6),
    )(index, values, *parts, cotangent, place)


def small_kernel(agg_ref, mgrad_ref, gate_ref, after_ref, mine_ref, theirs_ref):
    msg = lax.dot_general(
        agg_ref[...], mgrad_ref[...], (((0,), (0,)), ((), ())), preferred_element_type=F32
    )
    chips, rows, width = mine_ref.shape
    share = width // (2 * chips)
    tail = jnp.concatenate([gate_ref[...], jnp.zeros((rows - share - 1, width), F32)], axis=0)
    core = lax.axis_index("core")
    for this in range(2):
        @pl.when(core == this)
        def _():
            for out_ref, which in ((mine_ref, this), (theirs_ref, 1 - this)):
                for chip in range(chips):
                    at = (chip * 2 + which) * share
                    out_ref[chip, :share, :] = msg[at:at + share, :]
                    out_ref[chip, share:, :] = tail


def small_sums(aggregate, message_grad, gate_part, chips, after):
    width = aggregate.shape[1]
    vmem = pl.BlockSpec(memory_space=pltpu.VMEM)
    out = jax.ShapeDtypeStruct((chips, 24, width), F32)
    return pl.pallas_call(
        small_kernel,
        in_specs=[vmem] * 3 + [pl.BlockSpec(memory_space=pl.ANY)],
        out_specs=[vmem] * 2,
        out_shape=[out, out],
        compiler_params=params(24),
        cost_estimate=cost(4e8, 4e6),
    )(aggregate, message_grad, gate_part, after)


def down_rows(mine_ref, other_ref, grad_ref, other_grad_ref):
    docs = mine_ref.shape[2]
    rows = mine_ref.shape[0] * mine_ref.shape[1]
    left = jnp.concatenate(
        [mine_ref[...].reshape(rows, docs), other_ref[...].reshape(rows, docs)], axis=1
    )
    right = jnp.concatenate([grad_ref[...], other_grad_ref[...]], axis=0)
    return jnp.dot(left, right, preferred_element_type=F32)


def tiles_of(array):
    return [array[:, at:at + 128] for at in range(0, array.shape[1], 128)]


def two_terms(row):
    high = row.astype(BF16).astype(F32)
    return [high, row - high, jnp.zeros((14, 128), F32)]


def small_by_col_kernel(small_ref, other_small_ref, *out_refs):
    small = small_ref[...] + other_small_ref[...]
    chips = small.shape[0]
    msg = (small.shape[1] - 8) // 4
    blocks = []
    for chip in range(chips):
        for col in range(4):
            gate = small[chip, 4 * msg:4 * msg + 1, col * 128:(col + 1) * 128]
            cells = tiles_of(small[chip, col * msg:(col + 1) * msg, :]) + two_terms(gate)
            blocks.append(jnp.concatenate(cells, axis=0).astype(BF16))
    my_col = lax.axis_index("col")
    for first in range(4):
        @pl.when(my_col == first)
        def _():
            for k, out_ref in enumerate(out_refs):
                for chip in range(chips):
                    out_ref[chip] = blocks[chip * 4 + (first + k) % 4]


def small_by_col(small, other_small, cols):
    vmem = pl.BlockSpec(memory_space=pltpu.VMEM)
    return pl.pallas_call(
        small_by_col_kernel,
        in_specs=[vmem] * 2,
        out_specs=[vmem] * cols,
        out_shape=[bf16(small.shape[0], 32, 128)] * cols,
        compiler_params=params(24),
        cost_estimate=cost(1e6, 2e6),
    )(small, other_small)


def lead_kernel(*refs):
    total = sum([ref[...].astype(F32) for ref in refs[1:4]], refs[0][...].astype(F32))
    out_ref = refs[4]
    at = total.shape[1] - 16
    for chip in range(total.shape[0]):
        gate = total[chip, at:at + 1, :] + total[chip, at + 1:at + 2, :]
        cells = [total[chip, :at, :]] + two_terms(gate)
        out_ref[chip] = jnp.concatenate(cells, axis=0).astype(BF16)


def lead_sum(pieces):
    vmem = pl.BlockSpec(memory_space=pltpu.VMEM)
    return pl.pallas_call(
        lead_kernel,
        in_specs=[vmem] * 4,
        out_specs=vmem,
        out_shape=bf16(*pieces[0].shape),
        compiler_params=params(24),
        cost_estimate=cost(1e6, 1e6),
    )(*pieces)


def down_by_chip_kernel(mine_ref, other_ref, grad_ref, other_grad_ref, led_ref, out_ref):
    total = down_rows(mine_ref, other_ref, grad_ref, other_grad_ref)
    chips, share, _ = mine_ref.shape
    led = out_ref.shape[1] - led_ref.shape[1]
    for chip in range(chips):
        cells = tiles_of(total[chip * share:(chip + 1) * share, :])
        out_ref[chip, :led, :] = jnp.concatenate(cells, axis=0).astype(BF16)
        out_ref[chip, led:, :] = led_ref[chip]


def down_specs(mine, grad):
    chips, share, docs = mine.shape
    rows = pl.BlockSpec((chips // 4, share, docs), lambda i: (i, 0, 0))
    return [rows, rows, whole(*grad.shape), whole(*grad.shape)]


def down_by_chip(mine, other, grad, other_grad, led):
    chips, share, docs = mine.shape
    rows = share * grad.shape[1] // 128 + led.shape[1]
    by_chip = lambda size: pl.BlockSpec((chips // 4, size, 128), lambda i: (i, 0, 0))
    return pl.pallas_call(
        down_by_chip_kernel,
        grid=(4,),
        in_specs=down_specs(mine, grad) + [by_chip(led.shape[1])],
        out_specs=by_chip(rows),
        out_shape=bf16(chips, rows, 128),
        compiler_params=params(40),
        cost_estimate=cost(2e9, 12e6),
    )(mine, other, grad, other_grad, led)


def fold_kernel(parts_ref, out_ref):
    total = jnp.sum(parts_ref[...].astype(F32), axis=0)
    at = total.shape[0] - 16
    gate = total[at:at + 1, :] + total[at + 1:at + 2, :]
    out_ref[...] = jnp.concatenate([total[:at, :]] + two_terms(gate), axis=0).astype(BF16)


def fold(parts):
    chips, rows, width = parts.shape
    vmem = pl.BlockSpec(memory_space=pltpu.VMEM)
    return pl.pallas_call(
        fold_kernel,
        in_specs=[vmem],
        out_specs=vmem,
        out_shape=bf16(rows, width),
        compiler_params=params(24),
        cost_estimate=cost(1e6, 2e6),
    )(parts)


def finish_kernel(*refs):
    found, (down_ref, msg_ref, gate_ref) = refs[:4], refs[4:]
    share, width = down_ref.shape
    msg = msg_ref.shape[0]
    my_col = lax.axis_index("col")
    own, near, far, cross = (ref[...].astype(F32) for ref in found)
    total = (own + near) + (far + cross)
    at = 0
    for lane in range(0, width, 128):
        down_ref[:, lane:lane + 128] = total[at:at + share, :]
        at += share

    def from_col(col):
        step = my_col ^ col
        part = own[at:, :]
        for i, other in enumerate((near, far, cross)):
            part = jnp.where(step == i + 1, other[at:, :], part)
        return part

    for col in range(4):
        part = from_col(col)
        row = 0
        for lane in range(0, width, 128):
            msg_ref[col * msg // 4:(col + 1) * msg // 4, lane:lane + 128] = (
                part[row:row + msg // 4, :]
            )
            row += msg // 4
    first = lax.axis_index(ROWS) * msg
    gate = from_col(first // 128)[-16:, :]
    spread = jnp.broadcast_to(gate[0:1, :] + gate[1:2, :], (8, 128))
    gate_ref[...] = pltpu.roll(spread, (128 - first % 128) % 128, 1)[:1, :msg]


def finish(found, share, msg, width):
    vmem = pl.BlockSpec(memory_space=pltpu.VMEM)
    shape = lambda *dims: jax.ShapeDtypeStruct(dims, F32)
    return pl.pallas_call(
        finish_kernel,
        in_specs=[vmem] * 4,
        out_specs=[vmem] * 3,
        out_shape=[shape(share, width), shape(msg, width), shape(1, msg)],
        compiler_params=params(24),
        cost_estimate=cost(1e6, 1e6),
    )(*found)


def relay(rows):
    slots, width = rows.shape
    size = lax.axis_size(ROWS)
    moved = lax.all_to_all(
        rows.reshape(size, slots // size, width), ROWS, split_axis=0, concat_axis=0, tiled=True
    )
    return moved.reshape(slots, width)


def shards(doc_taps, w_down, owner_of, adj_values, adj_index, w_msg, gate_scale, cotangent):
    docs = doc_taps.shape[0]
    depth, width = w_down.shape
    row_size, cols = lax.axis_size(ROWS), lax.axis_size("col")
    my_row, my_col = lax.axis_index(ROWS), lax.axis_index("col")
    slots = row_size * SLOTS
    chips = row_size // 2
    values = adj_values[0]
    blocks = docs // 128
    index = (adj_index[0] // blocks - my_col) % cols * blocks + adj_index[0] % blocks
    gate = gate_scale.reshape(1, width)
    swap = lambda array: lax.ppermute(array, "core", [(0, 1), (1, 0)])

    taps = taps_by_tile(doc_taps)
    packed, slot = pool_and_pack(owner_of, taps, w_down, slots)
    incoming = relay(packed)
    mine, theirs, turned = pool_and_turn(taps, depth, chips, slot, slots)
    other = swap(theirs)

    owners = owner_of[0]
    counts = jnp.sum((owners.reshape(row_size, docs) == my_row).astype(jnp.int32), axis=1)
    lower = jnp.arange(row_size)[None, :] < jnp.arange(row_size)[:, None]
    starts = jnp.sum(jnp.where(lower, counts[None, :], 0), axis=1)
    in_slot = jnp.arange(SLOTS, dtype=jnp.int32)[None, :]
    position = jnp.where(in_slot < counts[:, None], starts[:, None] + in_slot, -1).reshape(slots)
    pos_row, pos_col = position.reshape(1, slots) + turned, position.reshape(slots, 1)

    owned = take(pos_row, incoming, docs, halves=True)
    side_out, aggregate, message_grad, low, high, gate_part = layer(
        index, values, gather_ring(*owned), cotangent, w_msg, gate
    )

    packed_back = back(index, values, gather_ring(low, high), cotangent, pos_col, slots)
    returned = relay(packed_back)

    small, other_small = small_sums(aggregate, message_grad, gate_part, chips, packed_back)
    pieces = small_by_col(small, swap(other_small), cols)
    led = lead_sum([pieces[0]] + [shift(pieces[k], k) for k in range(1, cols)])
    grad = take(slot.reshape(docs, 1), returned, docs, after=(led,))
    down = down_by_chip(mine, other, grad, swap(grad), led)
    down = lax.all_to_all(down, ("z", "x"), split_axis=0, concat_axis=0, tiled=True)
    own = fold(down)
    found = [own] + [
        lax.ppermute(own, "col", [(c, c ^ step) for c in range(4)]) for step in (1, 2, 3)
    ]
    grad_down, grad_msg, grad_gate = finish(found, depth // row_size, width // row_size, width)
    return side_out, grad_down, grad_msg, grad_gate.reshape(width // row_size)


def solution(mesh):
    rows, cols = mesh.devices.shape
    z = 4
    x = rows // (2 * z)
    split = Mesh(mesh.devices.reshape(z, x, 2, cols), ("z", "x", "core", "col"))
    each = ROWS + ("col",)
    placed = (
        P(each, None, None),
        P(),
        P("col", None),
        P(each, None, None, None),
        P(each, None),
        P(),
        P(),
        P(each, None),
    )
    return jax.shard_map(
        shards,
        mesh=split,
        in_specs=placed,
        out_specs=(P(each, None), P(ROWS, None), P(ROWS, None), P(ROWS)),
        check_vma=False,
    )
```

```python
import functools

import jax
import jax.numpy as jnp
import numpy as np
from jax import lax
from jax.experimental import pallas as pl
from jax.experimental.pallas import tpu as pltpu
from jax.sharding import Mesh
from jax.sharding import PartitionSpec as P

ROWS = ("z", "x", "core")
BF16 = jnp.bfloat16
F32 = jnp.float32
SLOTS = 72


def iota(shape, dim):
    return lax.broadcasted_iota(jnp.int32, shape, dim)


def one_hot(mask):
    return jnp.where(mask, 1.0, 0.0).astype(BF16)


def params(mib=60):
    return pltpu.CompilerParams(vmem_limit_bytes=mib * 1024 * 1024)


def cost(flops, moved, special=0):
    return pl.CostEstimate(flops=int(flops), bytes_accessed=int(moved), transcendentals=int(special))


def whole(*shape):
    return pl.BlockSpec(shape, lambda i: (0,) * len(shape))


def bf16(*shape):
    return jax.ShapeDtypeStruct(shape, BF16)


STREAMS = 4


def pool_tiles(pick, x_refs, pooled_ref):
    tiles = x_refs[0].shape[1] // 16
    docs = x_refs[0].shape[0]
    for stream, x_ref in enumerate(x_refs):
        block = jnp.concatenate(
            [
                x_ref[at:at + 16, t * 16:(t + 1) * 16, :].reshape(256, 128)
                for at in range(0, docs, 16)
                for t in range(tiles)
            ],
            axis=1,
        )
        mean = jnp.dot(pick[...], block, preferred_element_type=F32).astype(BF16)
        for group in range(docs // 16):
            first = stream * docs + group * 16
            for j in range(8):
                for t in range(tiles):
                    at, lane = (t * 8 + j) * 128, (group * tiles + t) * 128
                    pooled_ref[first:first + 16, at:at + 128] = (
                        mean[j * 16:(j + 1) * 16, lane:lane + 128]
                    )


def set_pick(pick):
    out_row, in_row = iota((128, 256), 0), iota((128, 256), 1)
    same_doc = out_row % 16 == in_row // 16
    same_tile = out_row // 16 == (in_row % 16) // 2
    pick[...] = jnp.where(same_doc & same_tile, 0.5, 0.0).astype(BF16)


def pool_kernel(owner_ref, *refs):
    x_refs, (w_hbm, out_ref, slot_ref) = refs[:STREAMS], refs[STREAMS:STREAMS + 3]
    pick, pooled, side, w_ref, w_sem, chosen = refs[STREAMS + 3:]
    at = pl.program_id(0)
    steps = pl.num_programs(0)
    docs = side.shape[0]
    step = STREAMS * x_refs[0].shape[0]
    share = out_ref.shape[0] // 6
    load = pltpu.make_async_copy(w_hbm, w_ref, w_sem)

    @pl.when(at == 0)
    def _():
        load.start()
        set_pick(pick)
        first = pl.multiple_of(lax.axis_index(ROWS) * docs, 128)
        dest = owner_ref[:, pl.ds(first, docs)]
        hit = iota((32, docs), 0) == dest
        earlier = one_hot(iota((docs, docs), 0) < iota((docs, docs), 1))
        before = jnp.dot(one_hot(hit), earlier, preferred_element_type=F32)
        rank = jnp.sum(jnp.where(hit, before, 0.0), axis=0, keepdims=True)
        slot_ref[...] = dest * SLOTS + rank.astype(jnp.int32)

    pool_tiles(pick, x_refs, pooled.at[pl.ds(pl.multiple_of(at * step, step), step)])
    rows = iota((share, docs), 0) + at * share
    chosen[pl.ds(pl.multiple_of(at * share, 16), share), :] = one_hot(rows == slot_ref[...])

    @pl.when(at == steps - 1)
    def _():
        load.wait()
        side[...] = jnp.dot(pooled[...], w_ref[...], preferred_element_type=F32).astype(BF16)
        for part in range(6):
            rows = slice(part * share, (part + 1) * share)
            out_ref[rows, :] = jnp.dot(
                chosen[rows, :], side[...], preferred_element_type=F32
            ).astype(BF16)


def turn_kernel(*refs):
    x_refs, (mine_ref, theirs_ref, done_ref, pick, pooled) = refs[:STREAMS], refs[STREAMS + 1:]

    @pl.when(pl.program_id(0) == 0)
    def _():
        set_pick(pick)
        done_ref[...] = jnp.zeros_like(done_ref)

    pool_tiles(pick, x_refs, pooled)
    rows = mine_ref.shape[1]
    core = lax.axis_index("core")
    for pair in range(mine_ref.shape[0] // 2):
        turned = pooled[:, pair * 4 * rows:(pair + 1) * 4 * rows].T
        for this in range(2):
            @pl.when(core == this)
            def _():
                for turned_ref, which in ((mine_ref, this), (theirs_ref, 1 - this)):
                    for chip in range(2):
                        at = (chip * 2 + which) * rows
                        turned_ref[pair * 2 + chip] = turned[at:at + rows, :]


def taps_by_tile(doc_taps):
    docs, tokens, depth = doc_taps.shape
    tiles = depth // 128
    taps = doc_taps.reshape(docs, tokens, tiles, 128).transpose(0, 2, 1, 3)
    return taps.reshape(docs, tokens * tiles, 128)


def streams(step, rows):
    def spec(stream):
        return pl.BlockSpec((step // STREAMS, rows, 128), lambda i: (i * STREAMS + stream, 0, 0))

    return [spec(stream) for stream in range(STREAMS)]


def pool_and_pack(owner_of, taps, w_down, slots):
    docs, rows, _ = taps.shape
    depth, width = w_down.shape
    return pl.pallas_call(
        pool_kernel,
        grid=(6,),
        in_specs=[
            whole(*owner_of.shape),
            *streams(docs // 6, rows),
            pl.BlockSpec(memory_space=pl.ANY),
        ],
        out_specs=[whole(slots, width), whole(1, docs)],
        out_shape=[bf16(slots, width), jax.ShapeDtypeStruct((1, docs), jnp.int32)],
        scratch_shapes=[
            pltpu.VMEM((128, 256), BF16),
            pltpu.VMEM((docs, depth), BF16),
            pltpu.VMEM((docs, width), BF16),
            pltpu.VMEM((depth, width), BF16),
            pltpu.SemaphoreType.DMA,
            pltpu.VMEM((slots, docs), BF16),
        ],
        compiler_params=params(),
        cost_estimate=cost(8e9, 23e6),
    )(owner_of, *[taps] * STREAMS, w_down)


def pool_and_turn(taps, depth, chips, after, slots):
    docs, rows, _ = taps.shape
    step = docs // 6
    turned = pl.BlockSpec((chips, depth // (2 * chips), step), lambda i: (0, 0, i))
    return pl.pallas_call(
        turn_kernel,
        grid=(6,),
        in_specs=streams(step, rows) + [pl.BlockSpec(memory_space=pl.ANY)],
        out_specs=[turned, turned, whole(1, slots)],
        out_shape=[bf16(chips, depth // (2 * chips), docs)] * 2
        + [jax.ShapeDtypeStruct((1, slots), jnp.int32)],
        scratch_shapes=[pltpu.VMEM((128, 256), BF16), pltpu.VMEM((step, depth), BF16)],
        compiler_params=params(),
        cost_estimate=cost(2e9, 24e6),
    )(*[taps] * STREAMS, after)


def take_kernel(waited, place_ref, table_ref, *out_refs):
    at = pl.program_id(0)
    out_refs = out_refs[waited:]
    depth = table_ref.shape[0]
    step = out_refs[0].shape[0]
    if place_ref.shape[0] == 1:
        mask = iota((step, depth), 0) + at * step == place_ref[...]
    else:
        mask = iota((step, depth), 1) == place_ref[...]
    rows = jnp.dot(one_hot(mask), table_ref[...], preferred_element_type=F32).astype(BF16)
    if len(out_refs) == 1:
        out_refs[0][...] = rows
    else:
        for i, out_ref in enumerate(out_refs):
            @pl.when(at == i)
            def _():
                out_ref[...] = rows


def take(place, table, count, halves=False, after=()):
    depth, width = table.shape
    step = count // 2
    if place.shape[0] == 1:
        place_spec = whole(1, depth)
    else:
        place_spec = pl.BlockSpec((step, 1), lambda i: (i, 0))
    if halves:
        out_specs, out_shape = [whole(step, width)] * 2, [bf16(step, width)] * 2
    else:
        out_specs, out_shape = pl.BlockSpec((step, width), lambda i: (i, 0)), bf16(count, width)
    return pl.pallas_call(
        functools.partial(take_kernel, len(after)),
        grid=(2,),
        in_specs=[place_spec, whole(depth, width)]
        + [pl.BlockSpec(memory_space=pl.ANY) for _ in after],
        out_specs=out_specs,
        out_shape=out_shape,
        compiler_params=params(24),
        cost_estimate=cost(2 * count * depth * width, 2e6),
    )(place, table, *after)


def shift(part, by):
    return lax.ppermute(part, "col", [(c, (c + by) % 4) for c in range(4)])


def gather_ring(low, high):
    before_low, after_high = shift(low, 1), shift(high, 3)
    before_high, after_low = shift(high, 1), shift(low, 3)
    far_low, far_high = shift(before_low, 1), shift(after_high, 3)
    return low, high, after_low, after_high, far_low, far_high, before_low, before_high


def stage(parts, table, sems):
    at = 0
    loads = []
    for i, part in enumerate(parts):
        rows = part.shape[0]
        loads.append(pltpu.make_async_copy(part, table.at[pl.ds(at, rows)], sems.at[i]))
        loads[-1].start()
        at += rows
    for load in loads:
        load.wait()


def block_row(index_ref, values_ref, table, row, per_row):
    entries = [row * per_row + k for k in range(per_row)]
    at = [pl.multiple_of(index_ref[entry] * 128, 128) for entry in entries]
    blocks = jnp.concatenate([values_ref[entry] for entry in entries], axis=1)
    picked = jnp.concatenate([table[pl.ds(first, 128), :] for first in at], axis=0)
    return jnp.dot(blocks, picked, preferred_element_type=F32)


def layer_kernel(index_ref, values_ref, *refs):
    parts = refs[:8]
    (cot_ref, w_ref, gate_ref) = refs[8:11]
    (side_out_ref, agg_ref, mgrad_ref, low_ref, high_ref, gpart_ref, table, sems) = refs[11:]
    at = pl.program_id(0)

    @pl.when(at == 0)
    def _():
        stage(parts, table, sems)

    step = cot_ref.shape[0]
    nodes = step * pl.num_programs(0)
    per_row = values_ref.shape[0] * 128 // nodes
    rows = step // 128
    for row in range(rows):
        agg_ref[row * 128:(row + 1) * 128, :] = block_row(
            index_ref, values_ref, table, at * rows + row, per_row
        ).astype(BF16)
    gate = gate_ref[...]
    part = None
    for third in range(rows):
        here = slice(third * 128, (third + 1) * 128)
        message = jnp.dot(agg_ref[here, :], w_ref[...], preferred_element_type=F32)
        squash = jax.nn.sigmoid(message)
        activated = message * squash
        upstream = cot_ref[here, :].astype(F32)
        at_row = pl.multiple_of(at * step + third * 128, 128)
        owned = table[pl.ds(at_row, 128), :]
        side_out_ref[here, :] = (owned.astype(F32) + gate * activated).astype(BF16)
        mgrad_ref[here, :] = (
            upstream * gate * squash * (1.0 + message * (1.0 - squash))
        ).astype(BF16)
        term = jnp.sum(upstream * activated, axis=0, keepdims=True)
        part = term if part is None else part + term
    agrad = lax.dot_general(
        mgrad_ref[...], w_ref[...], (((1,), (1,)), ((), ())), preferred_element_type=F32
    ).astype(BF16)

    @pl.when(at == 0)
    def _():
        low_ref[...] = agrad
        gpart_ref[...] = part

    @pl.when(at == 1)
    def _():
        high_ref[...] = agrad
        gpart_ref[...] += part


def layer(index, values, parts, cotangent, w_msg, gate):
    nodes, width = cotangent.shape
    step = nodes // 2
    rows = lambda size: pl.BlockSpec((step, size), lambda i: (i, 0))
    return pl.pallas_call(
        layer_kernel,
        grid=(2,),
        in_specs=[pl.BlockSpec(memory_space=pltpu.SMEM), whole(*values.shape)]
        + [pl.BlockSpec(memory_space=pl.ANY) for _ in parts]
        + [rows(width), whole(width, width), whole(1, width)],
        out_specs=[rows(width), rows(width), rows(width), whole(step, width), whole(step, width),
                   whole(1, width)],
        out_shape=[bf16(nodes, width), bf16(nodes, width), bf16(nodes, width), bf16(step, width),
                   bf16(step, width),
                   jax.ShapeDtypeStruct((1, width), F32)],
        scratch_shapes=[pltpu.VMEM((4 * nodes, width), BF16), pltpu.SemaphoreType.DMA((8,))],
        compiler_params=params(),
        cost_estimate=cost(12e8, 8e6, nodes * width),
    )(index, values, *parts, cotangent, w_msg, gate)


def back_kernel(index_ref, values_ref, *refs):
    parts, (cot_ref, place_ref), (out_ref, table, grad, sems) = refs[:8], refs[8:10], refs[-4:]
    nodes = cot_ref.shape[0]
    per_row = values_ref.shape[0] * 128 // nodes

    @pl.when(pl.program_id(0) == 0)
    def _():
        stage(parts, table, sems)
        for row in range(nodes // 128):
            at = slice(row * 128, (row + 1) * 128)
            total = block_row(index_ref, values_ref, table, row, per_row)
            upstream = cot_ref[at, :].astype(F32)
            grad[at, :] = (upstream + total).astype(BF16)

    mask = iota((out_ref.shape[0], nodes), 1) == place_ref[...]
    out_ref[...] = jnp.dot(one_hot(mask), grad[...], preferred_element_type=F32).astype(BF16)


def back(index, values, parts, cotangent, place, slots):
    nodes = cotangent.shape[0]
    wide = parts[0].shape[1]
    step = slots // 4
    return pl.pallas_call(
        back_kernel,
        grid=(4,),
        in_specs=[pl.BlockSpec(memory_space=pltpu.SMEM), whole(*values.shape)]
        + [pl.BlockSpec(memory_space=pltpu.HBM if i < 2 else pl.ANY) for i in range(len(parts))]
        + [whole(*cotangent.shape), pl.BlockSpec((step, 1), lambda i: (i, 0))],
        out_specs=pl.BlockSpec((step, wide), lambda i: (i, 0)),
        out_shape=bf16(slots, wide),
        scratch_shapes=[
            pltpu.VMEM((4 * nodes, wide), BF16),
            pltpu.VMEM((nodes, wide), BF16),
            pltpu.SemaphoreType.DMA((8,)),
        ],
        compiler_params=params(40),
        cost_estimate=cost(2 * slots * nodes * wide, 5e6),
    )(index, values, *parts, cotangent, place)


def small_kernel(agg_ref, mgrad_ref, gate_ref, after_ref, mine_ref, theirs_ref):
    msg = lax.dot_general(
        agg_ref[...], mgrad_ref[...], (((0,), (0,)), ((), ())), preferred_element_type=F32
    )
    chips, rows, width = mine_ref.shape
    share = width // (2 * chips)
    tail = jnp.concatenate([gate_ref[...], jnp.zeros((rows - share - 1, width), F32)], axis=0)
    core = lax.axis_index("core")
    for this in range(2):
        @pl.when(core == this)
        def _():
            for out_ref, which in ((mine_ref, this), (theirs_ref, 1 - this)):
                for chip in range(chips):
                    at = (chip * 2 + which) * share
                    out_ref[chip, :share, :] = msg[at:at + share, :]
                    out_ref[chip, share:, :] = tail


def small_sums(aggregate, message_grad, gate_part, chips, after):
    width = aggregate.shape[1]
    vmem = pl.BlockSpec(memory_space=pltpu.VMEM)
    out = jax.ShapeDtypeStruct((chips, 24, width), F32)
    return pl.pallas_call(
        small_kernel,
        in_specs=[vmem] * 3 + [pl.BlockSpec(memory_space=pl.ANY)],
        out_specs=[vmem] * 2,
        out_shape=[out, out],
        compiler_params=params(24),
        cost_estimate=cost(4e8, 4e6),
    )(aggregate, message_grad, gate_part, after)


def down_rows(mine_ref, other_ref, grad_ref, other_grad_ref):
    docs = mine_ref.shape[2]
    rows = mine_ref.shape[0] * mine_ref.shape[1]
    left = jnp.concatenate(
        [mine_ref[...].reshape(rows, docs), other_ref[...].reshape(rows, docs)], axis=1
    )
    right = jnp.concatenate([grad_ref[...], other_grad_ref[...]], axis=0)
    return jnp.dot(left, right, preferred_element_type=F32)


def tiles_of(array):
    return [array[:, at:at + 128] for at in range(0, array.shape[1], 128)]


def two_terms(row):
    high = row.astype(BF16).astype(F32)
    return [high, row - high, jnp.zeros((14, 128), F32)]


def small_by_col_kernel(small_ref, other_small_ref, *out_refs):
    small = small_ref[...] + other_small_ref[...]
    chips = small.shape[0]
    msg = (small.shape[1] - 8) // 4
    blocks = []
    for chip in range(chips):
        for col in range(4):
            gate = small[chip, 4 * msg:4 * msg + 1, col * 128:(col + 1) * 128]
            cells = tiles_of(small[chip, col * msg:(col + 1) * msg, :]) + two_terms(gate)
            blocks.append(jnp.concatenate(cells, axis=0).astype(BF16))
    my_col = lax.axis_index("col")
    for first in range(4):
        @pl.when(my_col == first)
        def _():
            for k, out_ref in enumerate(out_refs):
                for chip in range(chips):
                    out_ref[chip] = blocks[chip * 4 + (first + k) % 4]


def small_by_col(small, other_small, cols):
    vmem = pl.BlockSpec(memory_space=pltpu.VMEM)
    return pl.pallas_call(
        small_by_col_kernel,
        in_specs=[vmem] * 2,
        out_specs=[vmem] * cols,
        out_shape=[bf16(small.shape[0], 32, 128)] * cols,
        compiler_params=params(24),
        cost_estimate=cost(1e6, 2e6),
    )(small, other_small)


def lead_kernel(*refs):
    total = sum([ref[...].astype(F32) for ref in refs[1:4]], refs[0][...].astype(F32))
    out_ref = refs[4]
    at = total.shape[1] - 16
    for chip in range(total.shape[0]):
        gate = total[chip, at:at + 1, :] + total[chip, at + 1:at + 2, :]
        cells = [total[chip, :at, :]] + two_terms(gate)
        out_ref[chip] = jnp.concatenate(cells, axis=0).astype(BF16)


def lead_sum(pieces):
    vmem = pl.BlockSpec(memory_space=pltpu.VMEM)
    return pl.pallas_call(
        lead_kernel,
        in_specs=[vmem] * 4,
        out_specs=vmem,
        out_shape=bf16(*pieces[0].shape),
        compiler_params=params(24),
        cost_estimate=cost(1e6, 1e6),
    )(*pieces)


def down_by_chip_kernel(mine_ref, other_ref, grad_ref, other_grad_ref, led_ref, out_ref):
    total = down_rows(mine_ref, other_ref, grad_ref, other_grad_ref)
    chips, share, _ = mine_ref.shape
    led = out_ref.shape[1] - led_ref.shape[1]
    for chip in range(chips):
        cells = tiles_of(total[chip * share:(chip + 1) * share, :])
        out_ref[chip, :led, :] = jnp.concatenate(cells, axis=0).astype(BF16)
        out_ref[chip, led:, :] = led_ref[chip]


def down_specs(mine, grad):
    chips, share, docs = mine.shape
    rows = pl.BlockSpec((chips // 4, share, docs), lambda i: (i, 0, 0))
    return [rows, rows, whole(*grad.shape), whole(*grad.shape)]


def down_by_chip(mine, other, grad, other_grad, led):
    chips, share, docs = mine.shape
    rows = share * grad.shape[1] // 128 + led.shape[1]
    by_chip = lambda size: pl.BlockSpec((chips // 4, size, 128), lambda i: (i, 0, 0))
    return pl.pallas_call(
        down_by_chip_kernel,
        grid=(4,),
        in_specs=down_specs(mine, grad) + [by_chip(led.shape[1])],
        out_specs=by_chip(rows),
        out_shape=bf16(chips, rows, 128),
        compiler_params=params(40),
        cost_estimate=cost(2e9, 12e6),
    )(mine, other, grad, other_grad, led)


def fold_kernel(parts_ref, out_ref):
    total = jnp.sum(parts_ref[...].astype(F32), axis=0)
    at = total.shape[0] - 16
    gate = total[at:at + 1, :] + total[at + 1:at + 2, :]
    out_ref[...] = jnp.concatenate([total[:at, :]] + two_terms(gate), axis=0).astype(BF16)


def fold(parts):
    chips, rows, width = parts.shape
    vmem = pl.BlockSpec(memory_space=pltpu.VMEM)
    return pl.pallas_call(
        fold_kernel,
        in_specs=[vmem],
        out_specs=vmem,
        out_shape=bf16(rows, width),
        compiler_params=params(24),
        cost_estimate=cost(1e6, 2e6),
    )(parts)


def finish_kernel(*refs):
    found, (down_ref, msg_ref, gate_ref) = refs[:4], refs[4:]
    share, width = down_ref.shape
    msg = msg_ref.shape[0]
    my_col = lax.axis_index("col")
    own, near, far, cross = (ref[...].astype(F32) for ref in found)
    total = (own + near) + (far + cross)
    at = 0
    for lane in range(0, width, 128):
        down_ref[:, lane:lane + 128] = total[at:at + share, :]
        at += share

    def from_col(col):
        step = my_col ^ col
        part = own[at:, :]
        for i, other in enumerate((near, far, cross)):
            part = jnp.where(step == i + 1, other[at:, :], part)
        return part

    for col in range(4):
        part = from_col(col)
        row = 0
        for lane in range(0, width, 128):
            msg_ref[col * msg // 4:(col + 1) * msg // 4, lane:lane + 128] = (
                part[row:row + msg // 4, :]
            )
            row += msg // 4
    first = lax.axis_index(ROWS) * msg
    gate = from_col(first // 128)[-16:, :]
    spread = jnp.broadcast_to(gate[0:1, :] + gate[1:2, :], (8, 128))
    gate_ref[...] = pltpu.roll(spread, (128 - first % 128) % 128, 1)[:1, :msg]


def finish(found, share, msg, width):
    vmem = pl.BlockSpec(memory_space=pltpu.VMEM)
    shape = lambda *dims: jax.ShapeDtypeStruct(dims, F32)
    return pl.pallas_call(
        finish_kernel,
        in_specs=[vmem] * 4,
        out_specs=[vmem] * 3,
        out_shape=[shape(share, width), shape(msg, width), shape(1, msg)],
        compiler_params=params(24),
        cost_estimate=cost(1e6, 1e6),
    )(*found)


def relay(rows):
    slots, width = rows.shape
    size = lax.axis_size(ROWS)
    moved = lax.all_to_all(
        rows.reshape(size, slots // size, width), ROWS, split_axis=0, concat_axis=0, tiled=True
    )
    return moved.reshape(slots, width)


def shards(doc_taps, w_down, owner_of, adj_values, adj_index, w_msg, gate_scale, cotangent):
    docs = doc_taps.shape[0]
    depth, width = w_down.shape
    row_size, cols = lax.axis_size(ROWS), lax.axis_size("col")
    my_row, my_col = lax.axis_index(ROWS), lax.axis_index("col")
    slots = row_size * SLOTS
    chips = row_size // 2
    values = adj_values[0]
    blocks = docs // 128
    index = (adj_index[0] // blocks - my_col) % cols * blocks + adj_index[0] % blocks
    gate = gate_scale.reshape(1, width)
    swap = lambda array: lax.ppermute(array, "core", [(0, 1), (1, 0)])

    taps = taps_by_tile(doc_taps)
    packed, slot = pool_and_pack(owner_of, taps, w_down, slots)
    incoming = relay(packed)
    mine, theirs, turned = pool_and_turn(taps, depth, chips, slot, slots)
    other = swap(theirs)

    owners = owner_of[0]
    counts = jnp.sum((owners.reshape(row_size, docs) == my_row).astype(jnp.int32), axis=1)
    lower = jnp.arange(row_size)[None, :] < jnp.arange(row_size)[:, None]
    starts = jnp.sum(jnp.where(lower, counts[None, :], 0), axis=1)
    in_slot = jnp.arange(SLOTS, dtype=jnp.int32)[None, :]
    position = jnp.where(in_slot < counts[:, None], starts[:, None] + in_slot, -1).reshape(slots)
    pos_row, pos_col = position.reshape(1, slots) + turned, position.reshape(slots, 1)

    owned = take(pos_row, incoming, docs, halves=True)
    side_out, aggregate, message_grad, low, high, gate_part = layer(
        index, values, gather_ring(*owned), cotangent, w_msg, gate
    )

    packed_back = back(index, values, gather_ring(low, high), cotangent, pos_col, slots)
    returned = relay(packed_back)

    small, other_small = small_sums(aggregate, message_grad, gate_part, chips, packed_back)
    pieces = small_by_col(small, swap(other_small), cols)
    led = lead_sum([pieces[0]] + [shift(pieces[k], k) for k in range(1, cols)])
    grad = take(slot.reshape(docs, 1), returned, docs, after=(led,))
    down = down_by_chip(mine, other, grad, swap(grad), led)
    down = lax.all_to_all(down, ("z", "x"), split_axis=0, concat_axis=0, tiled=True)
    own = fold(down)
    found = [own] + [
        lax.ppermute(own, "col", [(c, c ^ step) for c in range(4)]) for step in (1, 2, 3)
    ]
    grad_down, grad_msg, grad_gate = finish(found, depth // row_size, width // row_size, width)
    return side_out, grad_down, grad_msg, grad_gate.reshape(width // row_size)


def solution(mesh):
    rows, cols = mesh.devices.shape
    z = 4
    x = rows // (2 * z)
    split = Mesh(mesh.devices.reshape(z, x, 2, cols), ("z", "x", "core", "col"))
    each = ROWS + ("col",)
    placed = (
        P(each, None, None),
        P(),
        P("col", None),
        P(each, None, None, None),
        P(each, None),
        P(),
        P(),
        P(each, None),
    )
    return jax.shard_map(
        shards,
        mesh=split,
        in_specs=placed,
        out_specs=(P(each, None), P(ROWS, None), P(ROWS, None), P(ROWS)),
        check_vma=False,
    )
```

```python
import functools

import jax
import jax.numpy as jnp
import numpy as np
from jax import lax
from jax.experimental import pallas as pl
from jax.experimental.pallas import tpu as pltpu
from jax.sharding import Mesh
from jax.sharding import PartitionSpec as P

ROWS = ("z", "x", "core")
BF16 = jnp.bfloat16
F32 = jnp.float32
SLOTS = 72


def iota(shape, dim):
    return lax.broadcasted_iota(jnp.int32, shape, dim)


def one_hot(mask):
    return jnp.where(mask, 1.0, 0.0).astype(BF16)


def params(mib=60):
    return pltpu.CompilerParams(vmem_limit_bytes=mib * 1024 * 1024)


def cost(flops, moved, special=0):
    return pl.CostEstimate(flops=int(flops), bytes_accessed=int(moved), transcendentals=int(special))


def whole(*shape):
    return pl.BlockSpec(shape, lambda i: (0,) * len(shape))


def bf16(*shape):
    return jax.ShapeDtypeStruct(shape, BF16)


STREAMS = 4


def pool_tiles(pick, x_refs, pooled_ref):
    tiles = x_refs[0].shape[1] // 16
    docs = x_refs[0].shape[0]
    for stream, x_ref in enumerate(x_refs):
        block = jnp.concatenate(
            [
                x_ref[at:at + 16, t * 16:(t + 1) * 16, :].reshape(256, 128)
                for at in range(0, docs, 16)
                for t in range(tiles)
            ],
            axis=1,
        )
        mean = jnp.dot(pick[...], block, preferred_element_type=F32).astype(BF16)
        for group in range(docs // 16):
            first = stream * docs + group * 16
            for j in range(8):
                for t in range(tiles):
                    at, lane = (t * 8 + j) * 128, (group * tiles + t) * 128
                    pooled_ref[first:first + 16, at:at + 128] = (
                        mean[j * 16:(j + 1) * 16, lane:lane + 128]
                    )


def set_pick(pick):
    out_row, in_row = iota((128, 256), 0), iota((128, 256), 1)
    same_doc = out_row % 16 == in_row // 16
    same_tile = out_row // 16 == (in_row % 16) // 2
    pick[...] = jnp.where(same_doc & same_tile, 0.5, 0.0).astype(BF16)


def pool_kernel(owner_ref, *refs):
    x_refs, (w_hbm, out_ref, slot_ref) = refs[:STREAMS], refs[STREAMS:STREAMS + 3]
    pick, pooled, side, w_ref, w_sem, chosen = refs[STREAMS + 3:]
    at = pl.program_id(0)
    steps = pl.num_programs(0)
    docs = side.shape[0]
    step = STREAMS * x_refs[0].shape[0]
    share = out_ref.shape[0] // 6
    load = pltpu.make_async_copy(w_hbm, w_ref, w_sem)

    @pl.when(at == 0)
    def _():
        load.start()
        set_pick(pick)
        first = pl.multiple_of(lax.axis_index(ROWS) * docs, 128)
        dest = owner_ref[:, pl.ds(first, docs)]
        hit = iota((32, docs), 0) == dest
        earlier = one_hot(iota((docs, docs), 0) < iota((docs, docs), 1))
        before = jnp.dot(one_hot(hit), earlier, preferred_element_type=F32)
        rank = jnp.sum(jnp.where(hit, before, 0.0), axis=0, keepdims=True)
        slot_ref[...] = dest * SLOTS + rank.astype(jnp.int32)

    pool_tiles(pick, x_refs, pooled.at[pl.ds(pl.multiple_of(at * step, step), step)])
    rows = iota((share, docs), 0) + at * share
    chosen[pl.ds(pl.multiple_of(at * share, 16), share), :] = one_hot(rows == slot_ref[...])

    @pl.when(at == steps - 1)
    def _():
        load.wait()
        side[...] = jnp.dot(pooled[...], w_ref[...], preferred_element_type=F32).astype(BF16)
        for part in range(6):
            rows = slice(part * share, (part + 1) * share)
            out_ref[rows, :] = jnp.dot(
                chosen[rows, :], side[...], preferred_element_type=F32
            ).astype(BF16)


def turn_kernel(*refs):
    x_refs, (mine_ref, theirs_ref, done_ref, pick, pooled) = refs[:STREAMS], refs[STREAMS + 1:]

    @pl.when(pl.program_id(0) == 0)
    def _():
        set_pick(pick)
        done_ref[...] = jnp.zeros_like(done_ref)

    pool_tiles(pick, x_refs, pooled)
    rows = mine_ref.shape[1]
    core = lax.axis_index("core")
    for pair in range(mine_ref.shape[0] // 2):
        turned = pooled[:, pair * 4 * rows:(pair + 1) * 4 * rows].T
        for this in range(2):
            @pl.when(core == this)
            def _():
                for turned_ref, which in ((mine_ref, this), (theirs_ref, 1 - this)):
                    for chip in range(2):
                        at = (chip * 2 + which) * rows
                        turned_ref[pair * 2 + chip] = turned[at:at + rows, :]


def taps_by_tile(doc_taps):
    docs, tokens, depth = doc_taps.shape
    tiles = depth // 128
    taps = doc_taps.reshape(docs, tokens, tiles, 128).transpose(0, 2, 1, 3)
    return taps.reshape(docs, tokens * tiles, 128)


def streams(step, rows):
    def spec(stream):
        return pl.BlockSpec((step // STREAMS, rows, 128), lambda i: (i * STREAMS + stream, 0, 0))

    return [spec(stream) for stream in range(STREAMS)]


def pool_and_pack(owner_of, taps, w_down, slots):
    docs, rows, _ = taps.shape
    depth, width = w_down.shape
    return pl.pallas_call(
        pool_kernel,
        grid=(6,),
        in_specs=[
            whole(*owner_of.shape),
            *streams(docs // 6, rows),
            pl.BlockSpec(memory_space=pl.ANY),
        ],
        out_specs=[whole(slots, width), whole(1, docs)],
        out_shape=[bf16(slots, width), jax.ShapeDtypeStruct((1, docs), jnp.int32)],
        scratch_shapes=[
            pltpu.VMEM((128, 256), BF16),
            pltpu.VMEM((docs, depth), BF16),
            pltpu.VMEM((docs, width), BF16),
            pltpu.VMEM((depth, width), BF16),
            pltpu.SemaphoreType.DMA,
            pltpu.VMEM((slots, docs), BF16),
        ],
        compiler_params=params(),
        cost_estimate=cost(8e9, 23e6),
    )(owner_of, *[taps] * STREAMS, w_down)


def pool_and_turn(taps, depth, chips, after, slots):
    docs, rows, _ = taps.shape
    step = docs // 6
    turned = pl.BlockSpec((chips, depth // (2 * chips), step), lambda i: (0, 0, i))
    return pl.pallas_call(
        turn_kernel,
        grid=(6,),
        in_specs=streams(step, rows) + [pl.BlockSpec(memory_space=pl.ANY)],
        out_specs=[turned, turned, whole(1, slots)],
        out_shape=[bf16(chips, depth // (2 * chips), docs)] * 2
        + [jax.ShapeDtypeStruct((1, slots), jnp.int32)],
        scratch_shapes=[pltpu.VMEM((128, 256), BF16), pltpu.VMEM((step, depth), BF16)],
        compiler_params=params(),
        cost_estimate=cost(2e9, 24e6),
    )(*[taps] * STREAMS, after)


def take_kernel(waited, place_ref, table_ref, *out_refs):
    at = pl.program_id(0)
    out_refs = out_refs[waited:]
    depth = table_ref.shape[0]
    step = out_refs[0].shape[0]
    if place_ref.shape[0] == 1:
        mask = iota((step, depth), 0) + at * step == place_ref[...]
    else:
        mask = iota((step, depth), 1) == place_ref[...]
    rows = jnp.dot(one_hot(mask), table_ref[...], preferred_element_type=F32).astype(BF16)
    if len(out_refs) == 1:
        out_refs[0][...] = rows
    else:
        for i, out_ref in enumerate(out_refs):
            @pl.when(at == i)
            def _():
                out_ref[...] = rows


def take(place, table, count, halves=False, after=()):
    depth, width = table.shape
    step = count // 2
    if place.shape[0] == 1:
        place_spec = whole(1, depth)
    else:
        place_spec = pl.BlockSpec((step, 1), lambda i: (i, 0))
    if halves:
        out_specs, out_shape = [whole(step, width)] * 2, [bf16(step, width)] * 2
    else:
        out_specs, out_shape = pl.BlockSpec((step, width), lambda i: (i, 0)), bf16(count, width)
    return pl.pallas_call(
        functools.partial(take_kernel, len(after)),
        grid=(2,),
        in_specs=[place_spec, whole(depth, width)]
        + [pl.BlockSpec(memory_space=pl.ANY) for _ in after],
        out_specs=out_specs,
        out_shape=out_shape,
        compiler_params=params(24),
        cost_estimate=cost(2 * count * depth * width, 2e6),
    )(place, table, *after)


def shift(part, by):
    return lax.ppermute(part, "col", [(c, (c + by) % 4) for c in range(4)])


def gather_ring(low, high):
    before_low, after_high = shift(low, 1), shift(high, 3)
    before_high, after_low = shift(high, 1), shift(low, 3)
    far_low, far_high = shift(before_low, 1), shift(after_high, 3)
    return low, high, after_low, after_high, far_low, far_high, before_low, before_high


def stage(parts, table):
    at = 0
    for part in parts:
        table[at:at + part.shape[0], :] = part[...]
        at += part.shape[0]


def block_row(index_ref, values_ref, table, row, per_row):
    entries = [row * per_row + k for k in range(per_row)]
    at = [pl.multiple_of(index_ref[entry] * 128, 128) for entry in entries]
    blocks = jnp.concatenate([values_ref[entry] for entry in entries], axis=1)
    picked = jnp.concatenate([table[pl.ds(first, 128), :] for first in at], axis=0)
    return jnp.dot(blocks, picked, preferred_element_type=F32)


def layer_kernel(index_ref, values_ref, *refs):
    parts = refs[:8]
    (cot_ref, w_ref, gate_ref) = refs[8:11]
    (side_out_ref, agg_ref, mgrad_ref, low_ref, high_ref, gpart_ref, table) = refs[11:]
    at = pl.program_id(0)

    @pl.when(at == 0)
    def _():
        stage(parts, table)

    step = cot_ref.shape[0]
    nodes = step * pl.num_programs(0)
    per_row = values_ref.shape[0] * 128 // nodes
    rows = step // 128
    for row in range(rows):
        agg_ref[row * 128:(row + 1) * 128, :] = block_row(
            index_ref, values_ref, table, at * rows + row, per_row
        ).astype(BF16)
    gate = gate_ref[...]
    part = None
    for third in range(rows):
        here = slice(third * 128, (third + 1) * 128)
        message = jnp.dot(agg_ref[here, :], w_ref[...], preferred_element_type=F32)
        squash = jax.nn.sigmoid(message)
        activated = message * squash
        upstream = cot_ref[here, :].astype(F32)
        at_row = pl.multiple_of(at * step + third * 128, 128)
        owned = table[pl.ds(at_row, 128), :]
        side_out_ref[here, :] = (owned.astype(F32) + gate * activated).astype(BF16)
        mgrad_ref[here, :] = (
            upstream * gate * squash * (1.0 + message * (1.0 - squash))
        ).astype(BF16)
        term = jnp.sum(upstream * activated, axis=0, keepdims=True)
        part = term if part is None else part + term
    agrad = lax.dot_general(
        mgrad_ref[...], w_ref[...], (((1,), (1,)), ((), ())), preferred_element_type=F32
    ).astype(BF16)

    @pl.when(at == 0)
    def _():
        low_ref[...] = agrad
        gpart_ref[...] = part

    @pl.when(at == 1)
    def _():
        high_ref[...] = agrad
        gpart_ref[...] += part


def layer(index, values, parts, cotangent, w_msg, gate):
    nodes, width = cotangent.shape
    step = nodes // 2
    rows = lambda size: pl.BlockSpec((step, size), lambda i: (i, 0))
    return pl.pallas_call(
        layer_kernel,
        grid=(2,),
        in_specs=[pl.BlockSpec(memory_space=pltpu.SMEM), whole(*values.shape)]
        + [whole(*part.shape) for part in parts]
        + [rows(width), whole(width, width), whole(1, width)],
        out_specs=[rows(width), rows(width), rows(width), whole(step, width), whole(step, width),
                   whole(1, width)],
        out_shape=[bf16(nodes, width), bf16(nodes, width), bf16(nodes, width), bf16(step, width),
                   bf16(step, width),
                   jax.ShapeDtypeStruct((1, width), F32)],
        scratch_shapes=[pltpu.VMEM((4 * nodes, width), BF16)],
        compiler_params=params(),
        cost_estimate=cost(12e8, 8e6, nodes * width),
    )(index, values, *parts, cotangent, w_msg, gate)


def keep_kernel(low_ref, high_ref, after_ref, out_ref):
    half = low_ref.shape[0]
    out_ref[:half, :] = low_ref[...]
    out_ref[half:, :] = high_ref[...]


def keep(low, high, after):
    half, width = low.shape
    vmem = pl.BlockSpec(memory_space=pltpu.VMEM)
    return pl.pallas_call(
        keep_kernel,
        in_specs=[vmem, vmem, pl.BlockSpec(memory_space=pl.ANY)],
        out_specs=vmem,
        out_shape=bf16(2 * half, width),
        compiler_params=params(24),
        cost_estimate=cost(1e6, 2e6),
    )(low, high, after)


def back_kernel(index_ref, values_ref, *refs):
    parts, (cot_ref, place_ref), (out_ref, table, grad) = refs[:7], refs[7:9], refs[-3:]
    nodes = cot_ref.shape[0]
    per_row = values_ref.shape[0] * 128 // nodes

    @pl.when(pl.program_id(0) == 0)
    def _():
        stage(parts, table)
        for row in range(nodes // 128):
            at = slice(row * 128, (row + 1) * 128)
            total = block_row(index_ref, values_ref, table, row, per_row)
            upstream = cot_ref[at, :].astype(F32)
            grad[at, :] = (upstream + total).astype(BF16)

    mask = iota((out_ref.shape[0], nodes), 1) == place_ref[...]
    out_ref[...] = jnp.dot(one_hot(mask), grad[...], preferred_element_type=F32).astype(BF16)


def back(index, values, parts, cotangent, place, slots):
    nodes = cotangent.shape[0]
    wide = parts[0].shape[1]
    step = slots // 4
    return pl.pallas_call(
        back_kernel,
        grid=(4,),
        in_specs=[pl.BlockSpec(memory_space=pltpu.SMEM), whole(*values.shape)]
        + [whole(*part.shape) for part in parts]
        + [whole(*cotangent.shape), pl.BlockSpec((step, 1), lambda i: (i, 0))],
        out_specs=pl.BlockSpec((step, wide), lambda i: (i, 0)),
        out_shape=bf16(slots, wide),
        scratch_shapes=[pltpu.VMEM((4 * nodes, wide), BF16), pltpu.VMEM((nodes, wide), BF16)],
        compiler_params=params(40),
        cost_estimate=cost(2 * slots * nodes * wide, 5e6),
    )(index, values, *parts, cotangent, place)


def small_kernel(agg_ref, mgrad_ref, gate_ref, after_ref, mine_ref, theirs_ref):
    msg = lax.dot_general(
        agg_ref[...], mgrad_ref[...], (((0,), (0,)), ((), ())), preferred_element_type=F32
    )
    chips, rows, width = mine_ref.shape
    share = width // (2 * chips)
    tail = jnp.concatenate([gate_ref[...], jnp.zeros((rows - share - 1, width), F32)], axis=0)
    core = lax.axis_index("core")
    for this in range(2):
        @pl.when(core == this)
        def _():
            for out_ref, which in ((mine_ref, this), (theirs_ref, 1 - this)):
                for chip in range(chips):
                    at = (chip * 2 + which) * share
                    out_ref[chip, :share, :] = msg[at:at + share, :]
                    out_ref[chip, share:, :] = tail


def small_sums(aggregate, message_grad, gate_part, chips, after):
    width = aggregate.shape[1]
    vmem = pl.BlockSpec(memory_space=pltpu.VMEM)
    out = jax.ShapeDtypeStruct((chips, 24, width), F32)
    return pl.pallas_call(
        small_kernel,
        in_specs=[vmem] * 3 + [pl.BlockSpec(memory_space=pl.ANY)],
        out_specs=[vmem] * 2,
        out_shape=[out, out],
        compiler_params=params(24),
        cost_estimate=cost(4e8, 4e6),
    )(aggregate, message_grad, gate_part, after)


def down_rows(mine_ref, other_ref, grad_ref, other_grad_ref):
    docs = mine_ref.shape[2]
    rows = mine_ref.shape[0] * mine_ref.shape[1]
    left = jnp.concatenate(
        [mine_ref[...].reshape(rows, docs), other_ref[...].reshape(rows, docs)], axis=1
    )
    right = jnp.concatenate([grad_ref[...], other_grad_ref[...]], axis=0)
    return jnp.dot(left, right, preferred_element_type=F32)


def tiles_of(array):
    return [array[:, at:at + 128] for at in range(0, array.shape[1], 128)]


def two_terms(row):
    high = row.astype(BF16).astype(F32)
    return [high, row - high, jnp.zeros((14, 128), F32)]


def small_by_col_kernel(small_ref, other_small_ref, *out_refs):
    small = small_ref[...] + other_small_ref[...]
    chips = small.shape[0]
    msg = (small.shape[1] - 8) // 4
    blocks = []
    for chip in range(chips):
        for col in range(4):
            gate = small[chip, 4 * msg:4 * msg + 1, col * 128:(col + 1) * 128]
            cells = tiles_of(small[chip, col * msg:(col + 1) * msg, :]) + two_terms(gate)
            blocks.append(jnp.concatenate(cells, axis=0).astype(BF16))
    my_col = lax.axis_index("col")
    for first in range(4):
        @pl.when(my_col == first)
        def _():
            for k, out_ref in enumerate(out_refs):
                for chip in range(chips):
                    out_ref[chip] = blocks[chip * 4 + (first + k) % 4]


def small_by_col(small, other_small, cols):
    vmem = pl.BlockSpec(memory_space=pltpu.VMEM)
    return pl.pallas_call(
        small_by_col_kernel,
        in_specs=[vmem] * 2,
        out_specs=[vmem] * cols,
        out_shape=[bf16(small.shape[0], 32, 128)] * cols,
        compiler_params=params(24),
        cost_estimate=cost(1e6, 2e6),
    )(small, other_small)


def lead_kernel(*refs):
    total = sum([ref[...].astype(F32) for ref in refs[1:4]], refs[0][...].astype(F32))
    out_ref = refs[4]
    at = total.shape[1] - 16
    for chip in range(total.shape[0]):
        gate = total[chip, at:at + 1, :] + total[chip, at + 1:at + 2, :]
        cells = [total[chip, :at, :]] + two_terms(gate)
        out_ref[chip] = jnp.concatenate(cells, axis=0).astype(BF16)


def lead_sum(pieces):
    vmem = pl.BlockSpec(memory_space=pltpu.VMEM)
    return pl.pallas_call(
        lead_kernel,
        in_specs=[vmem] * 4,
        out_specs=vmem,
        out_shape=bf16(*pieces[0].shape),
        compiler_params=params(24),
        cost_estimate=cost(1e6, 1e6),
    )(*pieces)


def down_by_chip_kernel(mine_ref, other_ref, grad_ref, other_grad_ref, led_ref, out_ref):
    total = down_rows(mine_ref, other_ref, grad_ref, other_grad_ref)
    chips, share, _ = mine_ref.shape
    led = out_ref.shape[1] - led_ref.shape[1]
    for chip in range(chips):
        cells = tiles_of(total[chip * share:(chip + 1) * share, :])
        out_ref[chip, :led, :] = jnp.concatenate(cells, axis=0).astype(BF16)
        out_ref[chip, led:, :] = led_ref[chip]


def down_specs(mine, grad):
    chips, share, docs = mine.shape
    rows = pl.BlockSpec((chips // 4, share, docs), lambda i: (i, 0, 0))
    return [rows, rows, whole(*grad.shape), whole(*grad.shape)]


def down_by_chip(mine, other, grad, other_grad, led):
    chips, share, docs = mine.shape
    rows = share * grad.shape[1] // 128 + led.shape[1]
    by_chip = lambda size: pl.BlockSpec((chips // 4, size, 128), lambda i: (i, 0, 0))
    return pl.pallas_call(
        down_by_chip_kernel,
        grid=(4,),
        in_specs=down_specs(mine, grad) + [by_chip(led.shape[1])],
        out_specs=by_chip(rows),
        out_shape=bf16(chips, rows, 128),
        compiler_params=params(40),
        cost_estimate=cost(2e9, 12e6),
    )(mine, other, grad, other_grad, led)


def fold_kernel(parts_ref, out_ref):
    total = jnp.sum(parts_ref[...].astype(F32), axis=0)
    at = total.shape[0] - 16
    gate = total[at:at + 1, :] + total[at + 1:at + 2, :]
    out_ref[...] = jnp.concatenate([total[:at, :]] + two_terms(gate), axis=0).astype(BF16)


def fold(parts):
    chips, rows, width = parts.shape
    vmem = pl.BlockSpec(memory_space=pltpu.VMEM)
    return pl.pallas_call(
        fold_kernel,
        in_specs=[vmem],
        out_specs=vmem,
        out_shape=bf16(rows, width),
        compiler_params=params(24),
        cost_estimate=cost(1e6, 2e6),
    )(parts)


def finish_kernel(*refs):
    found, (down_ref, msg_ref, gate_ref) = refs[:4], refs[4:]
    share, width = down_ref.shape
    msg = msg_ref.shape[0]
    my_col = lax.axis_index("col")
    own, near, far, cross = (ref[...].astype(F32) for ref in found)
    total = (own + near) + (far + cross)
    at = 0
    for lane in range(0, width, 128):
        down_ref[:, lane:lane + 128] = total[at:at + share, :]
        at += share

    def from_col(col):
        step = my_col ^ col
        part = own[at:, :]
        for i, other in enumerate((near, far, cross)):
            part = jnp.where(step == i + 1, other[at:, :], part)
        return part

    for col in range(4):
        part = from_col(col)
        row = 0
        for lane in range(0, width, 128):
            msg_ref[col * msg // 4:(col + 1) * msg // 4, lane:lane + 128] = (
                part[row:row + msg // 4, :]
            )
            row += msg // 4
    first = lax.axis_index(ROWS) * msg
    gate = from_col(first // 128)[-16:, :]
    spread = jnp.broadcast_to(gate[0:1, :] + gate[1:2, :], (8, 128))
    gate_ref[...] = pltpu.roll(spread, (128 - first % 128) % 128, 1)[:1, :msg]


def finish(found, share, msg, width):
    vmem = pl.BlockSpec(memory_space=pltpu.VMEM)
    shape = lambda *dims: jax.ShapeDtypeStruct(dims, F32)
    return pl.pallas_call(
        finish_kernel,
        in_specs=[vmem] * 4,
        out_specs=[vmem] * 3,
        out_shape=[shape(share, width), shape(msg, width), shape(1, msg)],
        compiler_params=params(24),
        cost_estimate=cost(1e6, 1e6),
    )(*found)


def relay(rows):
    slots, width = rows.shape
    size = lax.axis_size(ROWS)
    moved = lax.all_to_all(
        rows.reshape(size, slots // size, width), ROWS, split_axis=0, concat_axis=0, tiled=True
    )
    return moved.reshape(slots, width)


def shards(doc_taps, w_down, owner_of, adj_values, adj_index, w_msg, gate_scale, cotangent):
    docs = doc_taps.shape[0]
    depth, width = w_down.shape
    row_size, cols = lax.axis_size(ROWS), lax.axis_size("col")
    my_row, my_col = lax.axis_index(ROWS), lax.axis_index("col")
    slots = row_size * SLOTS
    chips = row_size // 2
    values = adj_values[0]
    blocks = docs // 128
    index = (adj_index[0] // blocks - my_col) % cols * blocks + adj_index[0] % blocks
    gate = gate_scale.reshape(1, width)
    swap = lambda array: lax.ppermute(array, "core", [(0, 1), (1, 0)])

    taps = taps_by_tile(doc_taps)
    packed, slot = pool_and_pack(owner_of, taps, w_down, slots)
    incoming = relay(packed)
    mine, theirs, turned = pool_and_turn(taps, depth, chips, slot, slots)
    other = swap(theirs)

    owners = owner_of[0]
    counts = jnp.sum((owners.reshape(row_size, docs) == my_row).astype(jnp.int32), axis=1)
    lower = jnp.arange(row_size)[None, :] < jnp.arange(row_size)[:, None]
    starts = jnp.sum(jnp.where(lower, counts[None, :], 0), axis=1)
    in_slot = jnp.arange(SLOTS, dtype=jnp.int32)[None, :]
    position = jnp.where(in_slot < counts[:, None], starts[:, None] + in_slot, -1).reshape(slots)
    pos_row, pos_col = position.reshape(1, slots) + turned, position.reshape(slots, 1)

    owned = take(pos_row, incoming, docs, halves=True)
    side_out, aggregate, message_grad, low, high, gate_part = layer(
        index, values, gather_ring(*owned), cotangent, w_msg, gate
    )

    ring = gather_ring(low, high)
    ring = (keep(low, high, ring[7]),) + ring[2:]
    packed_back = back(index, values, ring, cotangent, pos_col, slots)
    returned = relay(packed_back)

    small, other_small = small_sums(aggregate, message_grad, gate_part, chips, packed_back)
    pieces = small_by_col(small, swap(other_small), cols)
    led = lead_sum([pieces[0]] + [shift(pieces[k], k) for k in range(1, cols)])
    grad = take(slot.reshape(docs, 1), returned, docs, after=(led,))
    down = down_by_chip(mine, other, grad, swap(grad), led)
    down = lax.all_to_all(down, ("z", "x"), split_axis=0, concat_axis=0, tiled=True)
    own = fold(down)
    found = [own] + [
        lax.ppermute(own, "col", [(c, c ^ step) for c in range(4)]) for step in (1, 2, 3)
    ]
    grad_down, grad_msg, grad_gate = finish(found, depth // row_size, width // row_size, width)
    return side_out, grad_down, grad_msg, grad_gate.reshape(width // row_size)


def solution(mesh):
    rows, cols = mesh.devices.shape
    z = 4
    x = rows // (2 * z)
    split = Mesh(mesh.devices.reshape(z, x, 2, cols), ("z", "x", "core", "col"))
    each = ROWS + ("col",)
    placed = (
        P(each, None, None),
        P(),
        P("col", None),
        P(each, None, None, None),
        P(each, None),
        P(),
        P(),
        P(each, None),
    )
    return jax.shard_map(
        shards,
        mesh=split,
        in_specs=placed,
        out_specs=(P(each, None), P(ROWS, None), P(ROWS, None), P(ROWS)),
        check_vma=False,
    )
```
